32 devices in a mesh: fsdp: 8 (over z, x), tensor: 4 (over y, core).
Axes of the slice: x: 2, y: 2, z: 4, core: 2. Of those that a mesh axis runs over, the one named last changes fastest.
Arguments:
- layer_input: bfloat16 [8192, 1024], P(('fsdp', 'tensor')), may hold values from -6 to 6
- segment_ids: int32 [8, 1024], P('fsdp'), may hold values from 0 to 3, never falling along the last dimension, each value on 1 to 512 neighbouring positions
- pad_mask: int32 [8, 1024], P('fsdp'), may hold values 0 or 1
- attn_gain: float32 [1, 1024], replicated, may hold values from 0.1 to 1.9
- ffn_gain: float32 [1, 1024], replicated, may hold values from 0.1 to 1.9
- out_gain: float32 [1, 128], replicated, may hold values from 0.1 to 1.9
- qkv_weight: bfloat16 [1, 3, 1024, 1024], P(None, None, 'fsdp', 'tensor'), may hold values from -0.1875 to 0.1875
- beta_weight: bfloat16 [1, 1024, 8], P(None, 'fsdp', 'tensor'), may hold values from -0.1875 to 0.1875
- conv_weight: float32 [1, 3, 4, 1024], P(None, None, None, 'tensor'), may hold values from -3 to 3
- out_weight: bfloat16 [1, 1024, 1024], P(None, 'tensor', 'fsdp'), may hold values from -0.1875 to 0.1875
- expand_weight: bfloat16 [1, 2, 1024, 2816], P(None, None, 'fsdp', 'tensor'), may hold values from -0.1875 to 0.1875
- down_weight: bfloat16 [1, 2816, 1024], P(None, 'tensor', 'fsdp'), may hold values from -0.15625 to 0.15625
- cotangent: bfloat16 [8192, 1024], P(('fsdp', 'tensor')), may hold values from -6 to 6
Outputs:
- block_outs: bfloat16 [1, 8192, 1024], P(None, ('fsdp', 'tensor'))
- input_grad: float32 [8192, 1024], P(('fsdp', 'tensor'))
- attn_gain_grad: float32 [1, 1024], replicated
- ffn_gain_grad: float32 [1, 1024], replicated
- out_gain_grad: float32 [1, 128], replicated
- qkv_grad: float32 [1, 3, 1024, 1024], P(None, None, 'fsdp', 'tensor')
- beta_grad: float32 [1, 1024, 8], P(None, 'fsdp', 'tensor')
- conv_grad: float32 [1, 3, 4, 1024], P(None, None, None, 'tensor')
- out_grad: float32 [1, 1024, 1024], P(None, 'tensor', 'fsdp')
- expand_grad: float32 [1, 2, 1024, 2816], P(None, None, 'fsdp', 'tensor')
- down_grad: float32 [1, 2816, 1024], P(None, 'tensor', 'fsdp')
The draws below stay inside these ranges and needn't reach their ends.
Inputs may be any that keep to these rules, and one draw needn't show every extreme that they name: `segment_ids`: along each sequence the ids never fall; every id from 0 to 3 occurs on 1 to 512 consecutive tokens.
All inputs are finite; a program needn't handle non-finite values. No bound on the sum of `pad_mask` on one device may be relied on, other than what follows from the above.
Results may differ from the reference program's by a relative error of at most 0.012.
Values may be sent and summed in bfloat16 or wider, within the bound.
No kernel may reach another device: no remote copies, remote signals or barrier semaphores. Data moves between devices by JAX's collectives and lax.ppermute only.
A program may use at most 128 MiB of HBM per device.

```python
import math
import jax
import jax.numpy as jnp
import numpy as np
from jax import lax

D = 1024
HEADS = 8
HEAD = 128
FF = 2816
CONV = 4
SPAN = 64
LAYERS = 1
DOCS = 4
SEQ = 1024
DOC_MOST = 512
SEQS = 8
TOKENS = 8192
N_FSDP = 8


def with_ends(values, key, smallest, high):
    longest = values.shape.index(max(values.shape))
    spots = []
    for shift in (0, 1):
        where = [jax.random.randint(jax.random.fold_in(key, axis), (), 0, length) for axis, length in enumerate(values.shape)]
        where[longest] = (where[longest] + shift) % values.shape[longest]
        spots.append(tuple(where))
    return values.at[spots[0]].set(smallest).at[spots[1]].set(high)


def shard_levels(stream_key, dims, shards, low, largest):
    loudness, own = 1.0, jax.random.fold_in(stream_key, 6)
    for position, blocks in shards:
        steps = jnp.exp(jax.random.uniform(jax.random.fold_in(own, position), (blocks,), jnp.float32, low / len(shards), largest / len(shards)))
        loudness = loudness * jnp.repeat(steps, dims[position] // blocks).reshape([-1 if axis == position else 1 for axis in range(len(dims))])
    return loudness


def length_profile(number_of, total, most, lean):
    loads = [(1 << 20) // math.isqrt(standing ** lean) + 1 for standing in range(2, number_of + 1)]
    spare, counts = total - most - (number_of - 1), [1] * (number_of - 1)
    while spare > 0:
        free = [i for i in range(number_of - 1) if counts[i] < most]
        whole, remaining = sum([loads[i] for i in free]), spare
        for i in free:
            addition = min(most - counts[i], max(1, remaining * loads[i] // whole), spare)
            counts[i] = counts[i] + addition
            spare = spare - addition
    return np.array([most] + counts)


def ragged(own_key, count, total, most, lean):
    if count == 2:
        one = jax.random.randint(own_key, (), max(1, total - most), min(most, total - 1) + 1)
        return jnp.stack([one, total - one])
    tallies = jnp.asarray(length_profile(count, total, most, lean), jnp.int32)
    pairs = (count - 1) // 2
    giver, taker = tallies[1:1 + 2 * pairs:2], tallies[2:2 + 2 * pairs:2]
    margin = jnp.minimum(giver - 1, most - taker)
    shifted = jax.random.randint(jax.random.fold_in(own_key, 1), (pairs,), 0, 1 << 20) % (margin + 1)
    tallies = tallies.at[1:1 + 2 * pairs:2].set(giver - shifted).at[2:2 + 2 * pairs:2].set(taker + shifted)
    return tallies[jax.random.permutation(jax.random.fold_in(own_key, 2), count)]


def normal_values(key, extent, spread, most, shards=(), kind=jnp.bfloat16):
    drawn = jax.random.normal(key, extent, jnp.float32) * spread
    if len(shards) > 0:
        drawn = shard_levels(key, extent, shards, -0.22, 0.18) * drawn
    return jnp.clip(drawn, min=-most, max=most).astype(kind)


def setup_inputs(seed: int = 0) -> dict:
    splits = jax.random.split(jax.random.key(seed), 14)
    return {
        "layer_input": normal_values(splits[0], (TOKENS, D), 1.0, 6.0, ((0, 32),)),
        "segment_ids": jax.vmap(lambda own: jnp.searchsorted(jnp.cumsum(ragged(own, DOCS, SEQ, DOC_MOST, 1)), jnp.arange(SEQ), side="right"))(jax.random.split(splits[1], SEQS)).reshape((SEQS, SEQ)).astype(jnp.int32),
        "pad_mask": with_ends((jax.random.randint(splits[2], (SEQS, SEQ), 0, 16) < 15).astype(jnp.int32), jax.random.fold_in(splits[2], 1), 0, 1),
        "attn_gain": jnp.clip(1.0 + 0.18 * jax.random.normal(splits[3], (LAYERS, D), jnp.float32), 0.1, 1.9),
        "ffn_gain": jnp.clip(1.0 + 0.18 * jax.random.normal(splits[4], (LAYERS, D), jnp.float32), 0.1, 1.9),
        "out_gain": jnp.clip(1.0 + 0.18 * jax.random.normal(splits[5], (LAYERS, HEAD), jnp.float32), 0.1, 1.9),
        "qkv_weight": normal_values(splits[6], (LAYERS, 3, D, D), D ** -0.5, 0.1875, ((2, 8), (3, 4))),
        "beta_weight": normal_values(splits[7], (LAYERS, D, HEADS), D ** -0.5, 0.1875, ((1, 8), (2, 4))),
        "conv_weight": normal_values(splits[8], (LAYERS, 3, CONV, D), CONV ** -0.5, 3.0, ((3, 4),), jnp.float32),
        "out_weight": normal_values(splits[9], (LAYERS, D, D), D ** -0.5, 0.1875, ((1, 4), (2, 8))),
        "expand_weight": normal_values(splits[10], (LAYERS, 2, D, FF), D ** -0.5, 0.1875, ((2, 8), (3, 4))),
        "down_weight": normal_values(splits[11], (LAYERS, FF, D), (FF // 2) ** -0.5, 0.15625, ((1, 4), (2, 8))),
        "cotangent": normal_values(splits[12], (TOKENS, D), 1.0, 6.0, ((0, 32),)),
    }


highest_precision = lax.Precision.HIGHEST

@jax.custom_vjp
def low(v):
    return lax.optimization_barrier(v.astype(jnp.bfloat16)).astype(jnp.float32)

@jax.custom_vjp
def low_back(v):
    return v

def low_keep(v):
    return (low(v), None)

def low_pass(kept, grad):
    return (grad,)

def back_keep(v):
    return (v, None)

def back_low(kept, grad):
    return (low(grad),)
low.defvjp(low_keep, low_pass)
low_back.defvjp(back_keep, back_low)

def rms_norm(value_rows, gain):
    return value_rows * lax.rsqrt(lax.optimization_barrier(jnp.mean(value_rows * value_rows, axis=-1, keepdims=True)) + 1e-06) * gain

def conv_silu(value_rows, kernel, segments):
    tap_count = kernel.shape[0]
    seq_len = value_rows.shape[1]
    padded = jnp.pad(value_rows, ((0, 0), (tap_count - 1, 0), (0, 0)))
    seg_pad = jnp.concatenate([jnp.full((segments.shape[0], tap_count - 1), -1, jnp.int32), segments.astype(jnp.int32)], axis=1)
    summed = jnp.zeros_like(value_rows)
    for offset in range(tap_count):
        start_at = tap_count - 1 - offset
        same_doc = (seg_pad[:, start_at:start_at + seq_len] == segments).astype(value_rows.dtype)
        summed = summed + kernel[offset] * padded[:, start_at:start_at + seq_len] * same_doc[:, :, None]
    return jax.nn.silu(summed)

def unit_rows(value_rows):
    return value_rows * lax.rsqrt(lax.optimization_barrier(jnp.sum(value_rows * value_rows, axis=-1, keepdims=True)) + 1e-06)

def delta_spans(queries, key_vecs, value_vecs, beta_vals, segments):
    members, seq_len, head_dim = key_vecs.shape
    block_count = seq_len // SPAN

    def blocked(value_rows):
        return jnp.moveaxis(value_rows.reshape((members, block_count, SPAN) + value_rows.shape[2:]), 1, 0)
    identity = jnp.eye(SPAN, dtype=key_vecs.dtype)
    causal = jnp.tril(jnp.ones((SPAN, SPAN), key_vecs.dtype))

    def advance(carried, block):
        memory_state, previous = carried
        query_block, key_block, value_blk, beta_blk, seg_blk = block
        same_doc = (seg_blk[:, :, None] == seg_blk[:, None, :]).astype(key_block.dtype)
        leading_shape = (seg_blk == previous[:, None]).astype(key_block.dtype)
        trailing_shape = (seg_blk == seg_blk[:, -1:]).astype(key_block.dtype)
        products = jnp.einsum('nid,njd->nij', key_block, key_block, precision=highest_precision)
        system = identity + jnp.tril(beta_blk[:, :, None] * products * same_doc, -1)
        recalled_values = jnp.einsum('vhr,vcr->vch', memory_state, key_block, precision=highest_precision)
        right_side = beta_blk[:, :, None] * (value_blk - leading_shape[:, :, None] * recalled_values)
        state_update = jax.scipy.linalg.solve_triangular(system, right_side, lower=True, unit_diagonal=True)
        score_matrix = jnp.einsum('nid,njd->nij', query_block, key_block, precision=highest_precision) * same_doc * causal
        output_rows = leading_shape[:, :, None] * jnp.einsum('vhr,vcr->vch', memory_state, query_block, precision=highest_precision) + jnp.einsum('fwu,fug->fwg', score_matrix, state_update, precision=highest_precision)
        memory_state = leading_shape[:, -1][:, None, None] * memory_state + jnp.einsum('ytz,ytv->yzv', state_update * trailing_shape[:, :, None], key_block, precision=highest_precision)
        return ((memory_state, seg_blk[:, -1]), output_rows)
    start_mem = jnp.zeros((members, head_dim, head_dim), key_vecs.dtype)
    start_seg = jnp.full((members,), -1, jnp.int32)
    carried, outputs = lax.scan(jax.checkpoint(advance), (start_mem, start_seg), (blocked(queries), blocked(key_vecs), blocked(value_vecs), blocked(beta_vals), blocked(segments)))
    return jnp.moveaxis(outputs, 0, 1).reshape(members, seq_len, head_dim)

def mixer(query_pre, key_pre, value_pre, logits, kernels, gain_out, segments, pad_mask):
    batch_size, seq_len, channels = query_pre.shape
    head_count = channels // HEAD

    def heads_first(value_rows):
        return value_rows.reshape(batch_size, seq_len, head_count, HEAD).transpose(0, 2, 1, 3).reshape(batch_size * head_count, seq_len, HEAD)
    queries = unit_rows(heads_first(conv_silu(query_pre, kernels[0], segments)))
    key_vecs = unit_rows(heads_first(conv_silu(key_pre, kernels[1], segments)))
    value_vecs = heads_first(conv_silu(value_pre, kernels[2], segments))
    beta_vals = (jax.nn.sigmoid(logits) * pad_mask.astype(logits.dtype)[:, :, None]).transpose(0, 2, 1).reshape(batch_size * head_count, seq_len)
    seg_rep = jnp.repeat(segments.astype(jnp.int32), head_count, axis=0)
    output_rows = delta_spans(queries, key_vecs, value_vecs, beta_vals, seg_rep)
    output_rows = output_rows * lax.rsqrt(lax.optimization_barrier(jnp.mean(output_rows * output_rows, axis=-1, keepdims=True)) + 1e-05) * gain_out
    return output_rows.reshape(batch_size, head_count, seq_len, HEAD).transpose(0, 2, 1, 3).reshape(batch_size, seq_len, channels)

def forward(value_rows, segments, pad_mask, weights):
    gain_attn, gain_ffn, gain_out, qkv_all, beta_all, conv_all, output_stacked, expand_all, down_all = weights
    outputs = []
    for layer_index in range(LAYERS):
        normed = low(rms_norm(value_rows, gain_attn[layer_index]))
        projected = low_back(jnp.einsum('gld,sdc->sglc', normed, qkv_all[layer_index], precision=highest_precision))
        logits = low_back(jnp.einsum('gld,dh->glh', normed, beta_all[layer_index], precision=highest_precision))
        mixed_tokens = low(mixer(projected[0], projected[1], projected[2], logits, conv_all[layer_index], gain_out[layer_index], segments, pad_mask))
        value_rows = value_rows + low_back(jnp.einsum('orx,xm->orm', mixed_tokens, output_stacked[layer_index], precision=highest_precision))
        normed = low(rms_norm(value_rows, gain_ffn[layer_index]))
        expanded = low_back(jnp.einsum('gld,sdf->sglf', normed, expand_all[layer_index], precision=highest_precision))
        hidden = low(jax.nn.silu(expanded[0]) * expanded[1])
        value_rows = value_rows + low_back(jnp.einsum('glf,fd->gld', hidden, down_all[layer_index], precision=highest_precision))
        outputs.append(value_rows)
    return jnp.stack(outputs)

def reference(layer_input, segment_ids, pad_mask, attn_gain, ffn_gain, out_gain, qkv_weight, beta_weight, conv_weight, out_weight, expand_weight, down_weight, cotangent):
    params = tuple((param.astype(jnp.float32) for param in (attn_gain, ffn_gain, out_gain, qkv_weight, beta_weight, conv_weight, out_weight, expand_weight, down_weight)))
    per_group = max(1, min(N_FSDP, 4096 // SEQ))
    while N_FSDP % per_group != 0:
        per_group = per_group - 1
    groups = N_FSDP // per_group
    inputs = layer_input.astype(jnp.float32).reshape(groups, per_group, SEQ, D)
    seg_groups = segment_ids.astype(jnp.int32).reshape(groups, per_group, SEQ)
    mask_groups = pad_mask.astype(jnp.int32).reshape(groups, per_group, SEQ)
    cot_groups = cotangent.astype(jnp.float32).reshape(groups, per_group, SEQ, D)

    def group_step(totals, group_data):
        block_in, seg_now, mask_now, cot_now = group_data

        def forward_fn(value_rows, *weights):
            return forward(value_rows, seg_now, mask_now, weights)
        outputs, pullback = jax.vjp(forward_fn, block_in, *params)
        cot_seed = jnp.concatenate([jnp.zeros_like(outputs[:-1]), cot_now[None]], axis=0)
        gradients = pullback(cot_seed)
        totals = tuple((summed + extra for summed, extra in zip(totals, gradients[1:])))
        return (totals, (outputs, gradients[0]))
    zero_sums = tuple((jnp.zeros_like(param) for param in params))
    totals, (outputs, input_grad) = lax.scan(group_step, zero_sums, (inputs, seg_groups, mask_groups, cot_groups))
    block_outs = jnp.moveaxis(outputs, 1, 0).reshape(LAYERS, N_FSDP * SEQ, D).astype(jnp.bfloat16)
    return (block_outs, input_grad.reshape(N_FSDP * SEQ, D), totals[0], totals[1], totals[2], totals[3], totals[4], totals[5], totals[6], totals[7], totals[8])
```

```python
import functools
import jax
import jax.numpy as jnp
from jax import lax
from jax.experimental import pallas as pl
from jax.experimental.pallas import tpu as pltpu
from jax.sharding import PartitionSpec as P

HEAD = 128
C = 128
F32 = jnp.float32
BF = jnp.bfloat16

NN = (((1,), (0,)), ((), ()))
NT = (((1,), (1,)), ((), ()))
TN = (((0,), (0,)), ((), ()))


def dot1(a, b, dims=NN):
    return lax.dot_general(a.astype(BF), b.astype(BF), dims, preferred_element_type=F32)


def split(x):
    hi = x.astype(BF)
    return hi, (x - hi.astype(F32)).astype(BF)


def dot3(a, b, dims=NN):
    a1, a2 = split(a) if not isinstance(a, tuple) else a
    b1, b2 = split(b) if not isinstance(b, tuple) else b
    d = functools.partial(lax.dot_general, dimension_numbers=dims, preferred_element_type=F32)
    return d(a1, b1) + (d(a1, b2) + d(a2, b1))


def block_masks():
    r = lax.broadcasted_iota(jnp.int32, (C, C), 0)
    c = lax.broadcasted_iota(jnp.int32, (C, C), 1)
    return r, c


def invert(systems, dot):
    r, c = block_masks()
    eye = (r == c).astype(F32)
    x = r ^ c
    out = [eye - jnp.where((x == 1), low, 0.0) for low in systems]
    size = 2
    while size < C:
        here = (x >= size) & (x < 2 * size)
        mids = [dot(jnp.where(here, low, 0.0), t) for low, t in zip(systems, out)]
        out = [t - dot(t, m) for t, m in zip(out, mids)]
        size *= 2
    return out


def sigmoid(x):
    return 1.0 / (1.0 + jnp.exp(-x))


def taps_down(ext, rows, j):
    return lax.slice_in_dim(ext, 8 - j, 8 - j + rows, axis=0)


def fwd_kernel(heads, cb, seg_s, pre_ref, cols_ref, segr_ref, taps_ref, gain_ref,
               mixed_ref, conv_ref, o_ref, t_ref, a_ref, p_ref, n_ref, z_ref, s_ref, u_ref, g_ref,
               tail, state):
    step = pl.program_id(0)
    width = heads * HEAD
    rows = cb * C
    taps = taps_ref.shape[1]

    @pl.when(step == 0)
    def _():
        tail[...] = jnp.zeros_like(tail)
        state[...] = jnp.zeros_like(state)

    r, c = block_masks()
    parts = []
    for i in range(3):
        cur = pre_ref[:, i * width:(i + 1) * width]
        ext = jnp.concatenate([tail[:, i * width:(i + 1) * width], cur], axis=0)
        tot = cur * taps_ref[i, 0:1, :]
        for j in range(1, taps):
            tot = tot + taps_down(ext, rows, j) * taps_ref[i, j:j + 1, :] * cols_ref[:, j - 1:j]
        tail[:, i * width:(i + 1) * width] = cur[rows - 8:, :]
        conv_ref[:, i * width:(i + 1) * width] = tot
        parts.append(tot * sigmoid(tot))
    eye = (r == c).astype(F32)
    items = []
    for b in range(cb):
        sl = slice(b * C, (b + 1) * C)
        chunk = step * cb + b
        first = chunk * C
        prev = jnp.where(first > 0, seg_s[jnp.maximum(first - 1, 0)], -1)
        last = seg_s[first + C - 1]
        keep = (prev == last).astype(F32)
        segc = cols_ref[sl, 4:5]
        segr = segr_ref[0:1, sl]
        same = segc == segr
        lead = (segc == prev.astype(F32)).astype(F32)
        trail = (segc == last.astype(F32)).astype(F32)
        for h in range(heads):
            hs = slice(h * HEAD, (h + 1) * HEAD)
            q, k, v = (part[sl, hs] for part in parts)
            q = q * lax.rsqrt(jnp.sum(q * q, axis=-1, keepdims=True) + 1e-6)
            k = k * lax.rsqrt(jnp.sum(k * k, axis=-1, keepdims=True) + 1e-6)
            beta = sigmoid(pre_ref[sl, 3 * width + h:3 * width + h + 1]) * cols_ref[sl, 3:4]
            items.append(dict(b=b, h=h, q=q, k=k, v=v, beta=beta, same=same, lead=lead, trail=trail, keep=keep, sl=sl, hs=hs))
    for it in items:
        it["kk"] = split(it["k"])
        p = jnp.where(it["same"] & (r > c), dot3(it["kk"], it["kk"], NT), 0.0)
        it["p"] = p
        it["low"] = p * it["beta"]
        it["a"] = jnp.where(it["same"] & (r >= c), dot3(it["q"], it["kk"], NT), 0.0)
    inv = invert([it["low"] for it in items], dot3)
    for it, t in zip(items, inv):
        rhs = jnp.concatenate([it["beta"] * it["v"], (it["beta"] * it["lead"]) * it["k"]], axis=1)
        tw = dot3(t, rhs)
        tws = split(tw)
        aw = dot3(it["a"], tws)
        bz = dot3(it["trail"] * it["k"], tws, TN)
        it["tv"], it["w"] = tw[:, :HEAD], tw[:, HEAD:]
        it["o0"], it["n"] = aw[:, :HEAD], it["lead"] * it["q"] - aw[:, HEAD:]
        it["bk"], it["z"] = bz[:, :HEAD], it["keep"] * eye - bz[:, HEAD:]
        it["t"] = t
    for it in items:
        b, h = it["b"], it["h"]
        s = state[h]
        ss = split(s)
        u = it["tv"] - dot3(it["w"], ss)
        o = it["o0"] + dot3(it["n"], ss)
        g = it["v"] - it["lead"] * dot3(it["kk"], ss)
        state[h] = it["bk"] + dot3(it["z"], ss)
        s_ref[b, h] = s
        u_ref[b, h] = u
        g_ref[b, h] = g
        t_ref[b, h] = it["t"]
        a_ref[b, h] = it["a"]
        p_ref[b, h] = it["p"]
        n_ref[b, h] = it["n"]
        z_ref[b, h] = it["z"]
        o_ref[it["sl"], it["hs"]] = o
        mixed_ref[it["sl"], it["hs"]] = (o * lax.rsqrt(jnp.mean(o * o, axis=-1, keepdims=True) + 1e-5) * gain_ref[0:1, :]).astype(BF)


def bwd_kernel(heads, cb, seg_s, dmix_ref, pre_ref, conv_ref, o_ref, cols_ref, segr_ref, taps_ref, gain_ref,
               t_ref, a_ref, p_ref, n_ref, z_ref, s_ref, u_ref, g_ref,
               dpre_ref, dtap_ref, dgain_ref,
               head_rows, dstate):
    step = pl.program_id(0)
    steps = pl.num_programs(0)
    width = heads * HEAD
    rows = cb * C
    taps = taps_ref.shape[1]
    back = steps - 1 - step

    @pl.when(step == 0)
    def _():
        head_rows[...] = jnp.zeros_like(head_rows)
        dstate[...] = jnp.zeros_like(dstate)
        dtap_ref[...] = jnp.zeros_like(dtap_ref)
        dgain_ref[...] = jnp.zeros_like(dgain_ref)

    r, c = block_masks()
    dcs = [[[None] * heads for _ in range(cb)] for _ in range(3)]
    dgain = jnp.zeros((1, HEAD), F32)
    dlog = [None] * cb
    for b in reversed(range(cb)):
        sl = slice(b * C, (b + 1) * C)
        chunk = back * cb + b
        first = chunk * C
        prev = jnp.where(first > 0, seg_s[jnp.maximum(first - 1, 0)], -1)
        last = seg_s[first + C - 1]
        segc = cols_ref[sl, 4:5]
        segr = segr_ref[0:1, sl]
        same = segc == segr
        lead = (segc == prev.astype(F32)).astype(F32)
        trail = (segc == last.astype(F32)).astype(F32)
        lane = lax.broadcasted_iota(jnp.int32, (C, HEAD), 1)
        dl = jnp.zeros((C, HEAD), F32)
        for h in range(heads):
            hs = slice(h * HEAD, (h + 1) * HEAD)
            cq, ck, cv = (conv_ref[sl, i * width + h * HEAD:i * width + (h + 1) * HEAD] for i in range(3))
            gq, gk, gv = sigmoid(cq), sigmoid(ck), sigmoid(cv)
            q, k = cq * gq, ck * gk
            rq = lax.rsqrt(jnp.sum(q * q, axis=-1, keepdims=True) + 1e-6)
            rk = lax.rsqrt(jnp.sum(k * k, axis=-1, keepdims=True) + 1e-6)
            q, k = q * rq, k * rk
            gb = sigmoid(pre_ref[sl, 3 * width + h:3 * width + h + 1])
            pad = cols_ref[sl, 3:4]
            beta = gb * pad
            o = o_ref[sl, hs]
            dm = dmix_ref[sl, hs]
            ro = lax.rsqrt(jnp.mean(o * o, axis=-1, keepdims=True) + 1e-5)
            oh = o * ro
            dgain = dgain + jnp.sum(dm * oh, axis=0, keepdims=True)
            du0 = dm * gain_ref[0:1, :]
            do = ro * (du0 - oh * jnp.mean(du0 * oh, axis=-1, keepdims=True))
            ds1 = dstate[h]
            u = u_ref[b, h]
            s = s_ref[b, h]
            a = a_ref[b, h]
            p = p_ref[b, h]
            ks = split(k)
            ds1s = split(ds1)
            dos = split(do)
            us = split(u)
            dstate[h] = dot3(z_ref[b, h], ds1s, TN) + dot3(n_ref[b, h], dos, TN)
            du = dot3(a, dos, TN) + trail * dot3(ks, ds1s)
            dr = dot3(t_ref[b, h], du, TN)
            drs = split(dr)
            ss = split(s)
            dlow = jnp.where(same & (r > c), -dot3(drs, us, NT), 0.0)
            da = jnp.where(same & (r >= c), dot3(dos, us, NT), 0.0)
            dv = beta * dr
            dbeta = jnp.sum(dr * g_ref[b, h] , axis=-1, keepdims=True) + jnp.sum(dlow * p, axis=-1, keepdims=True)
            dp = split(beta * dlow)
            das = split(da)
            dq = lead * dot3(dos, ss, NT) + dot3(das, ks)
            dk = (dot3(das, q, TN) + trail * dot3(us, ds1s, NT) - (beta * lead) * dot3(drs, ss, NT)
                  + dot3(dp, ks) + dot3(dp, ks, TN))
            dsq = rq * (dq - q * jnp.sum(q * dq, axis=-1, keepdims=True))
            dsk = rk * (dk - k * jnp.sum(k * dk, axis=-1, keepdims=True))
            dcs[0][b][h] = dsq * gq * (1.0 + cq * (1.0 - gq))
            dcs[1][b][h] = dsk * gk * (1.0 + ck * (1.0 - gk))
            dcs[2][b][h] = dv * gv * (1.0 + cv * (1.0 - gv))
            dl = jnp.where(lane == h, dbeta * pad * gb * (1.0 - gb), dl)
        dlog[b] = dl
    dgain_ref[...] += dgain
    for b in range(cb):
        dpre_ref[b * C:(b + 1) * C, 3 * width:] = dlog[b].astype(BF)
    for i in range(3):
        dc = jnp.concatenate([jnp.concatenate(dcs[i][b], axis=1) for b in range(cb)], axis=0)
        pre = pre_ref[:, i * width:(i + 1) * width]
        tot = dc * taps_ref[i, 0:1, :]
        grads = [jnp.sum(dc * pre, axis=0, keepdims=True)]
        for j in range(1, taps):
            e = dc * cols_ref[:, j - 1:j]
            ext = jnp.concatenate([e, head_rows[j - 1, :, i * width:(i + 1) * width]], axis=0)
            head_rows[j - 1, :, i * width:(i + 1) * width] = e[:8]
            e = lax.slice_in_dim(ext, j, j + rows, axis=0)
            tot = tot + e * taps_ref[i, j:j + 1, :]
            grads.append(jnp.sum(e * pre, axis=0, keepdims=True))
        dpre_ref[:, i * width:(i + 1) * width] = tot.astype(BF)
        dtap_ref[i] += jnp.concatenate(grads, axis=0)


def mixer_fwd(pre, cols, segr, seg, taps, gain, cb=2):
    n, wide = pre.shape
    width = taps.shape[2]
    heads = width // HEAD
    rows = cb * C
    chunks = n // C
    sq = jax.ShapeDtypeStruct((chunks, heads, C, HEAD), F32)
    sqspec = pl.BlockSpec((cb, heads, C, HEAD), lambda i, s: (i, 0, 0, 0))
    row = lambda w: pl.BlockSpec((rows, w), lambda i, s: (i, 0))
    return pl.pallas_call(
        functools.partial(fwd_kernel, heads, cb),
        grid_spec=pltpu.PrefetchScalarGridSpec(
            num_scalar_prefetch=1, grid=(n // rows,),
            in_specs=[row(wide), row(cols.shape[1]), pl.BlockSpec((1, rows), lambda i, s: (0, i)),
                      pl.BlockSpec(taps.shape, lambda i, s: (0, 0, 0)), pl.BlockSpec((1, HEAD), lambda i, s: (0, 0))],
            out_specs=[row(width), row(3 * width), row(width)] + [sqspec] * 8,
            scratch_shapes=[pltpu.VMEM((8, 3 * width), F32), pltpu.VMEM((heads, HEAD, HEAD), F32)]),
        out_shape=[jax.ShapeDtypeStruct((n, width), BF), jax.ShapeDtypeStruct((n, 3 * width), F32),
                   jax.ShapeDtypeStruct((n, width), F32)] + [sq] * 8,
        compiler_params=pltpu.CompilerParams(dimension_semantics=("arbitrary",), vmem_limit_bytes=48 * 2**20),
        name="mixer_fwd",
    )(seg, pre, cols, segr, taps, gain)


def mixer_bwd(dmix, pre, cols, segr, seg, taps, gain, kept, cb=2):
    conv, o, *rest = kept
    n, wide = pre.shape
    width = taps.shape[2]
    heads = width // HEAD
    rows = cb * C
    steps = n // rows
    sqspec = pl.BlockSpec((cb, heads, C, HEAD), lambda i, s: (steps - 1 - i, 0, 0, 0))
    row = lambda w: pl.BlockSpec((rows, w), lambda i, s: (steps - 1 - i, 0))
    ntap = taps.shape[1]
    return pl.pallas_call(
        functools.partial(bwd_kernel, heads, cb),
        grid_spec=pltpu.PrefetchScalarGridSpec(
            num_scalar_prefetch=1, grid=(steps,),
            in_specs=[row(width), row(wide), row(3 * width), row(width), row(cols.shape[1]),
                      pl.BlockSpec((1, rows), lambda i, s: (0, steps - 1 - i)),
                      pl.BlockSpec(taps.shape, lambda i, s: (0, 0, 0)), pl.BlockSpec((1, HEAD), lambda i, s: (0, 0))] + [sqspec] * 8,
            out_specs=[row(wide), pl.BlockSpec(taps.shape, lambda i, s: (0, 0, 0)), pl.BlockSpec((1, HEAD), lambda i, s: (0, 0))],
            scratch_shapes=[pltpu.VMEM((ntap - 1, 8, 3 * width), F32), pltpu.VMEM((heads, HEAD, HEAD), F32)]),
        out_shape=[jax.ShapeDtypeStruct((n, wide), BF), jax.ShapeDtypeStruct(taps.shape, F32), jax.ShapeDtypeStruct((1, HEAD), F32)],
        compiler_params=pltpu.CompilerParams(dimension_semantics=("arbitrary",), vmem_limit_bytes=48 * 2**20),
        name="mixer_bwd",
    )(seg, dmix, pre, conv, o, cols, segr, taps, gain, *rest)


def columns(seg, pad):
    n = seg.shape[0]
    cols = []
    for j in range(1, 4):
        before = jnp.concatenate([jnp.full((j,), -1, seg.dtype), seg[:n - j]])
        cols.append((before == seg).astype(F32))
    cols += [pad.astype(F32), seg.astype(F32)]
    cols += [jnp.zeros((n,), F32)] * 3
    return jnp.stack(cols, axis=1)


def rms_norm(value_rows, gain):
    return (
        value_rows
        * lax.rsqrt(jnp.mean(value_rows * value_rows, axis=-1, keepdims=True) + 1e-06)
        * gain
    )


def gather_t(value):
    return lax.all_gather(value, "tensor", axis=0, tiled=True)


def scatter_t(value):
    return lax.psum_scatter(value, "tensor", scatter_dimension=0, tiled=True)


def on_device(
    layer_input, segment_ids, pad_mask, attn_gain, ffn_gain, out_gain,
    qkv_weight, beta_weight, conv_weight, out_weight, expand_weight, down_weight, cotangent,
):
    resid = layer_input.astype(F32)
    width = qkv_weight.shape[3]
    heads = beta_weight.shape[2]
    qkv_full = lax.all_gather(qkv_weight[0], "fsdp", axis=1, tiled=True)
    beta_full = lax.all_gather(beta_weight[0], "fsdp", axis=0, tiled=True)
    expand_full = lax.all_gather(expand_weight[0], "fsdp", axis=1, tiled=True)
    out_full = lax.all_gather(out_weight[0], "fsdp", axis=1, tiled=True)
    down_full = lax.all_gather(down_weight[0], "fsdp", axis=1, tiled=True)
    wide = jnp.concatenate(
        [qkv_full[0], qkv_full[1], qkv_full[2], jnp.pad(beta_full, ((0, 0), (0, HEAD - heads)))], axis=1
    )
    normed = rms_norm(resid, attn_gain[0]).astype(BF)
    gathered = gather_t(normed)
    pre = jnp.dot(gathered, wide, preferred_element_type=F32)
    seg = segment_ids[0]
    cols = columns(seg, pad_mask[0])
    segr = seg.astype(F32)[None]
    mixed, *kept = mixer_fwd(pre, cols, segr, seg, conv_weight[0], out_gain)
    resid_mid = resid + scatter_t(jnp.dot(mixed, out_full, preferred_element_type=F32))
    normed_ffn = rms_norm(resid_mid, ffn_gain[0]).astype(BF)
    gathered_ffn = gather_t(normed_ffn)
    expanded = jnp.einsum("ld,sdf->slf", gathered_ffn, expand_full, preferred_element_type=F32)
    gate, up = expanded[0], expanded[1]
    sig = jax.nn.sigmoid(gate)
    hidden = (gate * sig * up).astype(BF)
    resid_out = resid_mid + scatter_t(jnp.dot(hidden, down_full, preferred_element_type=F32))
    block_outs = resid_out.astype(BF)[None]

    grad = cotangent.astype(F32)
    grad_full = gather_t(cotangent)
    d_hidden = lax.dot_general(grad_full, down_full, NT, preferred_element_type=F32)
    d_down = lax.dot_general(hidden, grad_full, TN, preferred_element_type=F32)
    d_gate = d_hidden * up * sig * (1.0 + gate * (1.0 - sig))
    d_up = d_hidden * gate * sig
    d_expanded = jnp.stack([d_gate, d_up]).astype(BF)
    d_expand = jnp.einsum("ld,slf->sdf", gathered_ffn, d_expanded, preferred_element_type=F32)
    d_normed_ffn = scatter_t(jnp.einsum("slf,sdf->ld", d_expanded, expand_full, preferred_element_type=F32))
    unused, norm_back = jax.vjp(rms_norm, resid_mid, ffn_gain[0])
    d_mid, d_ffn_gain = norm_back(d_normed_ffn)
    grad = grad + d_mid
    grad_full = gather_t(grad.astype(BF))
    d_mixed = lax.dot_general(grad_full, out_full, NT, preferred_element_type=F32)
    d_out = lax.dot_general(mixed, grad_full, TN, preferred_element_type=F32)
    d_wide, d_taps, d_head = mixer_bwd(d_mixed, pre, cols, segr, seg, conv_weight[0], out_gain, kept)
    d_all = lax.dot_general(gathered, d_wide, TN, preferred_element_type=F32)
    d_qkv = jnp.stack([d_all[:, i * width:(i + 1) * width] for i in range(3)])
    d_beta = d_all[:, 3 * width:3 * width + heads]
    d_normed = scatter_t(lax.dot_general(d_wide, wide, NT, preferred_element_type=F32))
    unused, norm_back = jax.vjp(rms_norm, resid, attn_gain[0])
    d_resid, d_attn_gain = norm_back(d_normed)
    grad = grad + d_resid
    qkv_grad = lax.psum_scatter(d_qkv, "fsdp", scatter_dimension=1, tiled=True)
    beta_grad = lax.psum_scatter(d_beta, "fsdp", scatter_dimension=0, tiled=True)
    expand_grad = lax.psum_scatter(d_expand, "fsdp", scatter_dimension=1, tiled=True)
    out_grad = lax.psum_scatter(d_out, "fsdp", scatter_dimension=1, tiled=True)
    down_grad = lax.psum_scatter(d_down, "fsdp", scatter_dimension=1, tiled=True)
    conv_grad = lax.psum(d_taps, "fsdp")
    attn_total, ffn_total, head_total = lax.psum((d_attn_gain[None], d_ffn_gain[None], d_head), ("fsdp", "tensor"))
    return (
        block_outs, grad, attn_total, ffn_total, head_total, qkv_grad[None], beta_grad[None],
        conv_grad[None], out_grad[None], expand_grad[None], down_grad[None],
    )


def solution(mesh):
    in_specs = (
        P(("fsdp", "tensor"), None),
        P("fsdp", None),
        P("fsdp", None),
        P(),
        P(),
        P(),
        P(None, None, "fsdp", "tensor"),
        P(None, "fsdp", "tensor"),
        P(None, None, None, "tensor"),
        P(None, "tensor", "fsdp"),
        P(None, None, "fsdp", "tensor"),
        P(None, "tensor", "fsdp"),
        P(("fsdp", "tensor"), None),
    )
    out_specs = (
        P(None, ("fsdp", "tensor"), None),
        P(("fsdp", "tensor"), None),
        P(),
        P(),
        P(),
        P(None, None, "fsdp", "tensor"),
        P(None, "fsdp", "tensor"),
        P(None, None, None, "tensor"),
        P(None, "tensor", "fsdp"),
        P(None, None, "fsdp", "tensor"),
        P(None, "tensor", "fsdp"),
    )
    return jax.shard_map(
        on_device, mesh=mesh, in_specs=in_specs, out_specs=out_specs, check_vma=False
    )
```

```python
import functools
import jax
import jax.numpy as jnp
from jax import lax
from jax.experimental import pallas as pl
from jax.experimental.pallas import tpu as pltpu
from jax.sharding import PartitionSpec as P

HEAD = 128
C = 128
F32 = jnp.float32
BF = jnp.bfloat16

NN = (((1,), (0,)), ((), ()))
NT = (((1,), (1,)), ((), ()))
TN = (((0,), (0,)), ((), ()))


def dot1(a, b, dims=NN):
    return lax.dot_general(a.astype(BF), b.astype(BF), dims, preferred_element_type=F32)


def split(x):
    hi = x.astype(BF)
    return hi, (x - hi.astype(F32)).astype(BF)


def dot3(a, b, dims=NN):
    a1, a2 = split(a) if not isinstance(a, tuple) else a
    b1, b2 = split(b) if not isinstance(b, tuple) else b
    d = functools.partial(lax.dot_general, dimension_numbers=dims, preferred_element_type=F32)
    return d(a1, b1) + (d(a1, b2) + d(a2, b1))


def block_masks():
    r = lax.broadcasted_iota(jnp.int32, (C, C), 0)
    c = lax.broadcasted_iota(jnp.int32, (C, C), 1)
    return r, c


def invert(systems, dot):
    r, c = block_masks()
    eye = (r == c).astype(F32)
    x = r ^ c
    out = [eye - jnp.where((x == 1), low, 0.0) for low in systems]
    size = 2
    while size < C:
        here = (x >= size) & (x < 2 * size)
        mids = [dot(jnp.where(here, low, 0.0), t) for low, t in zip(systems, out)]
        out = [t - dot(t, m) for t, m in zip(out, mids)]
        size *= 2
    return out


def sigmoid(x):
    return 1.0 / (1.0 + jnp.exp(-x))


def taps_down(ext, rows, j):
    return lax.slice_in_dim(ext, 8 - j, 8 - j + rows, axis=0)


def fwd_kernel(heads, cb, seg_s, pre_ref, cols_ref, segr_ref, taps_ref, gain_ref,
               mixed_ref, conv_ref, o_ref, t_ref, a_ref, p_ref, n_ref, z_ref, s_ref, u_ref, g_ref,
               tail, state):
    step = pl.program_id(0)
    width = heads * HEAD
    rows = cb * C
    taps = taps_ref.shape[1]

    @pl.when(step == 0)
    def _():
        tail[...] = jnp.zeros_like(tail)
        state[...] = jnp.zeros_like(state)

    r, c = block_masks()
    parts = []
    for i in range(3):
        cur = pre_ref[:, i * width:(i + 1) * width]
        ext = jnp.concatenate([tail[:, i * width:(i + 1) * width], cur], axis=0)
        tot = cur * taps_ref[i, 0:1, :]
        for j in range(1, taps):
            tot = tot + taps_down(ext, rows, j) * taps_ref[i, j:j + 1, :] * cols_ref[:, j - 1:j]
        tail[:, i * width:(i + 1) * width] = cur[rows - 8:, :]
        conv_ref[:, i * width:(i + 1) * width] = tot
        parts.append(tot * sigmoid(tot))
    eye = (r == c).astype(F32)
    items = []
    for b in range(cb):
        sl = slice(b * C, (b + 1) * C)
        chunk = step * cb + b
        first = chunk * C
        prev = jnp.where(first > 0, seg_s[jnp.maximum(first - 1, 0)], -1)
        last = seg_s[first + C - 1]
        keep = (prev == last).astype(F32)
        segc = cols_ref[sl, 4:5]
        segr = segr_ref[0:1, sl]
        same = segc == segr
        lead = (segc == prev.astype(F32)).astype(F32)
        trail = (segc == last.astype(F32)).astype(F32)
        for h in range(heads):
            hs = slice(h * HEAD, (h + 1) * HEAD)
            q, k, v = (part[sl, hs] for part in parts)
            q = q * lax.rsqrt(jnp.sum(q * q, axis=-1, keepdims=True) + 1e-6)
            k = k * lax.rsqrt(jnp.sum(k * k, axis=-1, keepdims=True) + 1e-6)
            beta = sigmoid(pre_ref[sl, 3 * width + h:3 * width + h + 1]) * cols_ref[sl, 3:4]
            items.append(dict(b=b, h=h, q=q, k=k, v=v, beta=beta, same=same, lead=lead, trail=trail, keep=keep, sl=sl, hs=hs))
    for it in items:
        it["kk"] = split(it["k"])
        p = jnp.where(it["same"] & (r > c), dot3(it["kk"], it["kk"], NT), 0.0)
        it["p"] = p
        it["low"] = p * it["beta"]
        it["a"] = jnp.where(it["same"] & (r >= c), dot3(it["q"], it["kk"], NT), 0.0)
    inv = invert([it["low"] for it in items], dot3)
    for it, t in zip(items, inv):
        rhs = jnp.concatenate([it["beta"] * it["v"], (it["beta"] * it["lead"]) * it["k"]], axis=1)
        tw = dot3(t, rhs)
        tws = split(tw)
        aw = dot3(it["a"], tws)
        bz = dot3(it["trail"] * it["k"], tws, TN)
        it["tv"], it["w"] = tw[:, :HEAD], tw[:, HEAD:]
        it["o0"], it["n"] = aw[:, :HEAD], it["lead"] * it["q"] - aw[:, HEAD:]
        it["bk"], it["z"] = bz[:, :HEAD], it["keep"] * eye - bz[:, HEAD:]
        it["t"] = t
    for it in items:
        b, h = it["b"], it["h"]
        s = state[h]
        ss = split(s)
        u = it["tv"] - dot3(it["w"], ss)
        o = it["o0"] + dot3(it["n"], ss)
        g = it["v"] - it["lead"] * dot3(it["kk"], ss)
        state[h] = it["bk"] + dot3(it["z"], ss)
        s_ref[b, h] = s
        u_ref[b, h] = u
        g_ref[b, h] = g
        t_ref[b, h] = it["t"]
        a_ref[b, h] = it["a"]
        p_ref[b, h] = it["p"]
        n_ref[b, h] = it["n"]
        z_ref[b, h] = it["z"]
        o_ref[it["sl"], it["hs"]] = o
        mixed_ref[it["sl"], it["hs"]] = (o * lax.rsqrt(jnp.mean(o * o, axis=-1, keepdims=True) + 1e-5) * gain_ref[0:1, :]).astype(BF)


def bwd_kernel(heads, cb, seg_s, dmix_ref, pre_ref, conv_ref, o_ref, cols_ref, segr_ref, taps_ref, gain_ref,
               t_ref, a_ref, p_ref, n_ref, z_ref, s_ref, u_ref, g_ref,
               dpre_ref, dtap_ref, dgain_ref,
               head_rows, dstate):
    step = pl.program_id(0)
    steps = pl.num_programs(0)
    width = heads * HEAD
    rows = cb * C
    taps = taps_ref.shape[1]
    back = steps - 1 - step

    @pl.when(step == 0)
    def _():
        head_rows[...] = jnp.zeros_like(head_rows)
        dstate[...] = jnp.zeros_like(dstate)
        dtap_ref[...] = jnp.zeros_like(dtap_ref)
        dgain_ref[...] = jnp.zeros_like(dgain_ref)

    r, c = block_masks()
    dcs = [[[None] * heads for _ in range(cb)] for _ in range(3)]
    dgain = jnp.zeros((1, HEAD), F32)
    dlog = [None] * cb
    for b in reversed(range(cb)):
        sl = slice(b * C, (b + 1) * C)
        chunk = back * cb + b
        first = chunk * C
        prev = jnp.where(first > 0, seg_s[jnp.maximum(first - 1, 0)], -1)
        last = seg_s[first + C - 1]
        segc = cols_ref[sl, 4:5]
        segr = segr_ref[0:1, sl]
        same = segc == segr
        lead = (segc == prev.astype(F32)).astype(F32)
        trail = (segc == last.astype(F32)).astype(F32)
        lane = lax.broadcasted_iota(jnp.int32, (C, HEAD), 1)
        dl = jnp.zeros((C, HEAD), F32)
        for h in range(heads):
            hs = slice(h * HEAD, (h + 1) * HEAD)
            cq, ck, cv = (conv_ref[sl, i * width + h * HEAD:i * width + (h + 1) * HEAD] for i in range(3))
            gq, gk, gv = sigmoid(cq), sigmoid(ck), sigmoid(cv)
            q, k = cq * gq, ck * gk
            rq = lax.rsqrt(jnp.sum(q * q, axis=-1, keepdims=True) + 1e-6)
            rk = lax.rsqrt(jnp.sum(k * k, axis=-1, keepdims=True) + 1e-6)
            q, k = q * rq, k * rk
            gb = sigmoid(pre_ref[sl, 3 * width + h:3 * width + h + 1])
            pad = cols_ref[sl, 3:4]
            beta = gb * pad
            o = o_ref[sl, hs]
            dm = dmix_ref[sl, hs]
            ro = lax.rsqrt(jnp.mean(o * o, axis=-1, keepdims=True) + 1e-5)
            oh = o * ro
            dgain = dgain + jnp.sum(dm * oh, axis=0, keepdims=True)
            du0 = dm * gain_ref[0:1, :]
            do = ro * (du0 - oh * jnp.mean(du0 * oh, axis=-1, keepdims=True))
            ds1 = dstate[h]
            u = u_ref[b, h]
            s = s_ref[b, h]
            a = a_ref[b, h]
            p = p_ref[b, h]
            ks = split(k)
            ds1s = split(ds1)
            dos = split(do)
            us = split(u)
            dstate[h] = dot3(z_ref[b, h], ds1s, TN) + dot3(n_ref[b, h], dos, TN)
            du = dot3(a, dos, TN) + trail * dot3(ks, ds1s)
            dr = dot3(t_ref[b, h], du, TN)
            drs = split(dr)
            ss = split(s)
            dlow = jnp.where(same & (r > c), -dot3(drs, us, NT), 0.0)
            da = jnp.where(same & (r >= c), dot3(dos, us, NT), 0.0)
            dv = beta * dr
            dbeta = jnp.sum(dr * g_ref[b, h] , axis=-1, keepdims=True) + jnp.sum(dlow * p, axis=-1, keepdims=True)
            dp = split(beta * dlow)
            das = split(da)
            dq = lead * dot3(dos, ss, NT) + dot3(das, ks)
            dk = (dot3(das, q, TN) + trail * dot3(us, ds1s, NT) - (beta * lead) * dot3(drs, ss, NT)
                  + dot3(dp, ks) + dot3(dp, ks, TN))
            dsq = rq * (dq - q * jnp.sum(q * dq, axis=-1, keepdims=True))
            dsk = rk * (dk - k * jnp.sum(k * dk, axis=-1, keepdims=True))
            dcs[0][b][h] = dsq * gq * (1.0 + cq * (1.0 - gq))
            dcs[1][b][h] = dsk * gk * (1.0 + ck * (1.0 - gk))
            dcs[2][b][h] = dv * gv * (1.0 + cv * (1.0 - gv))
            dl = jnp.where(lane == h, dbeta * pad * gb * (1.0 - gb), dl)
        dlog[b] = dl
    dgain_ref[...] += dgain
    for b in range(cb):
        dpre_ref[b * C:(b + 1) * C, 3 * width:] = dlog[b].astype(BF)
    for i in range(3):
        dc = jnp.concatenate([jnp.concatenate(dcs[i][b], axis=1) for b in range(cb)], axis=0)
        pre = pre_ref[:, i * width:(i + 1) * width]
        tot = dc * taps_ref[i, 0:1, :]
        grads = [jnp.sum(dc * pre, axis=0, keepdims=True)]
        for j in range(1, taps):
            e = dc * cols_ref[:, j - 1:j]
            ext = jnp.concatenate([e, head_rows[j - 1, :, i * width:(i + 1) * width]], axis=0)
            head_rows[j - 1, :, i * width:(i + 1) * width] = e[:8]
            e = lax.slice_in_dim(ext, j, j + rows, axis=0)
            tot = tot + e * taps_ref[i, j:j + 1, :]
            grads.append(jnp.sum(e * pre, axis=0, keepdims=True))
        dpre_ref[:, i * width:(i + 1) * width] = tot.astype(BF)
        dtap_ref[i] += jnp.concatenate(grads, axis=0)


def mixer_fwd(pre, cols, segr, seg, taps, gain, cb=2):
    n, wide = pre.shape
    width = taps.shape[2]
    heads = width // HEAD
    rows = cb * C
    chunks = n // C
    sq = jax.ShapeDtypeStruct((chunks, heads, C, HEAD), F32)
    sqspec = pl.BlockSpec((cb, heads, C, HEAD), lambda i, s: (i, 0, 0, 0))
    row = lambda w: pl.BlockSpec((rows, w), lambda i, s: (i, 0))
    return pl.pallas_call(
        functools.partial(fwd_kernel, heads, cb),
        grid_spec=pltpu.PrefetchScalarGridSpec(
            num_scalar_prefetch=1, grid=(n // rows,),
            in_specs=[row(wide), row(cols.shape[1]), pl.BlockSpec((1, rows), lambda i, s: (0, i)),
                      pl.BlockSpec(taps.shape, lambda i, s: (0, 0, 0)), pl.BlockSpec((1, HEAD), lambda i, s: (0, 0))],
            out_specs=[row(width), row(3 * width), row(width)] + [sqspec] * 8,
            scratch_shapes=[pltpu.VMEM((8, 3 * width), F32), pltpu.VMEM((heads, HEAD, HEAD), F32)]),
        out_shape=[jax.ShapeDtypeStruct((n, width), BF), jax.ShapeDtypeStruct((n, 3 * width), F32),
                   jax.ShapeDtypeStruct((n, width), F32)] + [sq] * 8,
        compiler_params=pltpu.CompilerParams(dimension_semantics=("arbitrary",), vmem_limit_bytes=48 * 2**20),
        name="mixer_fwd",
    )(seg, pre, cols, segr, taps, gain)


def mixer_bwd(dmix, pre, cols, segr, seg, taps, gain, kept, cb=2):
    conv, o, *rest = kept
    n, wide = pre.shape
    width = taps.shape[2]
    heads = width // HEAD
    rows = cb * C
    steps = n // rows
    sqspec = pl.BlockSpec((cb, heads, C, HEAD), lambda i, s: (steps - 1 - i, 0, 0, 0))
    row = lambda w: pl.BlockSpec((rows, w), lambda i, s: (steps - 1 - i, 0))
    ntap = taps.shape[1]
    return pl.pallas_call(
        functools.partial(bwd_kernel, heads, cb),
        grid_spec=pltpu.PrefetchScalarGridSpec(
            num_scalar_prefetch=1, grid=(steps,),
            in_specs=[row(width), row(wide), row(3 * width), row(width), row(cols.shape[1]),
                      pl.BlockSpec((1, rows), lambda i, s: (0, steps - 1 - i)),
                      pl.BlockSpec(taps.shape, lambda i, s: (0, 0, 0)), pl.BlockSpec((1, HEAD), lambda i, s: (0, 0))] + [sqspec] * 8,
            out_specs=[row(wide), pl.BlockSpec(taps.shape, lambda i, s: (0, 0, 0)), pl.BlockSpec((1, HEAD), lambda i, s: (0, 0))],
            scratch_shapes=[pltpu.VMEM((ntap - 1, 8, 3 * width), F32), pltpu.VMEM((heads, HEAD, HEAD), F32)]),
        out_shape=[jax.ShapeDtypeStruct((n, wide), BF), jax.ShapeDtypeStruct(taps.shape, F32), jax.ShapeDtypeStruct((1, HEAD), F32)],
        compiler_params=pltpu.CompilerParams(dimension_semantics=("arbitrary",), vmem_limit_bytes=48 * 2**20),
        name="mixer_bwd",
    )(seg, dmix, pre, conv, o, cols, segr, taps, gain, *rest)


def columns(seg, pad):
    n = seg.shape[0]
    cols = []
    for j in range(1, 4):
        before = jnp.concatenate([jnp.full((j,), -1, seg.dtype), seg[:n - j]])
        cols.append((before == seg).astype(F32))
    cols += [pad.astype(F32), seg.astype(F32)]
    cols += [jnp.zeros((n,), F32)] * 3
    return jnp.stack(cols, axis=1)


def hop(value, axis, bit):
    n = lax.axis_size(axis)
    return lax.ppermute(value, axis, [(i, i ^ bit) for i in range(n)])


def tensor_bits():
    n = lax.axis_size("tensor")
    bits = []
    while n > 1:
        n //= 2
        bits.append(n)
    return bits


def gather_relative(value):
    blocks = value[None]
    for bit in tensor_bits():
        blocks = jnp.concatenate([blocks, hop(blocks, "tensor", bit)], axis=0)
    return blocks


def relative_order():
    order = [0]
    for bit in tensor_bits():
        order = order + [k ^ bit for k in order]
    return order


def gather_rows(value):
    n = lax.axis_size("tensor")
    me = lax.axis_index("tensor")
    blocks = [(0, value)]
    for bit in tensor_bits():
        sent = jnp.stack([b for _, b in blocks])
        got = hop(sent, "tensor", bit)
        blocks = blocks + [(k ^ bit, got[i]) for i, (k, _) in enumerate(blocks)]
    full = jnp.zeros((n,) + value.shape, value.dtype)
    for k, b in blocks:
        full = lax.dynamic_update_slice(full, b[None], (me ^ k,) + (0,) * value.ndim)
    return full.reshape((n * value.shape[0],) + value.shape[1:])


def ring_order(n):
    return [i for i in range(0, n, 2)] + [i for i in reversed(range(1, n, 2))]


def ring_gather(value):
    n = lax.axis_size("fsdp")
    order = ring_order(n)
    place = jnp.array([order.index(i) for i in range(n)], jnp.int32)
    there = jnp.array(order, jnp.int32)
    me = place[lax.axis_index("fsdp")]
    right = [(order[i], order[(i + 1) % n]) for i in range(n)]
    left = [(b, a) for a, b in right]
    rows = value.shape[0]
    full = jnp.zeros((n * rows,) + value.shape[1:], value.dtype)

    def put(full, part, steps, start):
        owner = there[lax.rem(me + steps + n, n)]
        return lax.dynamic_update_slice(full, part, (owner * rows + start,) + (0,) * (value.ndim - 1))

    full = put(full, value, 0, 0)
    a = b = value
    for k in range(1, n // 2 + 1):
        if 2 * k == n and rows % 32 == 0:
            half = rows // 2
            a = lax.ppermute(a[:half], "fsdp", right)
            b = lax.ppermute(b[half:], "fsdp", left)
            full = put(put(full, a, -k, 0), b, k, half)
        else:
            a = lax.ppermute(a, "fsdp", right)
            full = put(full, a, -k, 0)
            if 2 * k < n:
                b = lax.ppermute(b, "fsdp", left)
                full = put(full, b, k, 0)
    return full


def owner_sum(parts):
    n = lax.axis_size("fsdp")
    me = lax.axis_index("fsdp")
    total = lax.dynamic_index_in_dim(parts, me, 0, keepdims=False).astype(F32)
    got = []
    for k in range(1, n):
        block = lax.dynamic_index_in_dim(parts, me ^ k, 0, keepdims=False)
        got.append(hop(block, "fsdp", k))
    for g in got:
        total = total + g.astype(F32)
    return total


def all_sum(value, axis):
    n = lax.axis_size(axis)
    bit = 1
    while bit < n:
        value = value + hop(value, axis, bit)
        bit *= 2
    return value


def core_scatter(parts):
    core = lax.axis_index("tensor") % 2
    mine = lax.dynamic_index_in_dim(parts, core, 1, keepdims=False)
    theirs = lax.dynamic_index_in_dim(parts, 1 - core, 1, keepdims=False).astype(BF)
    return mine + hop(theirs, "tensor", 1).astype(F32)


def scatter_rows(parts):
    n = lax.axis_size("tensor")
    rows = parts.shape[0] // n
    blocks = core_scatter(parts.reshape(n // 2, 2, rows, parts.shape[1]))
    chip = lax.axis_index("tensor") // 2
    total = lax.dynamic_index_in_dim(blocks, chip, 0, keepdims=False)
    for k in range(1, n // 2):
        sent = lax.dynamic_index_in_dim(blocks, chip ^ k, 0, keepdims=False).astype(BF)
        total = total + hop(sent, "tensor", 2 * k).astype(F32)
    return total


def norm_factor(rows):
    return lax.rsqrt(jnp.mean(rows * rows, axis=-1, keepdims=True) + 1e-06)


def norm_grad(rows, factor, gain, d_normed):
    u = d_normed * gain
    return factor * u - rows * (factor * factor * factor) * jnp.mean(u * rows, axis=-1, keepdims=True)


def on_device(
    layer_input, segment_ids, pad_mask, attn_gain, ffn_gain, out_gain,
    qkv_weight, beta_weight, conv_weight, out_weight, expand_weight, down_weight, cotangent,
):
    n_t = lax.axis_size("tensor")
    n_f = lax.axis_size("fsdp")
    me_t = lax.axis_index("tensor")
    core = me_t % 2
    rows, d_model = layer_input.shape
    tokens = n_t * rows
    width = qkv_weight.shape[3]
    heads = beta_weight.shape[2]
    ff = down_weight.shape[1]
    shard = qkv_weight.shape[2]

    w = qkv_weight[0]
    wide_own = jnp.concatenate(
        [w[0], w[1], w[2], jnp.pad(beta_weight[0], ((0, 0), (0, HEAD - heads)))], axis=1
    )
    ffn_own = jnp.concatenate(
        [expand_weight[0, 0].T, expand_weight[0, 1].T, down_weight[0], out_weight[0]], axis=0
    )
    wide = ring_gather(wide_own)
    x_full = gather_rows(layer_input)
    ffn_all = lax.all_gather(ffn_own, "fsdp", axis=1, tiled=True)
    g_f = gather_rows(cotangent)

    seg = segment_ids[0]
    cols = columns(seg, pad_mask[0])
    segr = seg.astype(F32)[None]

    x_rows = x_full.astype(F32)
    factor_a = norm_factor(x_rows)
    normed_a = (x_rows * factor_a * attn_gain).astype(BF)
    pre = jnp.dot(normed_a, wide, preferred_element_type=F32)
    mixed, *kept = mixer_fwd(pre, cols, segr, seg, conv_weight[0], out_gain)

    expand_t = ffn_all[:2 * ff]
    down = ffn_all[2 * ff:3 * ff]
    out_own = ffn_all[3 * ff:]
    out_rel = gather_relative(out_own).reshape(n_t * width, d_model)
    mixed_rel = gather_relative(mixed)
    mixed_rel = jnp.concatenate([mixed_rel[i] for i in range(n_t)], axis=1)
    x_mid = x_rows + jnp.dot(mixed_rel, out_rel, preferred_element_type=F32)
    factor_f = norm_factor(x_mid)
    normed_f = (x_mid * factor_f * ffn_gain).astype(BF)

    expanded = lax.dot_general(expand_t, normed_f, NT, preferred_element_type=F32)
    gate, up = expanded[:ff], expanded[ff:]
    d_hidden = lax.dot_general(down, g_f, NT, preferred_element_type=F32)
    sig = jax.nn.sigmoid(gate)
    hidden = (gate * sig * up).astype(BF)
    d_gate = d_hidden * up * sig * (1.0 + gate * (1.0 - sig))
    d_up = d_hidden * gate * sig
    d_expanded = jnp.concatenate([d_gate.astype(BF), d_up.astype(BF)], axis=0)

    d_nf = lax.dot_general(d_expanded, expand_t, TN, preferred_element_type=F32)
    d_ffn_gain = jnp.sum(d_nf * (x_mid * factor_f), axis=0)
    d_nf = core_scatter(d_nf.reshape(n_t // 2, 2, rows, d_model))
    low = d_nf.astype(BF)
    d_nf = low.astype(F32)
    for k in range(1, n_t // 2):
        d_nf = d_nf + hop(low, "tensor", 2 * k).astype(F32)

    def of_core(full):
        return lax.dynamic_index_in_dim(full.reshape(n_t // 2, 2, rows, full.shape[1]), core, 1, keepdims=False)

    grad = of_core(g_f).astype(F32) + norm_grad(of_core(x_mid), of_core(factor_f), ffn_gain, d_nf)
    g_low = grad.astype(BF)
    other = hop(g_low, "tensor", 1)
    g_a = jnp.zeros((n_t // 2, 2, rows, d_model), BF)
    g_a = lax.dynamic_update_slice(g_a, g_low[:, None], (0, core, 0, 0))
    g_a = lax.dynamic_update_slice(g_a, other[:, None], (0, 1 - core, 0, 0))
    g_a = g_a.reshape(tokens, d_model)
    grad_own = lax.dynamic_index_in_dim(grad, me_t // 2, 0, keepdims=False)

    d_down = jnp.dot(hidden, g_f, preferred_element_type=BF)
    d_expand = jnp.dot(d_expanded, normed_f, preferred_element_type=BF)
    d_ffn = lax.psum_scatter(
        jnp.concatenate([d_expand, d_down], axis=0), "fsdp", scatter_dimension=1, tiled=True
    )

    d_mixed = lax.dot_general(g_a, out_own, NT, preferred_element_type=F32)
    d_wide, d_taps, d_head = mixer_bwd(d_mixed, pre, cols, segr, seg, conv_weight[0], out_gain, kept)
    d_out = lax.dot_general(mixed, g_a, TN, preferred_element_type=F32).astype(BF)
    out_grad = owner_sum(d_out.reshape(width, n_f, shard).transpose(1, 0, 2))

    ffn_part = lax.dot_general(hidden, down, TN, preferred_element_type=F32)
    own_mid = lax.dynamic_slice(x_mid, (me_t * rows, 0), (rows, d_model))
    block_outs = (own_mid + scatter_rows(ffn_part)).astype(BF)[None]

    d_all = lax.dot_general(normed_a, d_wide, TN, preferred_element_type=F32)
    qkv_sum = owner_sum(d_all[:, :3 * width].astype(BF).reshape(n_f, shard, 3 * width))
    qkv_grad = jnp.stack([qkv_sum[:, i * width:(i + 1) * width] for i in range(3)])
    d_na = lax.dot_general(d_wide, wide, NT, preferred_element_type=F32)
    d_attn_gain = jnp.sum(d_na * (x_rows * factor_a), axis=0)
    d_na = scatter_rows(d_na)
    own_x = layer_input.astype(F32)
    input_grad = grad_own + norm_grad(own_x, norm_factor(own_x), attn_gain, d_na)

    gains = jnp.concatenate([d_attn_gain, d_ffn_gain, d_head[0]]).reshape(-1, HEAD)
    gains = all_sum(gains, "tensor")
    d_beta = d_all[:, 3 * width:3 * width + heads].T.reshape(-1, HEAD)
    taps = d_taps.reshape(-1, HEAD)
    small = all_sum(jnp.concatenate([taps, d_beta, gains], axis=0), "fsdp")
    n1 = taps.shape[0]
    n2 = n1 + d_beta.shape[0]
    conv_grad = small[:n1].reshape(d_taps.shape)
    beta_all = small[n1:n2].reshape(heads, d_model)
    beta_grad = lax.dynamic_slice(beta_all, (0, lax.axis_index("fsdp") * shard), (heads, shard)).T
    gains = small[n2:].reshape(-1)
    attn_total = gains[:d_model][None]
    ffn_total = gains[d_model:2 * d_model][None]
    head_total = gains[2 * d_model:][None]

    expand_grad = jnp.stack([d_ffn[:ff].T, d_ffn[ff:2 * ff].T]).astype(F32)
    down_grad = d_ffn[2 * ff:].astype(F32)
    return (
        block_outs, input_grad, attn_total, ffn_total, head_total, qkv_grad[None], beta_grad[None],
        conv_grad[None], out_grad[None], expand_grad[None], down_grad[None],
    )


def solution(mesh):
    in_specs = (
        P(("fsdp", "tensor"), None),
        P("fsdp", None),
        P("fsdp", None),
        P(),
        P(),
        P(),
        P(None, None, "fsdp", "tensor"),
        P(None, "fsdp", "tensor"),
        P(None, None, None, "tensor"),
        P(None, "tensor", "fsdp"),
        P(None, None, "fsdp", "tensor"),
        P(None, "tensor", "fsdp"),
        P(("fsdp", "tensor"), None),
    )
    out_specs = (
        P(None, ("fsdp", "tensor"), None),
        P(("fsdp", "tensor"), None),
        P(),
        P(),
        P(),
        P(None, None, "fsdp", "tensor"),
        P(None, "fsdp", "tensor"),
        P(None, None, None, "tensor"),
        P(None, "tensor", "fsdp"),
        P(None, None, "fsdp", "tensor"),
        P(None, "tensor", "fsdp"),
    )
    return jax.shard_map(
        on_device, mesh=mesh, in_specs=in_specs, out_specs=out_specs, check_vma=False
    )
```

```python
import functools
import jax
import jax.numpy as jnp
from jax import lax
from jax.experimental import pallas as pl
from jax.experimental.pallas import tpu as pltpu
from jax.sharding import PartitionSpec as P

HEAD = 128
C = 128
F32 = jnp.float32
BF = jnp.bfloat16

NN = (((1,), (0,)), ((), ()))
NT = (((1,), (1,)), ((), ()))
TN = (((0,), (0,)), ((), ()))


def dot1(a, b, dims=NN):
    return lax.dot_general(a.astype(BF), b.astype(BF), dims, preferred_element_type=F32)


def split(x):
    hi = x.astype(BF)
    return hi, (x - hi.astype(F32)).astype(BF)


def dot3(a, b, dims=NN):
    a1, a2 = split(a) if not isinstance(a, tuple) else a
    b1, b2 = split(b) if not isinstance(b, tuple) else b
    ka, kb = dims[0][0][0], dims[0][1][0]
    left = jnp.concatenate([a1, a2], axis=ka)
    n = b1.shape[1 - kb]
    if n == 128:
        right = jnp.concatenate([jnp.concatenate([b1, b2], axis=1 - kb), jnp.concatenate([b1, jnp.zeros_like(b1)], axis=1 - kb)], axis=kb)
        r = lax.dot_general(left, right, dims, preferred_element_type=F32)
        return r[:, :128] + r[:, 128:]
    r = lax.dot_general(left, jnp.concatenate([b1, b1], axis=kb), dims, preferred_element_type=F32)
    return r + lax.dot_general(a1, b2, dims, preferred_element_type=F32)


def dot3_old(a, b, dims=NN):
    a1, a2 = split(a) if not isinstance(a, tuple) else a
    b1, b2 = split(b) if not isinstance(b, tuple) else b
    d = functools.partial(lax.dot_general, dimension_numbers=dims, preferred_element_type=F32)
    return d(a1, b1) + (d(a1, b2) + d(a2, b1))


def block_masks():
    r = lax.broadcasted_iota(jnp.int32, (C, C), 0)
    c = lax.broadcasted_iota(jnp.int32, (C, C), 1)
    return r, c


def invert(systems, dot):
    r, c = block_masks()
    eye = (r == c).astype(F32)
    x = r ^ c
    lows = [low.astype(BF) for low in systems]
    out = [eye - jnp.where((x == 1), low, 0.0) for low in systems]
    size = 2
    while size < C:
        here = (x >= size) & (x < 2 * size)
        short = [t.astype(BF) for t in out]
        mids = [dot1(jnp.where(here, low, 0.0).astype(BF), t) for low, t in zip(lows, short)]
        out = [t - dot1(b, m) for t, b, m in zip(out, short, mids)]
        size *= 2
    splits = [split(t) for t in out]
    errors = [eye - t - dot(low, p) for low, t, p in zip(systems, out, splits)]
    return [t + dot1(p[0], e) for t, p, e in zip(out, splits, errors)]


def sigmoid(x):
    return 1.0 / (1.0 + jnp.exp(-x))


def taps_down(ext, rows, j):
    return lax.slice_in_dim(ext, 8 - j, 8 - j + rows, axis=0)


def row_sum(x):
    return jnp.dot(x.astype(BF), jnp.ones((HEAD, HEAD), BF), preferred_element_type=F32)


def head_norm(x):
    return x * lax.rsqrt(row_sum(x * x) + 1e-6)


def segment_parts(seg_s, cols_ref, segr_ref, first, sl):
    prev = jnp.where(first > 0, seg_s[jnp.maximum(first - 1, 0)], -1)
    last = seg_s[first + C - 1]
    segc = cols_ref[sl, 4:5]
    same = segc == segr_ref[0:1, sl]
    lead = (segc == prev.astype(F32)).astype(F32)
    trail = (segc == last.astype(F32)).astype(F32)
    return same, lead, trail, (prev == last).astype(F32)


def fwd_kernel(heads, cb, base, seg_s, x_ref, wide_ref, again_ref, cols_ref, segr_ref, taps_ref, gain_ref, tail_in, state_in,
               mixed_ref, kept_ref, na_ref, pre_ref, conv_ref, o_ref, t_ref, a_ref, p_ref, n_ref, z_ref, s_ref, u_ref, g_ref,
               tail, state, line):
    step = pl.program_id(0)
    width = heads * HEAD
    rows = cb * C
    taps = taps_ref.shape[1]

    @pl.when(step == 0)
    def _():
        tail[...] = tail_in[...]
        state[...] = state_in[...]

    r, c = block_masks()
    x = x_ref[...].astype(F32)
    na = (x * lax.rsqrt(jnp.mean(x * x, axis=-1, keepdims=True) + 1e-6) * again_ref[0:1, :]).astype(BF)
    na_ref[...] = na
    pre_ref[...] = jnp.dot(na, wide_ref[...], preferred_element_type=F32)
    tap = lambda j: jnp.concatenate([taps_ref[i, j:j + 1, :] for i in range(3)], axis=1)
    cur = pre_ref[:, :3 * width]
    line[:8, :] = tail[...]
    line[8:, :] = cur
    tot = cur * tap(0)
    for j in range(1, taps):
        tot = tot + line[8 - j:8 - j + rows, :] * tap(j) * cols_ref[:, j - 1:j]
    tail[...] = line[rows:, :]
    conv_ref[...] = tot
    tot = tot * sigmoid(tot)
    parts = [tot[:, i * width:(i + 1) * width] for i in range(3)]
    eye = (r == c).astype(F32)
    items = []
    for b in range(cb):
        sl = slice(b * C, (b + 1) * C)
        same, lead, trail, keep = segment_parts(seg_s, cols_ref, segr_ref, ((base + step) * cb + b) * C, sl)
        for h in range(heads):
            hs = slice(h * HEAD, (h + 1) * HEAD)
            q, k, v = (part[sl, hs] for part in parts)
            beta = sigmoid(pre_ref[sl, 3 * width + h:3 * width + h + 1]) * cols_ref[sl, 3:4]
            items.append(dict(b=b, h=h, q=head_norm(q), k=head_norm(k), v=v, beta=beta, same=same, lead=lead,
                              trail=trail, keep=keep, sl=sl, hs=hs))
    for it in items:
        it["kk"] = split(it["k"])
        p = jnp.where(it["same"] & (r > c), dot3(it["kk"], it["kk"], NT), 0.0)
        it["p"] = p
        it["low"] = p * it["beta"]
        it["a"] = jnp.where(it["same"] & (r >= c), dot3(it["q"], it["kk"], NT), 0.0)
    inv = invert([it["low"] for it in items], dot3)
    for it, t in zip(items, inv):
        rhs = jnp.concatenate([it["beta"] * it["v"], (it["beta"] * it["lead"]) * it["k"]], axis=1)
        tw = dot3(t, rhs)
        tws = split(tw)
        aw = dot3(it["a"], tws)
        bz = dot3(it["trail"] * it["k"], tws, TN)
        it["tv"], it["w"] = tw[:, :HEAD], tw[:, HEAD:]
        it["o0"], it["n"] = aw[:, :HEAD], it["lead"] * it["q"] - aw[:, HEAD:]
        it["bk"], it["z"] = bz[:, :HEAD], it["keep"] * eye - bz[:, HEAD:]
        it["t"] = t
    for it in items:
        b, h = it["b"], it["h"]
        s = state[h]
        ss = split(s)
        u = it["tv"] - dot3(it["w"], ss)
        o = it["o0"] + dot3(it["n"], ss)
        g = it["v"] - it["lead"] * dot3(it["kk"], ss)
        state[h] = it["bk"] + dot3(it["z"], ss)
        s_ref[b, h] = s
        u_ref[b, h] = u
        g_ref[b, h] = g
        t_ref[b, h] = it["t"]
        a_ref[b, h] = it["a"]
        p_ref[b, h] = it["p"]
        n_ref[b, h] = it["n"]
        z_ref[b, h] = it["z"]
        o_ref[it["sl"], it["hs"]] = o
        mixed = (o * lax.rsqrt(row_sum(o * o) * (1.0 / HEAD) + 1e-5) * gain_ref[0:1, :]).astype(BF)
        mixed_ref[it["sl"], it["hs"]] = mixed
        kept_ref[it["sl"], it["hs"]] = mixed


def stage_bits(n):
    bits = [1 << i for i in range(n.bit_length() - 1)]
    return bits, bits[1:] + bits[:1]


def bwd_kernel(heads, cb, n_f, shard, seg_s, ga0_ref, ga0c_ref, ga1_ref, ga1c_ref, mix_ref, na_ref, out_ref, wide_ref, x_ref, dffn0_ref, dffn1_ref,
               pre_ref, conv_ref, o_ref, cols_ref, segr_ref, taps_ref, gain_ref,
               t_ref, a_ref, p_ref, n_ref, z_ref, s_ref, u_ref, g_ref,
               away1_ref, keep1_ref, away2_ref, keep2_ref, sna_ref, kna_ref, gains_ref, small_ref,
               head_rows, dstate, acc, dpre):
    step = pl.program_id(0)
    steps = pl.num_programs(0)
    width = heads * HEAD
    rows = cb * C
    taps = taps_ref.shape[1]
    back = steps - 1 - step
    core = lax.axis_index("tensor") % 2

    @pl.when(step == 0)
    def _():
        head_rows[...] = jnp.zeros_like(head_rows)
        dstate[...] = jnp.zeros_like(dstate)
        acc[...] = jnp.zeros_like(acc)
        gains_ref[...] = jnp.zeros_like(gains_ref)
        gains_ref[1:2, :] = dffn0_ref[...] + dffn1_ref[...]
        small_ref[...] = jnp.zeros_like(small_ref)

    r, c = block_masks()
    dcs = [[[None] * heads for _ in range(cb)] for _ in range(3)]
    dgain = jnp.zeros((1, HEAD), F32)
    dlog = [None] * cb
    ga = jnp.where(back % 2 == core, jnp.where(back >= 2, ga1_ref[...], ga0_ref[...]),
                   jnp.where(back >= 2, ga1c_ref[...], ga0c_ref[...]))
    dmix = jnp.dot(ga, out_ref[...], preferred_element_type=F32)
    acc[:, 3 * width:4 * width] += lax.dot_general(ga, mix_ref[...], TN, preferred_element_type=F32)
    for b in reversed(range(cb)):
        sl = slice(b * C, (b + 1) * C)
        same, lead, trail, keep = segment_parts(seg_s, cols_ref, segr_ref, (back * cb + b) * C, sl)
        lane = lax.broadcasted_iota(jnp.int32, (C, HEAD), 1)
        dl = jnp.zeros((C, HEAD), F32)
        for h in range(heads):
            hs = slice(h * HEAD, (h + 1) * HEAD)
            cq, ck, cv = (conv_ref[sl, i * width + h * HEAD:i * width + (h + 1) * HEAD] for i in range(3))
            gq, gk, gv = sigmoid(cq), sigmoid(ck), sigmoid(cv)
            q, k = cq * gq, ck * gk
            rq = lax.rsqrt(jnp.sum(q * q, axis=-1, keepdims=True) + 1e-6)
            rk = lax.rsqrt(jnp.sum(k * k, axis=-1, keepdims=True) + 1e-6)
            q, k = q * rq, k * rk
            gb = sigmoid(pre_ref[sl, 3 * width + h:3 * width + h + 1])
            pad = cols_ref[sl, 3:4]
            beta = gb * pad
            o = o_ref[sl, hs]
            dm = dmix[sl, hs]
            ro = lax.rsqrt(jnp.mean(o * o, axis=-1, keepdims=True) + 1e-5)
            oh = o * ro
            dgain = dgain + jnp.sum(dm * oh, axis=0, keepdims=True)
            du0 = dm * gain_ref[0:1, :]
            do = ro * (du0 - oh * jnp.mean(du0 * oh, axis=-1, keepdims=True))
            ds1 = dstate[h]
            u = u_ref[b, h]
            s = s_ref[b, h]
            a = a_ref[b, h]
            p = p_ref[b, h]
            ks = split(k)
            ds1s = split(ds1)
            dos = split(do)
            us = split(u)
            dstate[h] = dot3(z_ref[b, h], ds1s, TN) + dot3(n_ref[b, h], dos, TN)
            du = dot3(a, dos, TN) + trail * dot3(ks, ds1s)
            dr = dot3(t_ref[b, h], du, TN)
            drs = split(dr)
            ss = split(s)
            dlow = jnp.where(same & (r > c), -dot3(drs, us, NT), 0.0)
            da = jnp.where(same & (r >= c), dot3(dos, us, NT), 0.0)
            dv = beta * dr
            dbeta = jnp.sum(dr * g_ref[b, h] , axis=-1, keepdims=True) + jnp.sum(dlow * p, axis=-1, keepdims=True)
            dp = split(beta * dlow)
            das = split(da)
            dq = lead * dot3(dos, ss, NT) + dot3(das, ks)
            dk = (dot3(das, q, TN) + trail * dot3(us, ds1s, NT) - (beta * lead) * dot3(drs, ss, NT)
                  + dot3(dp, ks) + dot3(dp, ks, TN))
            dsq = rq * (dq - q * jnp.sum(q * dq, axis=-1, keepdims=True))
            dsk = rk * (dk - k * jnp.sum(k * dk, axis=-1, keepdims=True))
            dcs[0][b][h] = dsq * gq * (1.0 + cq * (1.0 - gq))
            dcs[1][b][h] = dsk * gk * (1.0 + ck * (1.0 - gk))
            dcs[2][b][h] = dv * gv * (1.0 + cv * (1.0 - gv))
            dl = jnp.where(lane == h, dbeta * pad * gb * (1.0 - gb), dl)
        dlog[b] = dl
    gains_ref[2:3, :HEAD] += dgain
    for b in range(cb):
        dpre[b * C:(b + 1) * C, 3 * width:] = dlog[b].astype(BF)
    for i in range(3):
        dc = jnp.concatenate([jnp.concatenate(dcs[i][b], axis=1) for b in range(cb)], axis=0)
        pre = pre_ref[:, i * width:(i + 1) * width]
        tot = dc * taps_ref[i, 0:1, :]
        grads = [jnp.sum(dc * pre, axis=0, keepdims=True)]
        for j in range(1, taps):
            e = dc * cols_ref[:, j - 1:j]
            ext = jnp.concatenate([e, head_rows[j - 1, :, i * width:(i + 1) * width]], axis=0)
            head_rows[j - 1, :, i * width:(i + 1) * width] = e[:8]
            e = lax.slice_in_dim(ext, j, j + rows, axis=0)
            tot = tot + e * taps_ref[i, j:j + 1, :]
            grads.append(jnp.sum(e * pre, axis=0, keepdims=True))
        dpre[:, i * width:(i + 1) * width] = tot.astype(BF)
        small_ref[taps * i:taps * (i + 1), :width] += jnp.concatenate(grads, axis=0)
    low = dpre[...]
    acc[:, :3 * width] += lax.dot_general(na_ref[...], low[:, :3 * width], TN, preferred_element_type=F32)
    acc[:, 4 * width:] += lax.dot_general(na_ref[...], low[:, 3 * width:], TN, preferred_element_type=F32)
    dna = lax.dot_general(low, wide_ref[...], NT, preferred_element_type=F32)
    x = x_ref[...].astype(F32)
    gains_ref[0:1, :] += jnp.sum(dna * (x * lax.rsqrt(jnp.mean(x * x, axis=-1, keepdims=True) + 1e-6)), axis=0, keepdims=True)

    @pl.when(back % 2 == core)
    def _():
        kna_ref[back // 2] = dna

    @pl.when(back % 2 != core)
    def _():
        sna_ref[back // 2] = dna.astype(BF)

    @pl.when(step == steps - 1)
    def _():
        small_ref[3 * taps:3 * taps + heads, :] = acc[:, 4 * width:].T[:heads, :]
        me = lax.axis_index("fsdp")
        first, second = stage_bits(n_f)
        half = 2 * width
        for ref, other, bit, lanes in ((away1_ref, keep1_ref, first[0], slice(0, half)), (away2_ref, keep2_ref, second[0], slice(half, 2 * half))):
            mine = (me // bit) % 2
            for j in range(n_f // 2):
                low_bits = j % bit
                there = (j - low_bits) * 2 + low_bits
                ref[j] = acc[pl.ds(pl.multiple_of((there + (1 - mine) * bit) * shard, 16), shard), lanes].astype(BF)
                other[j] = acc[pl.ds(pl.multiple_of((there + mine * bit) * shard, 16), shard), lanes].astype(other.dtype)


def whole(shape):
    return pl.BlockSpec(shape, lambda i, *_: (0,) * len(shape), pipeline_mode=pl.Buffered(1))


def shaped(shape, dtype=F32):
    return jax.ShapeDtypeStruct(shape, dtype)


def params(limit=60):
    return pltpu.CompilerParams(dimension_semantics=("arbitrary",), vmem_limit_bytes=limit * 2**20)


COST = pl.CostEstimate(flops=10**10, bytes_accessed=10**7, transcendentals=0)
TINY = pl.CostEstimate(flops=1, bytes_accessed=1, transcendentals=0)


def fwd_call_kernel(heads, cb, base, n_old, *refs):
    ins, rest = refs[:10], refs[10 + n_old:]
    outs, tail_out, state_out, tail, state, line = rest[:14], rest[14], rest[15], rest[16], rest[17], rest[18]
    fwd_kernel(heads, cb, base, *ins, *outs, tail, state, line)

    @pl.when(pl.program_id(0) == pl.num_programs(0) - 1)
    def _():
        tail_out[...] = tail[...]
        state_out[...] = state[...]


def mixer_fwd(part, parts, x, wide, again, cols, segr, seg, taps, gain, tail, state, old, cb=4):
    n, d = x.shape
    width = taps.shape[2]
    heads = width // HEAD
    wide_cols = 3 * width + HEAD
    rows = cb * C
    steps = n // parts // rows
    base = part * steps
    sq = shaped((n // C, heads, C, HEAD))
    sqspec = pl.BlockSpec((cb, heads, C, HEAD), lambda i, s: (i + base, 0, 0, 0))
    here = lambda w: pl.BlockSpec((rows, w), lambda i, s: (i + base, 0))
    ins = [x, wide, again, cols, segr, taps, gain, tail, state]
    kept = [shaped((n, width), BF), shaped((n, d), BF), shaped((n, wide_cols)), shaped((n, 3 * width)), shaped((n, width))] + [sq] * 8
    return pl.pallas_call(
        functools.partial(fwd_call_kernel, heads, cb, base, len(old)),
        grid_spec=pltpu.PrefetchScalarGridSpec(
            num_scalar_prefetch=1, grid=(steps,),
            in_specs=[here(d), whole((d, wide_cols)), whole((1, d)), here(cols.shape[1]),
                      pl.BlockSpec((1, rows), lambda i, s: (0, i + base)),
                      whole(taps.shape), whole((1, HEAD)), whole(tail.shape), whole(state.shape)]
            + [pl.BlockSpec(memory_space=pl.ANY)] * len(old),
            out_specs=[pl.BlockSpec((rows, width), lambda i, s: (i, 0)), here(width), here(d), here(wide_cols), here(3 * width), here(width)]
            + [sqspec] * 8 + [whole(tail.shape), whole(state.shape)],
            scratch_shapes=[pltpu.VMEM(tail.shape, F32), pltpu.VMEM(state.shape, F32), pltpu.VMEM((rows + 8, 3 * width), F32)]),
        out_shape=[shaped((n // parts, width), BF)] + kept + [shaped(tail.shape), shaped(state.shape)],
        input_output_aliases={1 + len(ins) + i: 1 + i for i in range(len(old))},
        compiler_params=params(),
        cost_estimate=COST,
        name="mixer_fwd",
    )(seg, *ins, *old)


def mixer_bwd(n_f, shard, ga, out, wide, x, dffn, cols, segr, seg, taps, gain, kept, cb=2):
    mix, na, pre, conv, o, *rest = kept
    n, wide_cols = pre.shape
    d = x.shape[1]
    width = taps.shape[2]
    heads = width // HEAD
    rows = cb * C
    steps = n // rows
    ntap = taps.shape[1]
    sqspec = pl.BlockSpec((cb, heads, C, HEAD), lambda i, s: (steps - 1 - i, 0, 0, 0))
    row = lambda w: pl.BlockSpec((rows, w), lambda i, s: (steps - 1 - i, 0))
    outs = [shaped((n_f // 2, shard, 2 * width), BF)] * 4 + [
            shaped((2, rows, d), BF), shaped((2, rows, d)), shaped((8, d)), shaped((16, d))]
    return pl.pallas_call(
        functools.partial(bwd_kernel, heads, cb, n_f, shard),
        grid_spec=pltpu.PrefetchScalarGridSpec(
            num_scalar_prefetch=1, grid=(steps,),
            in_specs=[whole((rows, d))] * 4 + [row(width), row(d), whole(out.shape), whole((d, wide_cols)), row(d), whole((1, d)), whole((1, d)),
                      row(wide_cols), row(3 * width), row(width),
                      row(cols.shape[1]), pl.BlockSpec((1, rows), lambda i, s: (0, steps - 1 - i)),
                      whole(taps.shape), whole((1, HEAD))] + [sqspec] * 8,
            out_specs=[whole(v.shape) for v in outs],
            scratch_shapes=[pltpu.VMEM((ntap - 1, 8, 3 * width), F32), pltpu.VMEM((heads, HEAD, HEAD), F32),
                            pltpu.VMEM((d, 4 * width + HEAD), F32), pltpu.VMEM((rows, wide_cols), BF)]),
        out_shape=outs,
        compiler_params=params(),
        cost_estimate=COST,
        name="mixer_bwd",
    )(seg, *ga, mix, na, out, wide, x, *dffn, pre, conv, o, cols, segr, taps, gain, *rest)


def fold_kernel(n_f, stage, k1_ref, g1_ref, k2_ref, g2_ref, a1_out, k1_out, a2_out, k2_out):
    me = lax.axis_index("fsdp")
    for order, keep, got, away_out, keep_out in ((0, k1_ref, g1_ref, a1_out, k1_out), (1, k2_ref, g2_ref, a2_out, k2_out)):
        bits = stage_bits(n_f)[order]
        bit = bits[stage]
        left = sorted(b for b in bits[stage:])
        place = 1 << left.index(bit)
        mine = (me // bit) % 2
        for j in range(keep.shape[0] // 2):
            low = j % place
            there = (j - low) * 2 + low
            theirs = there + (1 - mine) * place
            away_out[j] = (keep[theirs].astype(F32) + got[theirs].astype(F32)).astype(BF)
            ours = there + mine * place
            keep_out[j] = (keep[ours].astype(F32) + got[ours].astype(F32)).astype(keep_out.dtype)


def fold(n_f, stage, k1, g1, k2, g2):
    m, shard, w = k1.shape
    outs = [shaped((m // 2, shard, w), BF)] * 4
    return pl.pallas_call(
        functools.partial(fold_kernel, n_f, stage),
        out_shape=outs,
        compiler_params=pltpu.CompilerParams(vmem_limit_bytes=60 * 2**20),
        cost_estimate=TINY,
        name="fold",
    )(k1, g1, k2, g2)


def finish_kernel(heads, ntap, k1_ref, g1_ref, k2_ref, g2_ref, s_ref, *refs):
    got, (qkv_ref, out_ref, taps_ref, beta_ref, attn_ref, ffn_ref, head_ref, hold) = refs[:-8], refs[-8:]
    width = qkv_ref.shape[2]
    shard = qkv_ref.shape[1]
    a = k1_ref[0].astype(F32) + g1_ref[0].astype(F32)
    b = k2_ref[0].astype(F32) + g2_ref[0].astype(F32)
    qkv_ref[0] = a[:, :width]
    qkv_ref[1] = a[:, width:]
    qkv_ref[2] = b[:, :width]
    out_ref[...] = b[:, width:].T
    small = s_ref[...]
    for g in got:
        small = small + g[...]
    for i in range(3):
        taps_ref[i] = small[ntap * i:ntap * (i + 1), :width]
    attn_ref[...] = small[16:17]
    ffn_ref[...] = small[17:18]
    head_ref[...] = small[18:19, :HEAD]
    if shard == 128:
        hold[...] = small[8:16]
        me = lax.axis_index("fsdp")
        beta_ref[...] = hold[3 * ntap - 8:3 * ntap - 8 + heads, pl.ds(pl.multiple_of(me * shard, 128), shard)]
    else:
        beta_ref[...] = small[3 * ntap:3 * ntap + heads]


def finish(heads, ntap, k1, g1, k2, g2, small, got):
    m, shard, w = k1.shape
    d = small.shape[1]
    return pl.pallas_call(
        functools.partial(finish_kernel, heads, ntap),
        out_shape=[shaped((3, shard, w // 2)), shaped((w // 2, shard)), shaped((3, ntap, w // 2)),
                   shaped((heads, 128 if shard == 128 else d)), shaped((1, d)), shaped((1, d)), shaped((1, HEAD))],
        scratch_shapes=[pltpu.VMEM((8, d), F32)],
        compiler_params=pltpu.CompilerParams(vmem_limit_bytes=60 * 2**20),
        cost_estimate=TINY,
        name="finish",
    )(k1, g1, k2, g2, small, *got)


def ffn_kernel(ff, *refs):
    m, out, (x_ref, w_ref, gf_ref, gain_ref), rest = refs[:4], refs[4:8], refs[8:12], refs[12:]
    mid_ref, nf_ref, hid_ref, dgu_ref, keep_ref, send_ref, dgain_ref, hold = rest
    rows = keep_ref.shape[0]
    core = lax.axis_index("tensor") % 2
    mid = x_ref[...].astype(F32)
    for k in range(4):
        mid = mid + lax.dot_general(m[k][...], out[k][...], NT, preferred_element_type=F32)
    hold[...] = mid
    unit = mid * lax.rsqrt(jnp.mean(mid * mid, axis=-1, keepdims=True) + 1e-6)
    nf = (unit * gain_ref[0:1, :]).astype(BF)
    nf_ref[...] = nf
    mid_ref[...] = hold[pl.ds(pl.multiple_of(core * rows, 16), rows), :]
    gate = lax.dot_general(w_ref[:ff, :], nf, NT, preferred_element_type=F32)
    up = lax.dot_general(w_ref[ff:2 * ff, :], nf, NT, preferred_element_type=F32)
    dh = lax.dot_general(w_ref[2 * ff:, :], gf_ref[...], NT, preferred_element_type=F32)
    sig = sigmoid(gate)
    act = gate * sig
    hid_ref[...] = (act * up).astype(BF)
    dgu_ref[:ff, :] = (dh * up * sig * (1.0 + gate * (1.0 - sig))).astype(BF)
    dgu_ref[ff:, :] = (dh * act).astype(BF)
    dnf = lax.dot_general(dgu_ref[...], w_ref[:2 * ff, :], TN, preferred_element_type=F32)
    dgain_ref[...] = jnp.sum(dnf * unit, axis=0, keepdims=True)
    hold[...] = dnf
    keep_ref[...] = hold[pl.ds(pl.multiple_of(core * rows, 16), rows), :]
    send_ref[...] = hold[pl.ds(pl.multiple_of((1 - core) * rows, 16), rows), :].astype(BF)


def ffn(part, m, out, x, weights, gf, gain):
    n, width = m[0].shape
    d = x.shape[1]
    ff = weights.shape[0] // 3
    here = pl.BlockSpec((n, d), lambda i: (part, 0))
    outs = [shaped((n // 2, d)), shaped((n, d), BF), shaped((ff, n), BF), shaped((2 * ff, n), BF),
            shaped((n // 2, d)), shaped((n // 2, d), BF), shaped((1, d))]
    return pl.pallas_call(
        functools.partial(ffn_kernel, ff),
        grid=(1,),
        in_specs=[whole(v.shape) for v in (*m, *out)] + [here, whole(weights.shape), here, whole((1, d))],
        out_specs=[whole(v.shape) for v in outs],
        out_shape=outs,
        scratch_shapes=[pltpu.VMEM((n, d), F32)],
        compiler_params=params(),
        cost_estimate=COST,
        name="ffn",
    )(*m, *out, x, weights, gf, gain)


def grad_kernel(part, low_ref, other_ref, mid_ref, cot_ref, coty_ref, gain_ref, grad_ref, low_out):
    chip = lax.axis_index("tensor") // 2
    mid = mid_ref[...]
    factor = lax.rsqrt(jnp.mean(mid * mid, axis=-1, keepdims=True) + 1e-6)
    u = (low_ref[...].astype(F32) + other_ref[...].astype(F32)) * gain_ref[0:1, :]
    cot = jnp.where(chip == part, cot_ref[...], coty_ref[...]).astype(F32)
    grad = cot + factor * u - mid * (factor * factor * factor) * jnp.mean(u * mid, axis=-1, keepdims=True)
    grad_ref[...] = grad
    low_out[...] = grad.astype(BF)


def grad_rows(part, low, other, mid, cot, cot_y, gain):
    return pl.pallas_call(
        functools.partial(grad_kernel, part),
        out_shape=[shaped(mid.shape), shaped(mid.shape, BF)],
        compiler_params=pltpu.CompilerParams(vmem_limit_bytes=24 * 2**20),
        cost_estimate=TINY,
        name="grad_rows",
    )(low, other, mid, cot, cot_y, gain)


def down_kernel(hid0_ref, hid1_ref, w_ref, send_ref, keep_ref, hold):
    core = lax.axis_index("tensor") % 2
    rows = send_ref.shape[1]
    for i, hid in enumerate((hid0_ref, hid1_ref)):
        hold[...] = lax.dot_general(hid[...], w_ref[...], TN, preferred_element_type=F32)
        keep_ref[i] = hold[pl.ds(pl.multiple_of(core * rows, 16), rows), :]
        send_ref[i] = hold[pl.ds(pl.multiple_of((1 - core) * rows, 16), rows), :].astype(BF)


def down(hid0, hid1, weights, wait_for):
    ff, n = hid0.shape
    d = weights.shape[1]
    outs = [shaped((2, n // 2, d), BF), shaped((2, n // 2, d))]

    def body(*refs):
        down_kernel(*refs[:3], *refs[3 + len(wait_for):])

    return pl.pallas_call(
        body,
        grid=(1,),
        in_specs=[whole(hid0.shape)] * 2 + [pl.BlockSpec((ff, d), lambda i: (2, 0))] + [pl.BlockSpec(memory_space=pl.ANY)] * len(wait_for),
        out_specs=[whole(v.shape) for v in outs],
        out_shape=outs,
        scratch_shapes=[pltpu.VMEM((n, d), F32)],
        compiler_params=params(),
        cost_estimate=TINY,
        name="down",
    )(hid0, hid1, weights, *wait_for)


def ffn_grads_kernel(ff, parts, *refs):
    gf_ref, o_ref = refs[3 * parts], refs[-1]
    n = refs[0].shape[1]
    up = down = None
    for i in range(parts):
        dgu, hid, nf = refs[3 * i:3 * i + 3]
        a = jnp.dot(dgu[...], nf[...], preferred_element_type=F32)
        b = jnp.dot(hid[...], gf_ref[i * n:(i + 1) * n, :], preferred_element_type=F32)
        up = a if up is None else up + a
        down = b if down is None else down + b
    for k in range(o_ref.shape[0]):
        lanes = slice(k * 128, (k + 1) * 128)
        o_ref[k, :2 * ff, :] = up[:, lanes].astype(BF)
        o_ref[k, 2 * ff:, :] = down[:, lanes].astype(BF)


def ffn_grads(pieces, gf, wait_for, step=256):
    ff = pieces[0][1].shape[0]
    n, d = gf.shape
    flat, specs = [], []
    for dgu, hid, nf in pieces:
        flat += [dgu, hid, nf]
        specs += [whole(dgu.shape), whole(hid.shape), pl.BlockSpec((nf.shape[0], step), lambda i: (0, i))]
    return pl.pallas_call(
        functools.partial(ffn_grads_kernel, ff, len(pieces)),
        grid=(d // step,),
        in_specs=specs + [pl.BlockSpec((n, step), lambda i: (0, i))] + [pl.BlockSpec(memory_space=pl.ANY)] * len(wait_for),
        out_specs=pl.BlockSpec((step // 128, 3 * ff, 128), lambda i: (i, 0, 0)),
        out_shape=shaped((d // 128, 3 * ff, 128), BF),
        compiler_params=params(),
        cost_estimate=pl.CostEstimate(flops=5 * 10**9, bytes_accessed=10**7, transcendentals=0),
        name="ffn_grads",
    )(*flat, gf, *wait_for)


def to_chips_kernel(keep, got, wait_for, mine_ref, away_ref):
    chip = lax.axis_index("tensor") // 2
    mine_ref[...] = keep[chip] + got[chip].astype(F32)
    away_ref[...] = (keep[1 - chip] + got[1 - chip].astype(F32)).astype(BF)


def to_chips(keep, got, wait_for):
    spec = pl.BlockSpec(memory_space=pltpu.VMEM)
    return pl.pallas_call(
        to_chips_kernel,
        in_specs=[spec] * 2 + [pl.BlockSpec(memory_space=pl.ANY)],
        out_shape=[shaped(keep.shape[1:]), shaped(keep.shape[1:], BF)],
        compiler_params=pltpu.CompilerParams(vmem_limit_bytes=60 * 2**20),
        cost_estimate=TINY,
        name="to_chips",
    )(keep, got, wait_for)


def last_kernel(g0, g1, na, na_y, x_ref, gain_ref, mid0, mid1, out, out_y, in_ref, block_ref):
    first = lax.axis_index("tensor") // 2 == 0
    x = x_ref[...].astype(F32)
    factor = lax.rsqrt(jnp.mean(x * x, axis=-1, keepdims=True) + 1e-6)
    u = (na[...] + na_y[...].astype(F32)) * gain_ref[0:1, :]
    in_ref[...] = jnp.where(first, g0[...], g1[...]) + (factor * u - x * (factor * factor * factor) * jnp.mean(u * x, axis=-1, keepdims=True))
    block_ref[...] = (jnp.where(first, mid0[...], mid1[...]) + out[...] + out_y[...].astype(F32)).astype(BF)


def last_rows(g0, g1, na, na_y, x, gain, mid0, mid1, out, out_y):
    return pl.pallas_call(
        last_kernel,
        out_shape=[shaped(g0.shape), shaped(g0.shape, BF)],
        compiler_params=pltpu.CompilerParams(vmem_limit_bytes=60 * 2**20),
        cost_estimate=TINY,
        name="last_rows",
    )(g0, g1, na, na_y, x, gain, mid0, mid1, out, out_y)


def ffn_cast_kernel(d_ref, expand_ref, down_ref):
    ff = down_ref.shape[0]
    expand_ref[0] = d_ref[:ff, :].astype(F32)
    expand_ref[1] = d_ref[ff:2 * ff, :].astype(F32)
    down_ref[...] = d_ref[2 * ff:, :].astype(F32)


def ffn_cast(d):
    ff, w = d.shape[0] // 3, d.shape[1]
    return pl.pallas_call(
        ffn_cast_kernel,
        out_shape=[shaped((2, ff, w)), shaped((ff, w))],
        compiler_params=pltpu.CompilerParams(vmem_limit_bytes=60 * 2**20),
        cost_estimate=TINY,
        name="ffn_cast",
    )(d)


def pack_kernel(qkv_ref, beta_ref, out_ref, o_ref):
    width = qkv_ref.shape[2]
    n = o_ref.shape[0]
    for i in range(3):
        o_ref[:, i * width:(i + 1) * width] = qkv_ref[i]
    beta = beta_ref[...].astype(F32)
    heads = beta.shape[1]
    o_ref[:, 3 * width:3 * width + 128] = jnp.concatenate([beta, jnp.zeros((n, 128 - heads), F32)], axis=1).astype(BF)
    o_ref[:, 3 * width + 128:] = out_ref[...].astype(F32).T.astype(BF)


def pack(qkv, beta, out):
    n, width = qkv.shape[1:]
    return pl.pallas_call(
        pack_kernel,
        out_shape=shaped((n, 4 * width + 128), BF),
        compiler_params=pltpu.CompilerParams(vmem_limit_bytes=60 * 2**20),
        name="pack",
    )(qkv, beta, out)


def columns(seg, pad):
    n = seg.shape[0]
    cols = []
    for j in range(1, 4):
        before = jnp.concatenate([jnp.full((j,), -1, seg.dtype), seg[:n - j]])
        cols.append((before == seg).astype(F32))
    cols += [pad.astype(F32), seg.astype(F32)]
    cols += [jnp.zeros((n,), F32)] * 3
    return jnp.stack(cols, axis=1)


def hop(value, axis, bit):
    n = lax.axis_size(axis)
    return lax.ppermute(value, axis, [(i, i ^ bit) for i in range(n)])


def fence(*values):
    return lax.optimization_barrier(values)


def y_hop(value):
    return hop(value, "tensor", 2)


def core_hop(value):
    return hop(value, "tensor", 1)


def in_order(own, other_chip, pair):
    me = lax.axis_index("tensor")
    full = jnp.zeros((4,) + own.shape, own.dtype)
    for k, block in ((0, own), (2, other_chip), (1, pair[0]), (3, pair[1])):
        full = lax.dynamic_update_slice(full, block[None], (me ^ k,) + (0,) * own.ndim)
    return full.reshape((4 * own.shape[0],) + own.shape[1:])


class Ring:
    def __init__(self, value):
        n = lax.axis_size("fsdp")
        order = [i for i in range(0, n, 2)] + [i for i in reversed(range(1, n, 2))]
        me = lax.axis_index("fsdp")
        self.n = n
        self.me = jnp.where(me % 2 == 0, me // 2, n - 1 - me // 2)
        self.right = [(order[i], order[(i + 1) % n]) for i in range(n)]
        self.left = [(b, a) for a, b in self.right]
        self.rows = value.shape[0]
        self.full = jnp.zeros((n * self.rows,) + value.shape[1:], value.dtype)
        self.a = self.b = value
        self.k = 0
        self.put(value, 0, 0)

    def put(self, part, steps, start):
        place = lax.rem(self.me + steps + self.n, self.n)
        owner = jnp.where(place < self.n // 2, 2 * place, 2 * (self.n - 1 - place) + 1)
        self.full = lax.dynamic_update_slice(self.full, part, (owner * self.rows + start, 0))

    def step(self):
        self.k += 1
        k, half = self.k, self.rows // 2
        self.split = 2 * k == self.n and half % 16 == 0
        if self.split:
            self.a = lax.ppermute(self.a[:half], "fsdp", self.right)
            self.b = lax.ppermute(self.b[half:], "fsdp", self.left)
            return
        self.a = lax.ppermute(self.a, "fsdp", self.right)
        if 2 * k < self.n:
            self.b = lax.ppermute(self.b, "fsdp", self.left)

    def keep(self):
        self.put(self.a, -self.k, 0)
        if self.split or 2 * self.k < self.n:
            self.put(self.b, self.k, self.rows // 2 if self.split else 0)


def hop_sum(value, axis, bit):
    return value + hop(value, axis, bit)


def on_device(
    layer_input, segment_ids, pad_mask, attn_gain, ffn_gain, out_gain,
    qkv_weight, beta_weight, conv_weight, out_weight, expand_weight, down_weight, cotangent,
):
    n_f = lax.axis_size("fsdp")
    me_t = lax.axis_index("tensor")
    chip = me_t // 2
    rows, d_model = layer_input.shape
    width = qkv_weight.shape[3]
    heads = beta_weight.shape[2]
    ff = down_weight.shape[1]
    shard = qkv_weight.shape[2]
    taps = conv_weight[0]
    ntap = taps.shape[1]
    first_bits, second_bits = stage_bits(n_f)

    packed = pack(qkv_weight[0], beta_weight[0], out_weight[0])
    packed, expand_own, down_own = fence(packed, expand_weight[0], down_weight[0])
    ring = Ring(packed)
    ring.step()
    x_y = y_hop(layer_input)
    x_c = core_hop(layer_input)
    ffn_own = jnp.concatenate([expand_own[0].T, expand_own[1].T, down_own], axis=0)
    weights = lax.all_gather(ffn_own, "fsdp", axis=1, tiled=True)
    seg = segment_ids[0]
    cols = columns(seg, pad_mask[0])
    segr = seg.astype(F32)[None]
    ring.a, ring.b, x_y, x_c = fence(ring.a, ring.b, x_y, x_c)
    ring.keep()
    ring.step()
    x_cy = core_hop(x_y)
    c_y = y_hop(cotangent)
    c_c = core_hop(cotangent)
    ring.a, ring.b, x_cy = fence(ring.a, ring.b, x_cy)
    ring.keep()
    ring.step()
    x_full = in_order(layer_input, x_y, (x_c, x_cy))
    ring.a, ring.b, x_full, cols, c_y = fence(ring.a, ring.b, x_full, cols, c_y)
    ring.keep()
    while 2 * ring.k < n_f:
        ring.step()
        ring.keep()
    c_cy = core_hop(c_y)
    g_f = in_order(cotangent, c_y, (c_c, c_cy))
    wide, g_f = fence(ring.full, g_f)

    out_own = wide[:, 3 * width + HEAD:]
    tail = jnp.zeros((8, 3 * width), F32)
    state = jnp.zeros((heads, HEAD, HEAD), F32)

    def mix(i, tail, state, old):
        m, *kept, tail, state = mixer_fwd(i, 2, x_full, wide, attn_gain, cols, segr, seg, taps, out_gain, tail, state, old)
        return m, kept, tail, state

    ow_y = y_hop(out_own)
    ow_c = core_hop(out_own)
    m0, kept, tail, state = mix(0, tail, state, [])
    ow_y, ow_c, m0, tail, state = fence(ow_y, ow_c, m0, tail, state)
    m0_y = y_hop(m0)
    m0_c = core_hop(m0)
    ow_cy = core_hop(ow_y)
    m1, kept, tail, state = mix(1, tail, state, kept)
    m0_y, m0_c, ow_cy, m1 = fence(m0_y, m0_c, ow_cy, m1)

    def feed(i, *m):
        return ffn(i, m, (out_own, ow_y, ow_c, ow_cy), x_full, weights, g_f, ffn_gain)

    m1_y = y_hop(m1)
    m1_c = core_hop(m1)
    m0_cy = core_hop(m0_y)
    mid0, nf0, hid0, dgu0, keep0, send0, dgain0 = feed(0, m0, m0_y, m0_c, m0_cy)
    m1_y, m1_c, send0 = fence(m1_y, m1_c, send0)
    m1_cy = core_hop(m1_y)
    low0 = (keep0 + core_hop(send0).astype(F32)).astype(BF)
    m1_cy, low0 = fence(m1_cy, low0)
    low0_y = y_hop(low0)
    mid1, nf1, hid1, dgu1, keep1, send1, dgain1 = feed(1, m1, m1_y, m1_c, m1_cy)
    low0_y, send1 = fence(low0_y, send1)
    low1 = (keep1 + core_hop(send1).astype(F32)).astype(BF)
    grad0, ga0 = grad_rows(0, low0, low0_y, mid0, cotangent, c_y, ffn_gain)
    low1, ga0 = fence(low1, ga0)
    low1_y = y_hop(low1)
    ga0_c = core_hop(ga0)
    blocks = ffn_grads([(dgu0, hid0, nf0), (dgu1, hid1, nf1)], g_f, [low1])
    q = d_model // 128
    if q != n_f:
        blocks = blocks.reshape(q, 3 * ff, n_f // q, shard).transpose(0, 2, 1, 3).reshape(n_f, 3 * ff, shard)
    send_out, keep_out = down(hid0, hid1, weights, [blocks])
    low1_y, ga0_c, send_out, done_blocks = fence(low1_y, ga0_c, send_out, blocks)
    d_ffn = lax.psum_scatter(blocks, "fsdp", scatter_dimension=0, tiled=False)
    grad1, ga1 = grad_rows(1, low1, low1_y, mid1, cotangent, c_y, ffn_gain)
    ga1_c = core_hop(ga1)
    ga1, ga1_c = fence(ga1, ga1_c)

    out_c = core_hop(send_out)
    made = mixer_bwd(
        n_f, shard, (ga0, ga0_c, ga1, ga1_c), out_own, wide, x_full, (dgain0, dgain1), cols, segr, seg, taps, out_gain, kept)
    away1, k1, away2, k2, send_na, keep_na, gains, small, out_c = fence(*made, out_c)

    g1 = hop(away1, "fsdp", first_bits[0])
    g2 = hop(away2, "fsdp", second_bits[0])
    na_c = core_hop(send_na)
    gains_got = [hop(gains, "tensor", k) for k in range(1, 4)]
    out, out_away = to_chips(keep_out, out_c, done_blocks)
    na, na_away = to_chips(keep_na, na_c, gains)
    g1, g2, na_away, out_away, *gains_got = fence(g1, g2, na_away, out_away, *gains_got)
    count = len(first_bits)
    small = jnp.concatenate([small, gains + gains_got[0] + (gains_got[1] + gains_got[2])], axis=0)
    for stage in range(1, count):
        away1, k1, away2, k2 = fold(n_f, stage, k1, g1, k2, g2)
        if stage == 1:
            na_y, out_y = y_hop(na_away), y_hop(out_away)
        g1 = hop(away1, "fsdp", first_bits[stage])
        g2 = hop(away2, "fsdp", second_bits[stage])
        if stage < count - 1:
            small = hop_sum(small, "fsdp", first_bits[stage - 1])
            g1, g2, small, na_y = fence(g1, g2, small, na_y)
    if n_f == 8:
        got = [hop(small, "fsdp", k) for k in (2, 4, 6)]
    else:
        small = hop_sum(small, "fsdp", first_bits[count - 2])
        got = [hop(small, "fsdp", first_bits[count - 1])]
    input_grad, block_outs = last_rows(grad0, grad1, na, na_y, layer_input, attn_gain, mid0, mid1, out, out_y)
    block_outs = block_outs[None]
    qkv_grad, out_grad, conv_grad, beta_grad, attn_total, ffn_total, head_total = finish(heads, ntap, k1, g1, k2, g2, small, got)
    if shard != 128:
        beta_grad = lax.dynamic_slice(beta_grad, (0, lax.axis_index("fsdp") * shard), (heads, shard))
    beta_grad = beta_grad.T
    expand_grad, down_grad = ffn_cast(d_ffn)
    expand_grad = expand_grad.transpose(0, 2, 1)
    return (
        block_outs, input_grad, attn_total, ffn_total, head_total, qkv_grad[None], beta_grad[None],
        conv_grad[None], out_grad[None], expand_grad[None], down_grad[None],
    )


def solution(mesh):
    in_specs = (
        P(("fsdp", "tensor"), None),
        P("fsdp", None),
        P("fsdp", None),
        P(),
        P(),
        P(),
        P(None, None, "fsdp", "tensor"),
        P(None, "fsdp", "tensor"),
        P(None, None, None, "tensor"),
        P(None, "tensor", "fsdp"),
        P(None, None, "fsdp", "tensor"),
        P(None, "tensor", "fsdp"),
        P(("fsdp", "tensor"), None),
    )
    out_specs = (
        P(None, ("fsdp", "tensor"), None),
        P(("fsdp", "tensor"), None),
        P(),
        P(),
        P(),
        P(None, None, "fsdp", "tensor"),
        P(None, "fsdp", "tensor"),
        P(None, None, None, "tensor"),
        P(None, "tensor", "fsdp"),
        P(None, None, "fsdp", "tensor"),
        P(None, "tensor", "fsdp"),
    )
    return jax.shard_map(
        on_device, mesh=mesh, in_specs=in_specs, out_specs=out_specs, check_vma=False
    )
```

```python
import functools
import jax
import jax.numpy as jnp
from jax import lax
from jax.experimental import pallas as pl
from jax.experimental.pallas import tpu as pltpu
from jax.sharding import PartitionSpec as P

HEAD = 128
C = 128
F32 = jnp.float32
BF = jnp.bfloat16

NN = (((1,), (0,)), ((), ()))
NT = (((1,), (1,)), ((), ()))
TN = (((0,), (0,)), ((), ()))


def dot1(a, b, dims=NN):
    return lax.dot_general(a.astype(BF), b.astype(BF), dims, preferred_element_type=F32)


def split(x):
    hi = x.astype(BF)
    return hi, (x - hi.astype(F32)).astype(BF)


def dot3(a, b, dims=NN):
    a1, a2 = split(a) if not isinstance(a, tuple) else a
    b1, b2 = split(b) if not isinstance(b, tuple) else b
    ka, kb = dims[0][0][0], dims[0][1][0]
    left = jnp.concatenate([a1, a2], axis=ka)
    n = b1.shape[1 - kb]
    if n == 128:
        right = jnp.concatenate([jnp.concatenate([b1, b2], axis=1 - kb), jnp.concatenate([b1, jnp.zeros_like(b1)], axis=1 - kb)], axis=kb)
        r = lax.dot_general(left, right, dims, preferred_element_type=F32)
        return r[:, :128] + r[:, 128:]
    r = lax.dot_general(left, jnp.concatenate([b1, b1], axis=kb), dims, preferred_element_type=F32)
    return r + lax.dot_general(a1, b2, dims, preferred_element_type=F32)


def dot3_old(a, b, dims=NN):
    a1, a2 = split(a) if not isinstance(a, tuple) else a
    b1, b2 = split(b) if not isinstance(b, tuple) else b
    d = functools.partial(lax.dot_general, dimension_numbers=dims, preferred_element_type=F32)
    return d(a1, b1) + (d(a1, b2) + d(a2, b1))


def block_masks():
    r = lax.broadcasted_iota(jnp.int32, (C, C), 0)
    c = lax.broadcasted_iota(jnp.int32, (C, C), 1)
    return r, c


def invert(systems, dot):
    r, c = block_masks()
    eye = (r == c).astype(F32)
    x = r ^ c
    lows = [low.astype(BF) for low in systems]
    out = [eye - jnp.where((x == 1), low, 0.0) for low in systems]
    size = 2
    while size < C:
        here = (x >= size) & (x < 2 * size)
        short = [t.astype(BF) for t in out]
        mids = [dot1(jnp.where(here, low, 0.0).astype(BF), t) for low, t in zip(lows, short)]
        out = [t - dot1(b, m) for t, b, m in zip(out, short, mids)]
        size *= 2
    splits = [split(t) for t in out]
    errors = [eye - t - dot(low, p) for low, t, p in zip(systems, out, splits)]
    return [t + dot1(p[0], e) for t, p, e in zip(out, splits, errors)]


def sigmoid(x):
    return 1.0 / (1.0 + jnp.exp(-x))


def taps_down(ext, rows, j):
    return lax.slice_in_dim(ext, 8 - j, 8 - j + rows, axis=0)


def row_sum(x):
    return jnp.dot(x.astype(BF), jnp.ones((HEAD, HEAD), BF), preferred_element_type=F32)


def head_norm(x):
    return x * lax.rsqrt(row_sum(x * x) + 1e-6)


def segment_parts(seg_s, cols_ref, segr_ref, first, sl):
    prev = jnp.where(first > 0, seg_s[jnp.maximum(first - 1, 0)], -1)
    last = seg_s[first + C - 1]
    segc = cols_ref[sl, 4:5]
    same = segc == segr_ref[0:1, sl]
    lead = (segc == prev.astype(F32)).astype(F32)
    trail = (segc == last.astype(F32)).astype(F32)
    return same, lead, trail, (prev == last).astype(F32)


def fwd_kernel(heads, cb, base, seg_s, x_ref, wide_ref, again_ref, cols_ref, segr_ref, taps_ref, gain_ref, tail_in, state_in,
               mixed_ref, kept_ref, na_ref, pre_ref, conv_ref, o_ref, t_ref, a_ref, p_ref, n_ref, z_ref, s_ref, u_ref, g_ref,
               tail, state, line):
    step = pl.program_id(0)
    width = heads * HEAD
    rows = cb * C
    taps = taps_ref.shape[1]

    @pl.when(step == 0)
    def _():
        tail[...] = jnp.zeros_like(tail) if tail_in is None else tail_in[...]
        state[...] = jnp.zeros_like(state) if state_in is None else state_in[...]

    r, c = block_masks()
    x = x_ref[...].astype(F32)
    na = (x * lax.rsqrt(jnp.mean(x * x, axis=-1, keepdims=True) + 1e-6) * again_ref[0:1, :]).astype(BF)
    na_ref[...] = na
    pre_ref[...] = jnp.dot(na, wide_ref[...], preferred_element_type=F32)
    tap = lambda j: jnp.concatenate([taps_ref[i, j:j + 1, :] for i in range(3)], axis=1)
    cur = pre_ref[:, :3 * width]
    line[:8, :] = tail[...]
    line[8:, :] = cur
    tot = cur * tap(0)
    for j in range(1, taps):
        tot = tot + line[8 - j:8 - j + rows, :] * tap(j) * cols_ref[:, j - 1:j]
    tail[...] = line[rows:, :]
    conv_ref[...] = tot
    tot = tot * sigmoid(tot)
    parts = [tot[:, i * width:(i + 1) * width] for i in range(3)]
    eye = (r == c).astype(F32)
    items = []
    for b in range(cb):
        sl = slice(b * C, (b + 1) * C)
        same, lead, trail, keep = segment_parts(seg_s, cols_ref, segr_ref, ((base + step) * cb + b) * C, sl)
        for h in range(heads):
            hs = slice(h * HEAD, (h + 1) * HEAD)
            q, k, v = (part[sl, hs] for part in parts)
            beta = sigmoid(pre_ref[sl, 3 * width + h:3 * width + h + 1]) * cols_ref[sl, 3:4]
            items.append(dict(b=b, h=h, q=head_norm(q), k=head_norm(k), v=v, beta=beta, same=same, lead=lead,
                              trail=trail, keep=keep, sl=sl, hs=hs))
    for it in items:
        it["kk"] = split(it["k"])
        p = jnp.where(it["same"] & (r > c), dot3(it["kk"], it["kk"], NT), 0.0)
        it["p"] = p
        it["low"] = p * it["beta"]
        it["a"] = jnp.where(it["same"] & (r >= c), dot3(it["q"], it["kk"], NT), 0.0)
    inv = invert([it["low"] for it in items], dot3)
    for it, t in zip(items, inv):
        rhs = jnp.concatenate([it["beta"] * it["v"], (it["beta"] * it["lead"]) * it["k"]], axis=1)
        tw = dot3(t, rhs)
        tws = split(tw)
        aw = dot3(it["a"], tws)
        bz = dot3(it["trail"] * it["k"], tws, TN)
        it["tv"], it["w"] = tw[:, :HEAD], tw[:, HEAD:]
        it["o0"], it["n"] = aw[:, :HEAD], it["lead"] * it["q"] - aw[:, HEAD:]
        it["bk"], it["z"] = bz[:, :HEAD], it["keep"] * eye - bz[:, HEAD:]
        it["t"] = t
    for it in items:
        b, h = it["b"], it["h"]
        s = state[h]
        ss = split(s)
        u = it["tv"] - dot3(it["w"], ss)
        o = it["o0"] + dot3(it["n"], ss)
        g = it["v"] - it["lead"] * dot3(it["kk"], ss)
        state[h] = it["bk"] + dot3(it["z"], ss)
        s_ref[b, h] = s
        u_ref[b, h] = u
        g_ref[b, h] = g
        t_ref[b, h] = it["t"]
        a_ref[b, h] = it["a"]
        p_ref[b, h] = it["p"]
        n_ref[b, h] = it["n"]
        z_ref[b, h] = it["z"]
        o_ref[it["sl"], it["hs"]] = o
        mixed = (o * lax.rsqrt(row_sum(o * o) * (1.0 / HEAD) + 1e-5) * gain_ref[0:1, :]).astype(BF)
        mixed_ref[it["sl"], it["hs"]] = mixed
        kept_ref[it["sl"], it["hs"]] = mixed


def stage_bits(n):
    bits = [1 << i for i in range(n.bit_length() - 1)]
    return bits, [bits[1], bits[0]] + bits[2:]


def bwd_kernel(heads, cb, n_f, shard, seg_s, ga0_ref, ga0c_ref, ga1_ref, ga1c_ref, mix_ref, na_ref, out_ref, wide_ref, x_ref, dffn0_ref, dffn1_ref,
               pre_ref, conv_ref, o_ref, cols_ref, segr_ref, taps_ref, gain_ref,
               t_ref, a_ref, p_ref, n_ref, z_ref, s_ref, u_ref, g_ref,
               away1_ref, keep1_ref, away2_ref, keep2_ref, sna_ref, kna_ref, gains_ref, small_ref,
               head_rows, dstate, acc, dpre):
    step = pl.program_id(0)
    steps = pl.num_programs(0)
    width = heads * HEAD
    rows = cb * C
    taps = taps_ref.shape[1]
    back = steps - 1 - step
    core = lax.axis_index("tensor") % 2

    @pl.when(step == 0)
    def _():
        head_rows[...] = jnp.zeros_like(head_rows)
        dstate[...] = jnp.zeros_like(dstate)
        acc[...] = jnp.zeros_like(acc)
        gains_ref[...] = jnp.zeros_like(gains_ref)
        gains_ref[6:7, :] = dffn0_ref[...] + dffn1_ref[...]
        small_ref[...] = jnp.zeros_like(small_ref)

    r, c = block_masks()
    dcs = [[[None] * heads for _ in range(cb)] for _ in range(3)]
    dgain = jnp.zeros((1, HEAD), F32)
    dlog = [None] * cb
    ga = jnp.where(back % 2 == core, jnp.where(back >= 2, ga1_ref[...], ga0_ref[...]),
                   jnp.where(back >= 2, ga1c_ref[...], ga0c_ref[...]))
    dmix = jnp.dot(ga, out_ref[...], preferred_element_type=F32)
    acc[:, 3 * width:4 * width] += lax.dot_general(ga, mix_ref[...], TN, preferred_element_type=F32)
    for b in reversed(range(cb)):
        sl = slice(b * C, (b + 1) * C)
        same, lead, trail, keep = segment_parts(seg_s, cols_ref, segr_ref, (back * cb + b) * C, sl)
        lane = lax.broadcasted_iota(jnp.int32, (C, HEAD), 1)
        dl = jnp.zeros((C, HEAD), F32)
        for h in range(heads):
            hs = slice(h * HEAD, (h + 1) * HEAD)
            cq, ck, cv = (conv_ref[sl, i * width + h * HEAD:i * width + (h + 1) * HEAD] for i in range(3))
            gq, gk, gv = sigmoid(cq), sigmoid(ck), sigmoid(cv)
            q, k = cq * gq, ck * gk
            rq = lax.rsqrt(jnp.sum(q * q, axis=-1, keepdims=True) + 1e-6)
            rk = lax.rsqrt(jnp.sum(k * k, axis=-1, keepdims=True) + 1e-6)
            q, k = q * rq, k * rk
            gb = sigmoid(pre_ref[sl, 3 * width + h:3 * width + h + 1])
            pad = cols_ref[sl, 3:4]
            beta = gb * pad
            o = o_ref[sl, hs]
            dm = dmix[sl, hs]
            ro = lax.rsqrt(jnp.mean(o * o, axis=-1, keepdims=True) + 1e-5)
            oh = o * ro
            dgain = dgain + jnp.sum(dm * oh, axis=0, keepdims=True)
            du0 = dm * gain_ref[0:1, :]
            do = ro * (du0 - oh * jnp.mean(du0 * oh, axis=-1, keepdims=True))
            ds1 = dstate[h]
            u = u_ref[b, h]
            s = s_ref[b, h]
            a = a_ref[b, h]
            p = p_ref[b, h]
            ks = split(k)
            ds1s = split(ds1)
            dos = split(do)
            us = split(u)
            dstate[h] = dot3(z_ref[b, h], ds1s, TN) + dot3(n_ref[b, h], dos, TN)
            du = dot3(a, dos, TN) + trail * dot3(ks, ds1s)
            dr = dot3(t_ref[b, h], du, TN)
            drs = split(dr)
            ss = split(s)
            dlow = jnp.where(same & (r > c), -dot3(drs, us, NT), 0.0)
            da = jnp.where(same & (r >= c), dot3(dos, us, NT), 0.0)
            dv = beta * dr
            dbeta = jnp.sum(dr * g_ref[b, h] , axis=-1, keepdims=True) + jnp.sum(dlow * p, axis=-1, keepdims=True)
            dp = split(beta * dlow)
            das = split(da)
            dq = lead * dot3(dos, ss, NT) + dot3(das, ks)
            dk = (dot3(das, q, TN) + trail * dot3(us, ds1s, NT) - (beta * lead) * dot3(drs, ss, NT)
                  + dot3(dp, ks) + dot3(dp, ks, TN))
            dsq = rq * (dq - q * jnp.sum(q * dq, axis=-1, keepdims=True))
            dsk = rk * (dk - k * jnp.sum(k * dk, axis=-1, keepdims=True))
            dcs[0][b][h] = dsq * gq * (1.0 + cq * (1.0 - gq))
            dcs[1][b][h] = dsk * gk * (1.0 + ck * (1.0 - gk))
            dcs[2][b][h] = dv * gv * (1.0 + cv * (1.0 - gv))
            dl = jnp.where(lane == h, dbeta * pad * gb * (1.0 - gb), dl)
        dlog[b] = dl
    gains_ref[7:8, :HEAD] += dgain
    for b in range(cb):
        dpre[b * C:(b + 1) * C, 3 * width:] = dlog[b].astype(BF)
    for i in range(3):
        dc = jnp.concatenate([jnp.concatenate(dcs[i][b], axis=1) for b in range(cb)], axis=0)
        pre = pre_ref[:, i * width:(i + 1) * width]
        tot = dc * taps_ref[i, 0:1, :]
        grads = [jnp.sum(dc * pre, axis=0, keepdims=True)]
        for j in range(1, taps):
            e = dc * cols_ref[:, j - 1:j]
            ext = jnp.concatenate([e, head_rows[j - 1, :, i * width:(i + 1) * width]], axis=0)
            head_rows[j - 1, :, i * width:(i + 1) * width] = e[:8]
            e = lax.slice_in_dim(ext, j, j + rows, axis=0)
            tot = tot + e * taps_ref[i, j:j + 1, :]
            grads.append(jnp.sum(e * pre, axis=0, keepdims=True))
        dpre[:, i * width:(i + 1) * width] = tot.astype(BF)
        small_ref[i:i + 1, :taps * width] += jnp.concatenate(grads, axis=1)
    low = dpre[...]
    acc[:, :3 * width] += lax.dot_general(na_ref[...], low[:, :3 * width], TN, preferred_element_type=F32)
    acc[:, 4 * width:] += lax.dot_general(na_ref[...], low[:, 3 * width:], TN, preferred_element_type=F32)
    dna = lax.dot_general(low, wide_ref[...], NT, preferred_element_type=F32)
    x = x_ref[...].astype(F32)
    gains_ref[5:6, :] += jnp.sum(dna * (x * lax.rsqrt(jnp.mean(x * x, axis=-1, keepdims=True) + 1e-6)), axis=0, keepdims=True)

    @pl.when(back % 2 == core)
    def _():
        kna_ref[back // 2] = dna

    @pl.when(back % 2 != core)
    def _():
        sna_ref[back // 2] = dna.astype(BF)

    @pl.when(step == steps - 1)
    def _():
        small_ref[3:3 + heads, :] = acc[:, 4 * width:].T[:heads, :]
        me = lax.axis_index("fsdp")
        first, second = stage_bits(n_f)
        half = 2 * width
        for ref, other, bit, lanes in ((away1_ref, keep1_ref, first[0], slice(0, half)), (away2_ref, keep2_ref, second[0], slice(half, 2 * half))):
            mine = (me // bit) % 2
            for j in range(n_f // 2):
                low_bits = j % bit
                there = (j - low_bits) * 2 + low_bits
                ref[j] = acc[pl.ds(pl.multiple_of((there + (1 - mine) * bit) * shard, 16), shard), lanes].astype(BF)
                other[j] = acc[pl.ds(pl.multiple_of((there + mine * bit) * shard, 16), shard), lanes].astype(other.dtype)


def whole(shape):
    return pl.BlockSpec(shape, lambda i, *_: (0,) * len(shape), pipeline_mode=pl.Buffered(1))


def shaped(shape, dtype=F32):
    return jax.ShapeDtypeStruct(shape, dtype)


def params(limit=60):
    return pltpu.CompilerParams(dimension_semantics=("arbitrary",), vmem_limit_bytes=limit * 2**20)


COST = pl.CostEstimate(flops=10**10, bytes_accessed=10**7, transcendentals=0)
TINY = pl.CostEstimate(flops=1, bytes_accessed=1, transcendentals=0)


def fwd_call_kernel(heads, cb, base, n_old, *refs):
    ins, rest = ((*refs[:8], None, None), refs[8:]) if n_old == 0 else (refs[:10], refs[10 + n_old:])
    outs, tail_out, state_out, tail, state, line = rest[:14], rest[14], rest[15], rest[16], rest[17], rest[18]
    fwd_kernel(heads, cb, base, *ins, *outs, tail, state, line)

    @pl.when(pl.program_id(0) == pl.num_programs(0) - 1)
    def _():
        tail_out[...] = tail[...]
        state_out[...] = state[...]


def mixer_fwd(part, parts, x, wide, again, cols, segr, seg, taps, gain, tail, state, old, cb=4):
    n, d = x.shape
    width = taps.shape[2]
    heads = width // HEAD
    wide_cols = 3 * width + HEAD
    rows = cb * C
    steps = n // parts // rows
    base = part * steps
    sq = shaped((n // C, heads, C, HEAD))
    sqspec = pl.BlockSpec((cb, heads, C, HEAD), lambda i, s: (i + base, 0, 0, 0))
    here = lambda w: pl.BlockSpec((rows, w), lambda i, s: (i + base, 0))
    ins = [x, wide, again, cols, segr, taps, gain] + ([tail, state] if old else [])
    tail, state = shaped((8, 3 * width)), shaped((heads, HEAD, HEAD))
    kept = [shaped((n, width), BF), shaped((n, d), BF), shaped((n, wide_cols)), shaped((n, 3 * width)), shaped((n, width))] + [sq] * 8
    return pl.pallas_call(
        functools.partial(fwd_call_kernel, heads, cb, base, len(old)),
        grid_spec=pltpu.PrefetchScalarGridSpec(
            num_scalar_prefetch=1, grid=(steps,),
            in_specs=[here(d), whole((d, wide_cols)), whole((1, d)), here(cols.shape[1]),
                      pl.BlockSpec((1, rows), lambda i, s: (0, i + base)),
                      whole(taps.shape), whole((1, HEAD))] + ([whole(tail.shape), whole(state.shape)] if old else [])
            + [pl.BlockSpec(memory_space=pl.ANY)] * len(old),
            out_specs=[pl.BlockSpec((rows, width), lambda i, s: (i, 0)), here(width), here(d), here(wide_cols), here(3 * width), here(width)]
            + [sqspec] * 8 + [whole(tail.shape), whole(state.shape)],
            scratch_shapes=[pltpu.VMEM(tail.shape, F32), pltpu.VMEM(state.shape, F32), pltpu.VMEM((rows + 8, 3 * width), F32)]),
        out_shape=[shaped((n // parts, width), BF)] + kept + [shaped(tail.shape), shaped(state.shape)],
        input_output_aliases={1 + len(ins) + i: 1 + i for i in range(len(old))},
        compiler_params=params(),
        cost_estimate=COST,
        name="mixer_fwd",
    )(seg, *ins, *old)


def mixer_bwd(n_f, shard, ga, out, wide, x, dffn, cols, segr, seg, taps, gain, kept, cb=2):
    mix, na, pre, conv, o, *rest = kept
    n, wide_cols = pre.shape
    d = x.shape[1]
    width = taps.shape[2]
    heads = width // HEAD
    rows = cb * C
    steps = n // rows
    ntap = taps.shape[1]
    sqspec = pl.BlockSpec((cb, heads, C, HEAD), lambda i, s: (steps - 1 - i, 0, 0, 0))
    row = lambda w: pl.BlockSpec((rows, w), lambda i, s: (steps - 1 - i, 0))
    outs = [shaped((n_f // 2, shard, 2 * width), BF)] * 4 + [
            shaped((2, rows, d), BF), shaped((2, rows, d)), shaped((8, d)), shaped((8, d))]
    return pl.pallas_call(
        functools.partial(bwd_kernel, heads, cb, n_f, shard),
        grid_spec=pltpu.PrefetchScalarGridSpec(
            num_scalar_prefetch=1, grid=(steps,),
            in_specs=[whole((rows, d))] * 4 + [row(width), row(d), whole(out.shape), whole((d, wide_cols)), row(d), whole((1, d)), whole((1, d)),
                      row(wide_cols), row(3 * width), row(width),
                      row(cols.shape[1]), pl.BlockSpec((1, rows), lambda i, s: (0, steps - 1 - i)),
                      whole(taps.shape), whole((1, HEAD))] + [sqspec] * 8,
            out_specs=[whole(v.shape) for v in outs],
            scratch_shapes=[pltpu.VMEM((ntap - 1, 8, 3 * width), F32), pltpu.VMEM((heads, HEAD, HEAD), F32),
                            pltpu.VMEM((d, 4 * width + HEAD), F32), pltpu.VMEM((rows, wide_cols), BF)]),
        out_shape=outs,
        compiler_params=params(),
        cost_estimate=COST,
        name="mixer_bwd",
    )(seg, *ga, mix, na, out, wide, x, *dffn, pre, conv, o, cols, segr, taps, gain, *rest)


def fold_kernel(n_f, stage, k1_ref, g1_ref, k2_ref, g2_ref, a1_out, k1_out, a2_out, k2_out):
    me = lax.axis_index("fsdp")
    for order, keep, got, away_out, keep_out in ((0, k1_ref, g1_ref, a1_out, k1_out), (1, k2_ref, g2_ref, a2_out, k2_out)):
        bits = stage_bits(n_f)[order]
        bit = bits[stage]
        left = sorted(b for b in bits[stage:])
        place = 1 << left.index(bit)
        mine = (me // bit) % 2
        for j in range(keep.shape[0] // 2):
            low = j % place
            there = (j - low) * 2 + low
            theirs = there + (1 - mine) * place
            away_out[j] = (keep[theirs].astype(F32) + got[theirs].astype(F32)).astype(BF)
            ours = there + mine * place
            keep_out[j] = (keep[ours].astype(F32) + got[ours].astype(F32)).astype(keep_out.dtype)


def fold(n_f, stage, k1, g1, k2, g2):
    m, shard, w = k1.shape
    outs = [shaped((m // 2, shard, w), BF)] * 4
    return pl.pallas_call(
        functools.partial(fold_kernel, n_f, stage),
        out_shape=outs,
        compiler_params=pltpu.CompilerParams(vmem_limit_bytes=60 * 2**20),
        cost_estimate=TINY,
        name="fold",
    )(k1, g1, k2, g2)


def finish_kernel(heads, ntap, k1_ref, g1_ref, k2_ref, g2_ref, s_ref, *refs):
    got, (qkv_ref, out_ref, taps_ref, beta_ref, attn_ref, ffn_ref, head_ref, hold) = refs[:-9], refs[-8:]
    width = qkv_ref.shape[2]
    shard = qkv_ref.shape[1]
    a = k1_ref[0].astype(F32) + g1_ref[0].astype(F32)
    b = k2_ref[0].astype(F32) + g2_ref[0].astype(F32)
    qkv_ref[0] = a[:, :width]
    qkv_ref[1] = a[:, width:]
    qkv_ref[2] = b[:, :width]
    out_ref[...] = b[:, width:].T
    small = s_ref[...]
    for g in got:
        small = small + g[...]
    width = taps_ref.shape[2]
    for i in range(3):
        for k in range(ntap):
            taps_ref[i, k:k + 1, :] = small[i:i + 1, k * width:(k + 1) * width]
    attn_ref[...] = small[5:6]
    ffn_ref[...] = small[6:7]
    head_ref[...] = small[7:8, :HEAD]
    if shard == 128:
        hold[...] = small
        me = lax.axis_index("fsdp")
        beta_ref[...] = hold[3:3 + heads, pl.ds(pl.multiple_of(me * shard, 128), shard)]
    else:
        beta_ref[...] = small[3:3 + heads]


def finish(heads, ntap, k1, g1, k2, g2, small, got, wait_for):
    m, shard, w = k1.shape
    d = small.shape[1]
    return pl.pallas_call(
        functools.partial(finish_kernel, heads, ntap),
        in_specs=[pl.BlockSpec(memory_space=pltpu.VMEM)] * (5 + len(got)) + [pl.BlockSpec(memory_space=pl.ANY)],
        out_shape=[shaped((3, shard, w // 2)), shaped((w // 2, shard)), shaped((3, ntap, w // 2)),
                   shaped((heads, 128 if shard == 128 else d)), shaped((1, d)), shaped((1, d)), shaped((1, HEAD))],
        scratch_shapes=[pltpu.VMEM((8, d), F32)],
        compiler_params=pltpu.CompilerParams(vmem_limit_bytes=60 * 2**20),
        cost_estimate=TINY,
        name="finish",
    )(k1, g1, k2, g2, small, *got, wait_for)


def ffn_kernel(ff, *refs):
    m, out, (x_ref, w_ref, gf_ref, gain_ref), rest = refs[:4], refs[4:8], refs[8:12], refs[12:]
    mid_ref, nf_ref, hid_ref, dgu_ref, keep_ref, send_ref, dgain_ref, hold = rest
    rows = keep_ref.shape[0]
    core = lax.axis_index("tensor") % 2
    mid = x_ref[...].astype(F32)
    for k in range(4):
        mid = mid + lax.dot_general(m[k][...], out[k][...], NT, preferred_element_type=F32)
    hold[...] = mid
    unit = mid * lax.rsqrt(jnp.mean(mid * mid, axis=-1, keepdims=True) + 1e-6)
    nf = (unit * gain_ref[0:1, :]).astype(BF)
    nf_ref[...] = nf
    mid_ref[...] = hold[pl.ds(pl.multiple_of(core * rows, 16), rows), :]
    gate = lax.dot_general(w_ref[:ff, :], nf, NT, preferred_element_type=F32)
    up = lax.dot_general(w_ref[ff:2 * ff, :], nf, NT, preferred_element_type=F32)
    dh = lax.dot_general(w_ref[2 * ff:, :], gf_ref[...], NT, preferred_element_type=F32)
    sig = sigmoid(gate)
    act = gate * sig
    hid_ref[...] = (act * up).astype(BF)
    dgu_ref[:ff, :] = (dh * up * sig * (1.0 + gate * (1.0 - sig))).astype(BF)
    dgu_ref[ff:, :] = (dh * act).astype(BF)
    dnf = lax.dot_general(dgu_ref[...], w_ref[:2 * ff, :], TN, preferred_element_type=F32)
    dgain_ref[...] = jnp.sum(dnf * unit, axis=0, keepdims=True)
    hold[...] = dnf
    keep_ref[...] = hold[pl.ds(pl.multiple_of(core * rows, 16), rows), :]
    send_ref[...] = hold[pl.ds(pl.multiple_of((1 - core) * rows, 16), rows), :].astype(BF)


def ffn(part, m, out, x, weights, gf, gain):
    n, width = m[0].shape
    d = x.shape[1]
    ff = weights.shape[0] // 3
    here = pl.BlockSpec((n, d), lambda i: (part, 0))
    outs = [shaped((n // 2, d)), shaped((n, d), BF), shaped((ff, n), BF), shaped((2 * ff, n), BF),
            shaped((n // 2, d)), shaped((n // 2, d), BF), shaped((1, d))]
    return pl.pallas_call(
        functools.partial(ffn_kernel, ff),
        grid=(1,),
        in_specs=[whole(v.shape) for v in (*m, *out)] + [here, whole(weights.shape), here, whole((1, d))],
        out_specs=[whole(v.shape) for v in outs],
        out_shape=outs,
        scratch_shapes=[pltpu.VMEM((n, d), F32)],
        compiler_params=params(),
        cost_estimate=COST,
        name="ffn",
    )(*m, *out, x, weights, gf, gain)


def grad_kernel(part, n, *refs):
    lows, others, (mid_ref, cot_ref, coty_ref, gain_ref, grad_ref, low_out) = refs[:n], refs[n:2 * n], refs[2 * n:]
    chip = lax.axis_index("tensor") // 2
    mid = mid_ref[...]
    factor = lax.rsqrt(jnp.mean(mid * mid, axis=-1, keepdims=True) + 1e-6)
    d_nf = jnp.concatenate([a[...].astype(F32) + b[...].astype(F32) for a, b in zip(lows, others)], axis=0)
    u = d_nf * gain_ref[0:1, :]
    cot = jnp.where(chip == part, cot_ref[...], coty_ref[...]).astype(F32)
    grad = cot + factor * u - mid * (factor * factor * factor) * jnp.mean(u * mid, axis=-1, keepdims=True)
    grad_ref[...] = grad
    low_out[...] = grad.astype(BF)


def grad_rows(part, lows, others, mid, cot, cot_y, gain):
    return pl.pallas_call(
        functools.partial(grad_kernel, part, len(lows)),
        out_shape=[shaped(mid.shape), shaped(mid.shape, BF)],
        compiler_params=pltpu.CompilerParams(vmem_limit_bytes=24 * 2**20),
        cost_estimate=TINY,
        name="grad_rows",
    )(*lows, *others, mid, cot, cot_y, gain)


def down_kernel(hid0_ref, hid1_ref, w_ref, send_ref, keep_ref, hold):
    core = lax.axis_index("tensor") % 2
    rows = send_ref.shape[1]
    for i, hid in enumerate((hid0_ref, hid1_ref)):
        hold[...] = lax.dot_general(hid[...], w_ref[...], TN, preferred_element_type=F32)
        keep_ref[i] = hold[pl.ds(pl.multiple_of(core * rows, 16), rows), :]
        send_ref[i] = hold[pl.ds(pl.multiple_of((1 - core) * rows, 16), rows), :].astype(BF)


def down(hid0, hid1, weights, wait_for):
    ff, n = hid0.shape
    d = weights.shape[1]
    outs = [shaped((2, n // 2, d), BF), shaped((2, n // 2, d))]

    def body(*refs):
        down_kernel(*refs[:3], *refs[3 + len(wait_for):])

    return pl.pallas_call(
        body,
        grid=(1,),
        in_specs=[whole(hid0.shape)] * 2 + [pl.BlockSpec((ff, d), lambda i: (2, 0))] + [pl.BlockSpec(memory_space=pl.ANY)] * len(wait_for),
        out_specs=[whole(v.shape) for v in outs],
        out_shape=outs,
        scratch_shapes=[pltpu.VMEM((n, d), F32)],
        compiler_params=params(),
        cost_estimate=TINY,
        name="down",
    )(hid0, hid1, weights, *wait_for)


def ffn_grads_kernel(ff, parts, *refs):
    gf_ref, o_ref = refs[3 * parts], refs[-1]
    n = refs[0].shape[1]
    up = down = None
    for i in range(parts):
        dgu, hid, nf = refs[3 * i:3 * i + 3]
        a = jnp.dot(dgu[...], nf[...], preferred_element_type=F32)
        b = jnp.dot(hid[...], gf_ref[i * n:(i + 1) * n, :], preferred_element_type=F32)
        up = a if up is None else up + a
        down = b if down is None else down + b
    for k in range(o_ref.shape[0]):
        lanes = slice(k * 128, (k + 1) * 128)
        o_ref[k, :2 * ff, :] = up[:, lanes].astype(BF)
        o_ref[k, 2 * ff:, :] = down[:, lanes].astype(BF)


def ffn_grads(pieces, gf, wait_for, step=256):
    ff = pieces[0][1].shape[0]
    n, d = gf.shape
    flat, specs = [], []
    for dgu, hid, nf in pieces:
        flat += [dgu, hid, nf]
        specs += [whole(dgu.shape), whole(hid.shape), pl.BlockSpec((nf.shape[0], step), lambda i: (0, i))]
    return pl.pallas_call(
        functools.partial(ffn_grads_kernel, ff, len(pieces)),
        grid=(d // step,),
        in_specs=specs + [pl.BlockSpec((n, step), lambda i: (0, i))] + [pl.BlockSpec(memory_space=pl.ANY)] * len(wait_for),
        out_specs=pl.BlockSpec((step // 128, 3 * ff, 128), lambda i: (i, 0, 0)),
        out_shape=shaped((d // 128, 3 * ff, 128), BF),
        compiler_params=params(),
        cost_estimate=pl.CostEstimate(flops=5 * 10**9, bytes_accessed=10**7, transcendentals=0),
        name="ffn_grads",
    )(*flat, gf, *wait_for)


def to_chips_kernel(keep, got, wait_for, mine_ref, away_ref):
    chip = lax.axis_index("tensor") // 2
    mine_ref[...] = keep[chip] + got[chip].astype(F32)
    away_ref[...] = (keep[1 - chip] + got[1 - chip].astype(F32)).astype(BF)


def to_chips(keep, got, wait_for):
    spec = pl.BlockSpec(memory_space=pltpu.VMEM)
    return pl.pallas_call(
        to_chips_kernel,
        in_specs=[spec] * 2 + [pl.BlockSpec(memory_space=pl.ANY)],
        out_shape=[shaped(keep.shape[1:]), shaped(keep.shape[1:], BF)],
        compiler_params=pltpu.CompilerParams(vmem_limit_bytes=60 * 2**20),
        cost_estimate=TINY,
        name="to_chips",
    )(keep, got, wait_for)


def last_kernel(g0, g1, na, na_y, x_ref, gain_ref, mid0, mid1, out, out_y, in_ref, block_ref):
    first = lax.axis_index("tensor") // 2 == 0
    x = x_ref[...].astype(F32)
    factor = lax.rsqrt(jnp.mean(x * x, axis=-1, keepdims=True) + 1e-6)
    u = (na[...] + na_y[...].astype(F32)) * gain_ref[0:1, :]
    in_ref[...] = jnp.where(first, g0[...], g1[...]) + (factor * u - x * (factor * factor * factor) * jnp.mean(u * x, axis=-1, keepdims=True))
    block_ref[...] = (jnp.where(first, mid0[...], mid1[...]) + out[...] + out_y[...].astype(F32)).astype(BF)


def last_rows(g0, g1, na, na_y, x, gain, mid0, mid1, out, out_y):
    return pl.pallas_call(
        last_kernel,
        out_shape=[shaped(g0.shape), shaped(g0.shape, BF)],
        compiler_params=pltpu.CompilerParams(vmem_limit_bytes=60 * 2**20),
        cost_estimate=TINY,
        name="last_rows",
    )(g0, g1, na, na_y, x, gain, mid0, mid1, out, out_y)


def ffn_cast_kernel(d_ref, expand_ref, down_ref):
    ff = down_ref.shape[0]
    expand_ref[0] = d_ref[:ff, :].astype(F32)
    expand_ref[1] = d_ref[ff:2 * ff, :].astype(F32)
    down_ref[...] = d_ref[2 * ff:, :].astype(F32)


def ffn_cast(d):
    ff, w = d.shape[0] // 3, d.shape[1]
    return pl.pallas_call(
        ffn_cast_kernel,
        out_shape=[shaped((2, ff, w)), shaped((ff, w))],
        compiler_params=pltpu.CompilerParams(vmem_limit_bytes=60 * 2**20),
        cost_estimate=TINY,
        name="ffn_cast",
    )(d)


def ffn_split_kernel(ff, parts, *refs):
    blocks, expand, away, keep = refs[-1], refs[-4], refs[-3], refs[-2]
    ffn_grads_kernel(ff, parts, *refs[:3 * parts + 1], blocks)
    me = lax.axis_index("fsdp")
    for k in range(blocks.shape[0]):
        expand[k] = blocks[k, :2 * ff, :]
        block = pl.program_id(0) * blocks.shape[0] + k

        @pl.when(block % 2 == me % 2)
        def _(k=k, block=block):
            keep[block // 2] = blocks[k, 2 * ff:, :]

        @pl.when(block % 2 != me % 2)
        def _(k=k, block=block):
            away[block // 2] = blocks[k, 2 * ff:, :]


def ffn_split_grads(pieces, gf, wait_for, step=256):
    ff = pieces[0][1].shape[0]
    n, d = gf.shape
    flat, specs = [], []
    for dgu, hid, nf in pieces:
        flat += [dgu, hid, nf]
        specs += [whole(dgu.shape), whole(hid.shape), pl.BlockSpec((nf.shape[0], step), lambda i: (0, i))]
    per = step // 128
    halves = shaped((d // 256, ff, 128), BF)
    return pl.pallas_call(
        functools.partial(ffn_split_kernel, ff, len(pieces)),
        grid=(d // step,),
        in_specs=specs + [pl.BlockSpec((n, step), lambda i: (0, i))] + [pl.BlockSpec(memory_space=pl.ANY)] * len(wait_for),
        out_specs=[pl.BlockSpec((per, 2 * ff, 128), lambda i: (i, 0, 0)), whole(halves.shape), whole(halves.shape)],
        out_shape=[shaped((d // 128, 2 * ff, 128), BF), halves, halves],
        scratch_shapes=[pltpu.VMEM((per, 3 * ff, 128), BF)],
        compiler_params=params(),
        cost_estimate=COST,
        name="ffn_grads",
    )(*flat, gf, *wait_for)


def halve_kernel(bit, k_ref, g_ref, wait_for, away, keep):
    mine = (lax.axis_index("fsdp") // bit) % 2
    count = k_ref.shape[0] // 2
    for j in range(count):
        ours, theirs = (2 * j + mine, 2 * j + 1 - mine) if bit == 2 else (mine, 1 - mine)
        away[j] = (k_ref[theirs].astype(F32) + g_ref[theirs].astype(F32)).astype(BF)
        keep[j] = (k_ref[ours].astype(F32) + g_ref[ours].astype(F32)).astype(BF)


def halve(bit, k, g, wait_for):
    m, ff, w = k.shape
    spec = pl.BlockSpec(memory_space=pltpu.VMEM)
    return pl.pallas_call(
        functools.partial(halve_kernel, bit),
        in_specs=[spec] * 2 + [pl.BlockSpec(memory_space=pl.ANY)],
        out_shape=[shaped((m // 2, ff, w), BF)] * 2,
        compiler_params=pltpu.CompilerParams(vmem_limit_bytes=60 * 2**20),
        cost_estimate=TINY,
        name="halve",
    )(k, g, wait_for)


def split_cast_kernel(d_ref, k_ref, g_ref, expand_ref, down_ref):
    ff = down_ref.shape[0]
    expand_ref[0] = d_ref[:ff, :].astype(F32)
    expand_ref[1] = d_ref[ff:, :].astype(F32)
    down_ref[...] = k_ref[0].astype(F32) + g_ref[0].astype(F32)


def split_cast(d, k, g):
    ff, w = d.shape[0] // 2, d.shape[1]
    return pl.pallas_call(
        split_cast_kernel,
        out_shape=[shaped((2, ff, w)), shaped((ff, w))],
        compiler_params=pltpu.CompilerParams(vmem_limit_bytes=60 * 2**20),
        cost_estimate=TINY,
        name="ffn_cast",
    )(d, k, g)


def pack_kernel(qkv_ref, beta_ref, out_ref, o_ref):
    width = qkv_ref.shape[2]
    n = o_ref.shape[0]
    for i in range(3):
        o_ref[:, i * width:(i + 1) * width] = qkv_ref[i]
    beta = beta_ref[...].astype(F32)
    heads = beta.shape[1]
    o_ref[:, 3 * width:3 * width + 128] = jnp.concatenate([beta, jnp.zeros((n, 128 - heads), F32)], axis=1).astype(BF)
    o_ref[:, 3 * width + 128:] = out_ref[...].astype(F32).T.astype(BF)


def pack(qkv, beta, out):
    n, width = qkv.shape[1:]
    return pl.pallas_call(
        pack_kernel,
        out_shape=shaped((n, 4 * width + 128), BF),
        compiler_params=pltpu.CompilerParams(vmem_limit_bytes=60 * 2**20),
        name="pack",
    )(qkv, beta, out)


def columns(seg, pad):
    n = seg.shape[0]
    cols = []
    for j in range(1, 4):
        before = jnp.concatenate([jnp.full((j,), -1, seg.dtype), seg[:n - j]])
        cols.append((before == seg).astype(F32))
    cols += [pad.astype(F32), seg.astype(F32)]
    cols += [jnp.zeros((n,), F32)] * 3
    return jnp.stack(cols, axis=1)


def hop(value, axis, bit):
    n = lax.axis_size(axis)
    return lax.ppermute(value, axis, [(i, i ^ bit) for i in range(n)])


def fence(*values):
    return lax.optimization_barrier(values)


def y_hop(value):
    return hop(value, "tensor", 2)


def core_hop(value):
    return hop(value, "tensor", 1)


def in_order(own, other_chip, pair):
    me = lax.axis_index("tensor")
    full = jnp.zeros((4,) + own.shape, own.dtype)
    for k, block in ((0, own), (2, other_chip), (1, pair[0]), (3, pair[1])):
        full = lax.dynamic_update_slice(full, block[None], (me ^ k,) + (0,) * own.ndim)
    return full.reshape((4 * own.shape[0],) + own.shape[1:])


class Ring:
    def __init__(self, value):
        n = lax.axis_size("fsdp")
        order = [i for i in range(0, n, 2)] + [i for i in reversed(range(1, n, 2))]
        me = lax.axis_index("fsdp")
        self.n = n
        self.me = jnp.where(me % 2 == 0, me // 2, n - 1 - me // 2)
        self.right = [(order[i], order[(i + 1) % n]) for i in range(n)]
        self.left = [(b, a) for a, b in self.right]
        self.rows = value.shape[0]
        self.full = jnp.zeros((n * self.rows,) + value.shape[1:], value.dtype)
        self.a = self.b = value
        self.k = 0
        self.put(value, 0, 0)

    def put(self, part, steps, start):
        place = lax.rem(self.me + steps + self.n, self.n)
        owner = jnp.where(place < self.n // 2, 2 * place, 2 * (self.n - 1 - place) + 1)
        self.full = lax.dynamic_update_slice(self.full, part, (owner * self.rows + start, 0))

    def step(self):
        self.k += 1
        k, half = self.k, self.rows // 2
        self.split = 2 * k == self.n and half % 16 == 0
        if self.split:
            self.a = lax.ppermute(self.a[:half], "fsdp", self.right)
            self.b = lax.ppermute(self.b[half:], "fsdp", self.left)
            return
        self.a = lax.ppermute(self.a, "fsdp", self.right)
        if 2 * k < self.n:
            self.b = lax.ppermute(self.b, "fsdp", self.left)

    def keep(self):
        self.put(self.a, -self.k, 0)
        if self.split or 2 * self.k < self.n:
            self.put(self.b, self.k, self.rows // 2 if self.split else 0)


def hop_sum(value, axis, bit):
    return value + hop(value, axis, bit)


def on_device(
    layer_input, segment_ids, pad_mask, attn_gain, ffn_gain, out_gain,
    qkv_weight, beta_weight, conv_weight, out_weight, expand_weight, down_weight, cotangent,
):
    n_f = lax.axis_size("fsdp")
    me_t = lax.axis_index("tensor")
    chip = me_t // 2
    rows, d_model = layer_input.shape
    width = qkv_weight.shape[3]
    heads = beta_weight.shape[2]
    ff = down_weight.shape[1]
    shard = qkv_weight.shape[2]
    taps = conv_weight[0]
    ntap = taps.shape[1]
    first_bits, second_bits = stage_bits(n_f)

    packed = pack(qkv_weight[0], beta_weight[0], out_weight[0])
    packed, expand_own, down_own = fence(packed, expand_weight[0], down_weight[0])
    ring = Ring(packed)
    ring.step()
    x_y = y_hop(layer_input)
    x_c = core_hop(layer_input)
    ffn_own = jnp.concatenate([expand_own[0].T, expand_own[1].T, down_own], axis=0)
    weights = lax.all_gather(ffn_own, "fsdp", axis=1, tiled=True)
    seg = segment_ids[0]
    cols = columns(seg, pad_mask[0])
    segr = seg.astype(F32)[None]
    ring.a, ring.b, x_y, x_c = fence(ring.a, ring.b, x_y, x_c)
    ring.keep()
    ring.step()
    x_cy = core_hop(x_y)
    c_y = y_hop(cotangent)
    c_c = core_hop(cotangent)
    ring.a, ring.b, x_cy = fence(ring.a, ring.b, x_cy)
    ring.keep()
    ring.step()
    x_full = in_order(layer_input, x_y, (x_c, x_cy))
    ring.a, ring.b, x_full, cols, c_y = fence(ring.a, ring.b, x_full, cols, c_y)
    ring.keep()
    while 2 * ring.k < n_f:
        ring.step()
        ring.keep()
    c_cy = core_hop(c_y)
    g_f = in_order(cotangent, c_y, (c_c, c_cy))
    wide, g_f = fence(ring.full, g_f)

    out_own = wide[:, 3 * width + HEAD:]
    tail = state = None

    def mix(i, tail, state, old):
        m, *kept, tail, state = mixer_fwd(i, 2, x_full, wide, attn_gain, cols, segr, seg, taps, out_gain, tail, state, old)
        return m, kept, tail, state

    ow_y = y_hop(out_own)
    ow_c = core_hop(out_own)
    m0, kept, tail, state = mix(0, tail, state, [])
    ow_y, ow_c, m0, tail, state = fence(ow_y, ow_c, m0, tail, state)
    m0_y = y_hop(m0)
    m0_c = core_hop(m0)
    ow_cy = core_hop(ow_y)
    m1, kept, tail, state = mix(1, tail, state, kept)
    m0_y, m0_c, ow_cy, m1 = fence(m0_y, m0_c, ow_cy, m1)

    def feed(i, *m):
        return ffn(i, m, (out_own, ow_y, ow_c, ow_cy), x_full, weights, g_f, ffn_gain)

    m1_y = y_hop(m1)
    m1_c = core_hop(m1)
    m0_cy = core_hop(m0_y)
    mid0, nf0, hid0, dgu0, keep0, send0, dgain0 = feed(0, m0, m0_y, m0_c, m0_cy)
    m1_y, m1_c, send0 = fence(m1_y, m1_c, send0)
    m1_cy = core_hop(m1_y)
    low0 = (keep0 + core_hop(send0).astype(F32)).astype(BF)
    m1_cy, low0 = fence(m1_cy, low0)
    low0_y = y_hop(low0)
    mid1, nf1, hid1, dgu1, keep1, send1, dgain1 = feed(1, m1, m1_y, m1_c, m1_cy)
    low0_y, send1 = fence(low0_y, send1)
    cut = rows // 2
    got1 = core_hop(send1)
    low1 = (keep1[:cut] + got1[:cut].astype(F32)).astype(BF)
    low1b = (keep1[cut:] + got1[cut:].astype(F32)).astype(BF)
    grad0, ga0 = grad_rows(0, [low0], [low0_y], mid0, cotangent, c_y, ffn_gain)
    low1, low1b, ga0 = fence(low1, low1b, ga0)
    low1_y, low1b_y = y_hop(low1), y_hop(low1b)
    ga0_c = core_hop(ga0)
    blocks = ffn_grads([(dgu0, hid0, nf0), (dgu1, hid1, nf1)], g_f, [low1])
    q = d_model // 128
    if q != n_f:
        blocks = blocks.reshape(q, 3 * ff, n_f // q, shard).transpose(0, 2, 1, 3).reshape(n_f, 3 * ff, shard)
    send_out, keep_out = down(hid0, hid1, weights, [blocks])
    low1_y, ga0_c, blocks = fence(low1_y, ga0_c, blocks)
    low1b_y, send_out, done_blocks = fence(low1b_y, send_out, blocks)
    d_ffn = lax.psum_scatter(blocks, "fsdp", scatter_dimension=0, tiled=False)
    grad1, ga1 = grad_rows(1, [low1, low1b], [low1_y, low1b_y], mid1, cotangent, c_y, ffn_gain)
    ga1_c = core_hop(ga1)
    ga1, ga1_c = fence(ga1, ga1_c)

    out_c = core_hop(send_out)
    made = mixer_bwd(
        n_f, shard, (ga0, ga0_c, ga1, ga1_c), out_own, wide, x_full, (dgain0, dgain1), cols, segr, seg, taps, out_gain, kept)
    away1, k1, away2, k2, send_na, keep_na, gains, small, out_c = fence(*made, out_c)

    g1 = hop(away1, "fsdp", first_bits[0])
    g2 = hop(away2, "fsdp", second_bits[0])
    na_c = core_hop(send_na)
    gains_got = [hop(gains, "tensor", k) for k in range(1, 4)]
    out, out_away = to_chips(keep_out, out_c, done_blocks)
    na, na_away = to_chips(keep_na, na_c, gains)
    g1, g2, na_away, out_away, *gains_got = fence(g1, g2, na_away, out_away, *gains_got)
    count = len(first_bits)
    small = small + gains + gains_got[0] + (gains_got[1] + gains_got[2])
    for stage in range(1, count):
        away1, k1, away2, k2 = fold(n_f, stage, k1, g1, k2, g2)
        if stage == 1:
            na_y, out_y = y_hop(na_away), y_hop(out_away)
        g1 = hop(away1, "fsdp", first_bits[stage])
        g2 = hop(away2, "fsdp", second_bits[stage])
        if stage < count - 1:
            small = hop_sum(small, "fsdp", first_bits[stage - 1])
            g1, g2, small, na_y = fence(g1, g2, small, na_y)
    if n_f == 8:
        got = [hop(small, "fsdp", k) for k in (2, 4, 6)]
    else:
        small = hop_sum(small, "fsdp", first_bits[count - 2])
        got = [hop(small, "fsdp", first_bits[count - 1])]
    input_grad, block_outs = last_rows(grad0, grad1, na, na_y, layer_input, attn_gain, mid0, mid1, out, out_y)
    block_outs = block_outs[None]
    expand_grad, down_grad = ffn_cast(d_ffn)
    qkv_grad, out_grad, conv_grad, beta_grad, attn_total, ffn_total, head_total = finish(heads, ntap, k1, g1, k2, g2, small, got, down_grad)
    if shard != 128:
        beta_grad = lax.dynamic_slice(beta_grad, (0, lax.axis_index("fsdp") * shard), (heads, shard))
    beta_grad = beta_grad.T
    expand_grad = expand_grad.transpose(0, 2, 1)
    return (
        block_outs, input_grad, attn_total, ffn_total, head_total, qkv_grad[None], beta_grad[None],
        conv_grad[None], out_grad[None], expand_grad[None], down_grad[None],
    )


def solution(mesh):
    in_specs = (
        P(("fsdp", "tensor"), None),
        P("fsdp", None),
        P("fsdp", None),
        P(),
        P(),
        P(),
        P(None, None, "fsdp", "tensor"),
        P(None, "fsdp", "tensor"),
        P(None, None, None, "tensor"),
        P(None, "tensor", "fsdp"),
        P(None, None, "fsdp", "tensor"),
        P(None, "tensor", "fsdp"),
        P(("fsdp", "tensor"), None),
    )
    out_specs = (
        P(None, ("fsdp", "tensor"), None),
        P(("fsdp", "tensor"), None),
        P(),
        P(),
        P(),
        P(None, None, "fsdp", "tensor"),
        P(None, "fsdp", "tensor"),
        P(None, None, None, "tensor"),
        P(None, "tensor", "fsdp"),
        P(None, None, "fsdp", "tensor"),
        P(None, "tensor", "fsdp"),
    )
    return jax.shard_map(
        on_device, mesh=mesh, in_specs=in_specs, out_specs=out_specs, check_vma=False
    )
```

```python
import functools
import jax
import jax.numpy as jnp
from jax import lax
from jax.experimental import pallas as pl
from jax.experimental.pallas import tpu as pltpu
from jax.sharding import PartitionSpec as P

HEAD = 128
C = 128
F32 = jnp.float32
BF = jnp.bfloat16

NN = (((1,), (0,)), ((), ()))
NT = (((1,), (1,)), ((), ()))
TN = (((0,), (0,)), ((), ()))


def dot1(a, b, dims=NN):
    return lax.dot_general(a.astype(BF), b.astype(BF), dims, preferred_element_type=F32)


def split(x):
    hi = x.astype(BF)
    return hi, (x - hi.astype(F32)).astype(BF)


def dot3(a, b, dims=NN):
    a1, a2 = split(a) if not isinstance(a, tuple) else a
    b1, b2 = split(b) if not isinstance(b, tuple) else b
    ka, kb = dims[0][0][0], dims[0][1][0]
    left = jnp.concatenate([a1, a2], axis=ka)
    n = b1.shape[1 - kb]
    if n == 128:
        right = jnp.concatenate([jnp.concatenate([b1, b2], axis=1 - kb), jnp.concatenate([b1, jnp.zeros_like(b1)], axis=1 - kb)], axis=kb)
        r = lax.dot_general(left, right, dims, preferred_element_type=F32)
        return r[:, :128] + r[:, 128:]
    r = lax.dot_general(left, jnp.concatenate([b1, b1], axis=kb), dims, preferred_element_type=F32)
    return r + lax.dot_general(a1, b2, dims, preferred_element_type=F32)


def dot3_old(a, b, dims=NN):
    a1, a2 = split(a) if not isinstance(a, tuple) else a
    b1, b2 = split(b) if not isinstance(b, tuple) else b
    d = functools.partial(lax.dot_general, dimension_numbers=dims, preferred_element_type=F32)
    return d(a1, b1) + (d(a1, b2) + d(a2, b1))


def block_masks():
    r = lax.broadcasted_iota(jnp.int32, (C, C), 0)
    c = lax.broadcasted_iota(jnp.int32, (C, C), 1)
    return r, c


def invert(systems, dot):
    r, c = block_masks()
    eye = (r == c).astype(F32)
    x = r ^ c
    lows = [low.astype(BF) for low in systems]
    out = [eye - jnp.where((x == 1), low, 0.0) for low in systems]
    size = 2
    while size < C:
        here = (x >= size) & (x < 2 * size)
        short = [t.astype(BF) for t in out]
        mids = [dot1(jnp.where(here, low, 0.0).astype(BF), t) for low, t in zip(lows, short)]
        out = [t - dot1(b, m) for t, b, m in zip(out, short, mids)]
        size *= 2
    splits = [split(t) for t in out]
    errors = [eye - t - dot(low, p) for low, t, p in zip(systems, out, splits)]
    return [t + dot1(p[0], e) for t, p, e in zip(out, splits, errors)]


def sigmoid(x):
    return 1.0 / (1.0 + jnp.exp(-x))


def taps_down(ext, rows, j):
    return lax.slice_in_dim(ext, 8 - j, 8 - j + rows, axis=0)


def row_sum(x):
    return jnp.dot(x.astype(BF), jnp.ones((HEAD, HEAD), BF), preferred_element_type=F32)


def head_norm(x):
    return x * lax.rsqrt(row_sum(x * x) + 1e-6)


def segment_parts(seg_s, cols_ref, segr_ref, first, sl):
    prev = jnp.where(first > 0, seg_s[jnp.maximum(first - 1, 0)], -1)
    last = seg_s[first + C - 1]
    segc = cols_ref[sl, 4:5]
    same = segc == segr_ref[0:1, sl]
    lead = (segc == prev.astype(F32)).astype(F32)
    trail = (segc == last.astype(F32)).astype(F32)
    return same, lead, trail, (prev == last).astype(F32)


def fwd_kernel(heads, cb, base, seg_s, x_ref, wide_ref, again_ref, cols_ref, segr_ref, taps_ref, gain_ref, tail_in, state_in,
               mixed_ref, kept_ref, na_ref, pre_ref, conv_ref, o_ref, t_ref, a_ref, p_ref, n_ref, z_ref, s_ref, u_ref, g_ref,
               tail, state, line):
    step = pl.program_id(0)
    width = heads * HEAD
    rows = cb * C
    taps = taps_ref.shape[1]

    @pl.when(step == 0)
    def _():
        tail[...] = jnp.zeros_like(tail) if tail_in is None else tail_in[...]
        state[...] = jnp.zeros_like(state) if state_in is None else state_in[...]

    r, c = block_masks()
    x = x_ref[...].astype(F32)
    na = (x * lax.rsqrt(jnp.mean(x * x, axis=-1, keepdims=True) + 1e-6) * again_ref[0:1, :]).astype(BF)
    na_ref[...] = na
    pre_ref[...] = jnp.dot(na, wide_ref[...], preferred_element_type=F32)
    tap = lambda j: jnp.concatenate([taps_ref[i, j:j + 1, :] for i in range(3)], axis=1)
    cur = pre_ref[:, :3 * width]
    line[:8, :] = tail[...]
    line[8:, :] = cur
    tot = cur * tap(0)
    for j in range(1, taps):
        tot = tot + line[8 - j:8 - j + rows, :] * tap(j) * cols_ref[:, j - 1:j]
    tail[...] = line[rows:, :]
    conv_ref[...] = tot
    tot = tot * sigmoid(tot)
    parts = [tot[:, i * width:(i + 1) * width] for i in range(3)]
    eye = (r == c).astype(F32)
    items = []
    for b in range(cb):
        sl = slice(b * C, (b + 1) * C)
        same, lead, trail, keep = segment_parts(seg_s, cols_ref, segr_ref, ((base + step) * cb + b) * C, sl)
        for h in range(heads):
            hs = slice(h * HEAD, (h + 1) * HEAD)
            q, k, v = (part[sl, hs] for part in parts)
            beta = sigmoid(pre_ref[sl, 3 * width + h:3 * width + h + 1]) * cols_ref[sl, 3:4]
            items.append(dict(b=b, h=h, q=head_norm(q), k=head_norm(k), v=v, beta=beta, same=same, lead=lead,
                              trail=trail, keep=keep, sl=sl, hs=hs))
    for it in items:
        it["kk"] = split(it["k"])
        p = jnp.where(it["same"] & (r > c), dot3(it["kk"], it["kk"], NT), 0.0)
        it["p"] = p
        it["low"] = p * it["beta"]
        it["a"] = jnp.where(it["same"] & (r >= c), dot3(it["q"], it["kk"], NT), 0.0)
    inv = invert([it["low"] for it in items], dot3)
    for it, t in zip(items, inv):
        rhs = jnp.concatenate([it["beta"] * it["v"], (it["beta"] * it["lead"]) * it["k"]], axis=1)
        tw = dot3(t, rhs)
        tws = split(tw)
        aw = dot3(it["a"], tws)
        bz = dot3(it["trail"] * it["k"], tws, TN)
        it["tv"], it["w"] = tw[:, :HEAD], tw[:, HEAD:]
        it["o0"], it["n"] = aw[:, :HEAD], it["lead"] * it["q"] - aw[:, HEAD:]
        it["bk"], it["z"] = bz[:, :HEAD], it["keep"] * eye - bz[:, HEAD:]
        it["t"] = t
    for it in items:
        b, h = it["b"], it["h"]
        s = state[h]
        ss = split(s)
        u = it["tv"] - dot3(it["w"], ss)
        o = it["o0"] + dot3(it["n"], ss)
        g = it["v"] - it["lead"] * dot3(it["kk"], ss)
        state[h] = it["bk"] + dot3(it["z"], ss)
        s_ref[b, h] = s
        u_ref[b, h] = u
        g_ref[b, h] = g
        t_ref[b, h] = it["t"]
        a_ref[b, h] = it["a"]
        p_ref[b, h] = it["p"]
        n_ref[b, h] = it["n"]
        z_ref[b, h] = it["z"]
        o_ref[it["sl"], it["hs"]] = o
        mixed = (o * lax.rsqrt(row_sum(o * o) * (1.0 / HEAD) + 1e-5) * gain_ref[0:1, :]).astype(BF)
        mixed_ref[it["sl"], it["hs"]] = mixed
        kept_ref[it["sl"], it["hs"]] = mixed


def stage_bits(n):
    bits = [1 << i for i in range(n.bit_length() - 1)]
    return bits, [bits[1], bits[0]] + bits[2:]


def bwd_kernel(heads, cb, n_f, shard, seg_s, ga0_ref, ga0c_ref, ga1_ref, ga1c_ref, mix_ref, na_ref, out_ref, wide_ref, x_ref, dffn0_ref, dffn1_ref,
               pre_ref, conv_ref, o_ref, cols_ref, segr_ref, taps_ref, gain_ref,
               t_ref, a_ref, p_ref, n_ref, z_ref, s_ref, u_ref, g_ref,
               away1_ref, keep1_ref, away2_ref, keep2_ref, sna_ref, kna_ref, gains_ref, small_ref,
               head_rows, dstate, acc, dpre):
    step = pl.program_id(0)
    steps = pl.num_programs(0)
    width = heads * HEAD
    rows = cb * C
    taps = taps_ref.shape[1]
    back = steps - 1 - step
    core = lax.axis_index("tensor") % 2

    @pl.when(step == 0)
    def _():
        head_rows[...] = jnp.zeros_like(head_rows)
        dstate[...] = jnp.zeros_like(dstate)
        acc[...] = jnp.zeros_like(acc)
        gains_ref[...] = jnp.zeros_like(gains_ref)
        gains_ref[6:7, :] = dffn0_ref[...] + dffn1_ref[...]
        small_ref[...] = jnp.zeros_like(small_ref)

    r, c = block_masks()
    dcs = [[[None] * heads for _ in range(cb)] for _ in range(3)]
    dgain = jnp.zeros((1, HEAD), F32)
    dlog = [None] * cb
    ga = jnp.where(back % 2 == core, jnp.where(back >= 2, ga1_ref[...], ga0_ref[...]),
                   jnp.where(back >= 2, ga1c_ref[...], ga0c_ref[...]))
    dmix = jnp.dot(ga, out_ref[...], preferred_element_type=F32)
    acc[:, 3 * width:4 * width] += lax.dot_general(ga, mix_ref[...], TN, preferred_element_type=F32)
    for b in reversed(range(cb)):
        sl = slice(b * C, (b + 1) * C)
        same, lead, trail, keep = segment_parts(seg_s, cols_ref, segr_ref, (back * cb + b) * C, sl)
        lane = lax.broadcasted_iota(jnp.int32, (C, HEAD), 1)
        dl = jnp.zeros((C, HEAD), F32)
        for h in range(heads):
            hs = slice(h * HEAD, (h + 1) * HEAD)
            cq, ck, cv = (conv_ref[sl, i * width + h * HEAD:i * width + (h + 1) * HEAD] for i in range(3))
            gq, gk, gv = sigmoid(cq), sigmoid(ck), sigmoid(cv)
            q, k = cq * gq, ck * gk
            rq = lax.rsqrt(jnp.sum(q * q, axis=-1, keepdims=True) + 1e-6)
            rk = lax.rsqrt(jnp.sum(k * k, axis=-1, keepdims=True) + 1e-6)
            q, k = q * rq, k * rk
            gb = sigmoid(pre_ref[sl, 3 * width + h:3 * width + h + 1])
            pad = cols_ref[sl, 3:4]
            beta = gb * pad
            o = o_ref[sl, hs]
            dm = dmix[sl, hs]
            ro = lax.rsqrt(jnp.mean(o * o, axis=-1, keepdims=True) + 1e-5)
            oh = o * ro
            dgain = dgain + jnp.sum(dm * oh, axis=0, keepdims=True)
            du0 = dm * gain_ref[0:1, :]
            do = ro * (du0 - oh * jnp.mean(du0 * oh, axis=-1, keepdims=True))
            ds1 = dstate[h]
            u = u_ref[b, h]
            s = s_ref[b, h]
            a = a_ref[b, h]
            p = p_ref[b, h]
            ks = split(k)
            ds1s = split(ds1)
            dos = split(do)
            us = split(u)
            dstate[h] = dot3(z_ref[b, h], ds1s, TN) + dot3(n_ref[b, h], dos, TN)
            du = dot3(a, dos, TN) + trail * dot3(ks, ds1s)
            dr = dot3(t_ref[b, h], du, TN)
            drs = split(dr)
            ss = split(s)
            dlow = jnp.where(same & (r > c), -dot3(drs, us, NT), 0.0)
            da = jnp.where(same & (r >= c), dot3(dos, us, NT), 0.0)
            dv = beta * dr
            dbeta = jnp.sum(dr * g_ref[b, h] , axis=-1, keepdims=True) + jnp.sum(dlow * p, axis=-1, keepdims=True)
            dp = split(beta * dlow)
            das = split(da)
            dq = lead * dot3(dos, ss, NT) + dot3(das, ks)
            dk = (dot3(das, q, TN) + trail * dot3(us, ds1s, NT) - (beta * lead) * dot3(drs, ss, NT)
                  + dot3(dp, ks) + dot3(dp, ks, TN))
            dsq = rq * (dq - q * jnp.sum(q * dq, axis=-1, keepdims=True))
            dsk = rk * (dk - k * jnp.sum(k * dk, axis=-1, keepdims=True))
            dcs[0][b][h] = dsq * gq * (1.0 + cq * (1.0 - gq))
            dcs[1][b][h] = dsk * gk * (1.0 + ck * (1.0 - gk))
            dcs[2][b][h] = dv * gv * (1.0 + cv * (1.0 - gv))
            dl = jnp.where(lane == h, dbeta * pad * gb * (1.0 - gb), dl)
        dlog[b] = dl
    gains_ref[7:8, :HEAD] += dgain
    for b in range(cb):
        dpre[b * C:(b + 1) * C, 3 * width:] = dlog[b].astype(BF)
    for i in range(3):
        dc = jnp.concatenate([jnp.concatenate(dcs[i][b], axis=1) for b in range(cb)], axis=0)
        pre = pre_ref[:, i * width:(i + 1) * width]
        tot = dc * taps_ref[i, 0:1, :]
        grads = [jnp.sum(dc * pre, axis=0, keepdims=True)]
        for j in range(1, taps):
            e = dc * cols_ref[:, j - 1:j]
            ext = jnp.concatenate([e, head_rows[j - 1, :, i * width:(i + 1) * width]], axis=0)
            head_rows[j - 1, :, i * width:(i + 1) * width] = e[:8]
            e = lax.slice_in_dim(ext, j, j + rows, axis=0)
            tot = tot + e * taps_ref[i, j:j + 1, :]
            grads.append(jnp.sum(e * pre, axis=0, keepdims=True))
        dpre[:, i * width:(i + 1) * width] = tot.astype(BF)
        small_ref[i:i + 1, :taps * width] += jnp.concatenate(grads, axis=1)
    low = dpre[...]
    acc[:, :3 * width] += lax.dot_general(na_ref[...], low[:, :3 * width], TN, preferred_element_type=F32)
    acc[:, 4 * width:] += lax.dot_general(na_ref[...], low[:, 3 * width:], TN, preferred_element_type=F32)
    dna = lax.dot_general(low, wide_ref[...], NT, preferred_element_type=F32)
    x = x_ref[...].astype(F32)
    gains_ref[5:6, :] += jnp.sum(dna * (x * lax.rsqrt(jnp.mean(x * x, axis=-1, keepdims=True) + 1e-6)), axis=0, keepdims=True)

    @pl.when(back % 2 == core)
    def _():
        kna_ref[back // 2] = dna

    @pl.when(back % 2 != core)
    def _():
        sna_ref[back // 2] = dna.astype(BF)

    @pl.when(step == steps - 1)
    def _():
        small_ref[3:3 + heads, :] = acc[:, 4 * width:].T[:heads, :]
        me = lax.axis_index("fsdp")
        first, second = stage_bits(n_f)
        half = 2 * width
        for ref, other, bit, lanes in ((away1_ref, keep1_ref, first[0], slice(0, half)), (away2_ref, keep2_ref, second[0], slice(half, 2 * half))):
            mine = (me // bit) % 2
            for j in range(n_f // 2):
                low_bits = j % bit
                there = (j - low_bits) * 2 + low_bits
                ref[j] = acc[pl.ds(pl.multiple_of((there + (1 - mine) * bit) * shard, 16), shard), lanes].astype(BF)
                other[j] = acc[pl.ds(pl.multiple_of((there + mine * bit) * shard, 16), shard), lanes].astype(other.dtype)


def whole(shape):
    return pl.BlockSpec(shape, lambda i, *_: (0,) * len(shape), pipeline_mode=pl.Buffered(1))


def shaped(shape, dtype=F32):
    return jax.ShapeDtypeStruct(shape, dtype)


def params(limit=60):
    return pltpu.CompilerParams(dimension_semantics=("arbitrary",), vmem_limit_bytes=limit * 2**20)


COST = pl.CostEstimate(flops=10**10, bytes_accessed=10**7, transcendentals=0)
TINY = pl.CostEstimate(flops=1, bytes_accessed=1, transcendentals=0)


def fwd_call_kernel(heads, cb, base, n_old, *refs):
    ins, rest = ((*refs[:8], None, None), refs[8:]) if n_old == 0 else (refs[:10], refs[10 + n_old:])
    outs, tail_out, state_out, tail, state, line = rest[:14], rest[14], rest[15], rest[16], rest[17], rest[18]
    fwd_kernel(heads, cb, base, *ins, *outs, tail, state, line)

    @pl.when(pl.program_id(0) == pl.num_programs(0) - 1)
    def _():
        tail_out[...] = tail[...]
        state_out[...] = state[...]


def mixer_fwd(part, parts, x, wide, again, cols, segr, seg, taps, gain, tail, state, old, cb=4):
    n, d = x.shape
    width = taps.shape[2]
    heads = width // HEAD
    wide_cols = 3 * width + HEAD
    rows = cb * C
    steps = n // parts // rows
    base = part * steps
    sq = shaped((n // C, heads, C, HEAD))
    sqspec = pl.BlockSpec((cb, heads, C, HEAD), lambda i, s: (i + base, 0, 0, 0))
    here = lambda w: pl.BlockSpec((rows, w), lambda i, s: (i + base, 0))
    ins = [x, wide, again, cols, segr, taps, gain] + ([tail, state] if old else [])
    tail, state = shaped((8, 3 * width)), shaped((heads, HEAD, HEAD))
    kept = [shaped((n, width), BF), shaped((n, d), BF), shaped((n, wide_cols)), shaped((n, 3 * width)), shaped((n, width))] + [sq] * 8
    return pl.pallas_call(
        functools.partial(fwd_call_kernel, heads, cb, base, len(old)),
        grid_spec=pltpu.PrefetchScalarGridSpec(
            num_scalar_prefetch=1, grid=(steps,),
            in_specs=[here(d), whole((d, wide_cols)), whole((1, d)), here(cols.shape[1]),
                      pl.BlockSpec((1, rows), lambda i, s: (0, i + base)),
                      whole(taps.shape), whole((1, HEAD))] + ([whole(tail.shape), whole(state.shape)] if old else [])
            + [pl.BlockSpec(memory_space=pl.ANY)] * len(old),
            out_specs=[pl.BlockSpec((rows, width), lambda i, s: (i, 0)), here(width), here(d), here(wide_cols), here(3 * width), here(width)]
            + [sqspec] * 8 + [whole(tail.shape), whole(state.shape)],
            scratch_shapes=[pltpu.VMEM(tail.shape, F32), pltpu.VMEM(state.shape, F32), pltpu.VMEM((rows + 8, 3 * width), F32)]),
        out_shape=[shaped((n // parts, width), BF)] + kept + [shaped(tail.shape), shaped(state.shape)],
        input_output_aliases={1 + len(ins) + i: 1 + i for i in range(len(old))},
        compiler_params=params(),
        cost_estimate=COST,
        name="mixer_fwd",
    )(seg, *ins, *old)


def mixer_bwd(n_f, shard, ga, out, wide, x, dffn, cols, segr, seg, taps, gain, kept, cb=2):
    mix, na, pre, conv, o, *rest = kept
    n, wide_cols = pre.shape
    d = x.shape[1]
    width = taps.shape[2]
    heads = width // HEAD
    rows = cb * C
    steps = n // rows
    ntap = taps.shape[1]
    sqspec = pl.BlockSpec((cb, heads, C, HEAD), lambda i, s: (steps - 1 - i, 0, 0, 0))
    row = lambda w: pl.BlockSpec((rows, w), lambda i, s: (steps - 1 - i, 0))
    outs = [shaped((n_f // 2, shard, 2 * width), BF)] * 4 + [
            shaped((2, rows, d), BF), shaped((2, rows, d)), shaped((8, d)), shaped((8, d))]
    return pl.pallas_call(
        functools.partial(bwd_kernel, heads, cb, n_f, shard),
        grid_spec=pltpu.PrefetchScalarGridSpec(
            num_scalar_prefetch=1, grid=(steps,),
            in_specs=[whole((rows, d))] * 4 + [row(width), row(d), whole(out.shape), whole((d, wide_cols)), row(d), whole((1, d)), whole((1, d)),
                      row(wide_cols), row(3 * width), row(width),
                      row(cols.shape[1]), pl.BlockSpec((1, rows), lambda i, s: (0, steps - 1 - i)),
                      whole(taps.shape), whole((1, HEAD))] + [sqspec] * 8,
            out_specs=[whole(v.shape) for v in outs],
            scratch_shapes=[pltpu.VMEM((ntap - 1, 8, 3 * width), F32), pltpu.VMEM((heads, HEAD, HEAD), F32),
                            pltpu.VMEM((d, 4 * width + HEAD), F32), pltpu.VMEM((rows, wide_cols), BF)]),
        out_shape=outs,
        compiler_params=params(),
        cost_estimate=COST,
        name="mixer_bwd",
    )(seg, *ga, mix, na, out, wide, x, *dffn, pre, conv, o, cols, segr, taps, gain, *rest)


def fold_kernel(n_f, stage, k1_ref, g1_ref, k2_ref, g2_ref, a1_out, k1_out, a2_out, k2_out):
    me = lax.axis_index("fsdp")
    for order, keep, got, away_out, keep_out in ((0, k1_ref, g1_ref, a1_out, k1_out), (1, k2_ref, g2_ref, a2_out, k2_out)):
        bits = stage_bits(n_f)[order]
        bit = bits[stage]
        left = sorted(b for b in bits[stage:])
        place = 1 << left.index(bit)
        mine = (me // bit) % 2
        for j in range(keep.shape[0] // 2):
            low = j % place
            there = (j - low) * 2 + low
            theirs = there + (1 - mine) * place
            away_out[j] = (keep[theirs].astype(F32) + got[theirs].astype(F32)).astype(BF)
            ours = there + mine * place
            keep_out[j] = (keep[ours].astype(F32) + got[ours].astype(F32)).astype(keep_out.dtype)


def fold(n_f, stage, k1, g1, k2, g2):
    m, shard, w = k1.shape
    outs = [shaped((m // 2, shard, w), BF)] * 4
    return pl.pallas_call(
        functools.partial(fold_kernel, n_f, stage),
        out_shape=outs,
        compiler_params=pltpu.CompilerParams(vmem_limit_bytes=60 * 2**20),
        cost_estimate=TINY,
        name="fold",
    )(k1, g1, k2, g2)


def finish_kernel(heads, ntap, k1_ref, g1_ref, k2_ref, g2_ref, s_ref, *refs):
    got, (qkv_ref, out_ref, taps_ref, beta_ref, attn_ref, ffn_ref, head_ref, hold) = refs[:-9], refs[-8:]
    width = qkv_ref.shape[2]
    shard = qkv_ref.shape[1]
    a = k1_ref[0].astype(F32) + g1_ref[0].astype(F32)
    b = k2_ref[0].astype(F32) + g2_ref[0].astype(F32)
    qkv_ref[0] = a[:, :width]
    qkv_ref[1] = a[:, width:]
    qkv_ref[2] = b[:, :width]
    out_ref[...] = b[:, width:].T
    small = s_ref[...]
    for g in got:
        small = small + g[...]
    width = taps_ref.shape[2]
    for i in range(3):
        for k in range(ntap):
            taps_ref[i, k:k + 1, :] = small[i:i + 1, k * width:(k + 1) * width]
    attn_ref[...] = small[5:6]
    ffn_ref[...] = small[6:7]
    head_ref[...] = small[7:8, :HEAD]
    if shard == 128:
        hold[...] = small
        me = lax.axis_index("fsdp")
        beta_ref[...] = hold[3:3 + heads, pl.ds(pl.multiple_of(me * shard, 128), shard)]
    else:
        beta_ref[...] = small[3:3 + heads]


def finish(heads, ntap, k1, g1, k2, g2, small, got, wait_for):
    m, shard, w = k1.shape
    d = small.shape[1]
    return pl.pallas_call(
        functools.partial(finish_kernel, heads, ntap),
        in_specs=[pl.BlockSpec(memory_space=pltpu.VMEM)] * (5 + len(got)) + [pl.BlockSpec(memory_space=pl.ANY)],
        out_shape=[shaped((3, shard, w // 2)), shaped((w // 2, shard)), shaped((3, ntap, w // 2)),
                   shaped((heads, 128 if shard == 128 else d)), shaped((1, d)), shaped((1, d)), shaped((1, HEAD))],
        scratch_shapes=[pltpu.VMEM((8, d), F32)],
        compiler_params=pltpu.CompilerParams(vmem_limit_bytes=60 * 2**20),
        cost_estimate=TINY,
        name="finish",
    )(k1, g1, k2, g2, small, *got, wait_for)


def ffn_kernel(ff, *refs):
    m, out, (x_ref, w_ref, gf_ref, gain_ref), rest = refs[:4], refs[4:8], refs[8:12], refs[12:]
    mid_ref, nf_ref, hid_ref, dgu_ref, keep_ref, send_ref, dgain_ref, hold = rest
    rows = keep_ref.shape[0]
    core = lax.axis_index("tensor") % 2
    mid = x_ref[...].astype(F32)
    for k in range(4):
        mid = mid + lax.dot_general(m[k][...], out[k][...], NT, preferred_element_type=F32)
    hold[...] = mid
    unit = mid * lax.rsqrt(jnp.mean(mid * mid, axis=-1, keepdims=True) + 1e-6)
    nf = (unit * gain_ref[0:1, :]).astype(BF)
    nf_ref[...] = nf
    mid_ref[...] = hold[pl.ds(pl.multiple_of(core * rows, 16), rows), :]
    gate = lax.dot_general(w_ref[:ff, :], nf, NT, preferred_element_type=F32)
    up = lax.dot_general(w_ref[ff:2 * ff, :], nf, NT, preferred_element_type=F32)
    dh = lax.dot_general(w_ref[2 * ff:, :], gf_ref[...], NT, preferred_element_type=F32)
    sig = sigmoid(gate)
    act = gate * sig
    hid_ref[...] = (act * up).astype(BF)
    dgu_ref[:ff, :] = (dh * up * sig * (1.0 + gate * (1.0 - sig))).astype(BF)
    dgu_ref[ff:, :] = (dh * act).astype(BF)
    dnf = lax.dot_general(dgu_ref[...], w_ref[:2 * ff, :], TN, preferred_element_type=F32)
    dgain_ref[...] = jnp.sum(dnf * unit, axis=0, keepdims=True)
    hold[...] = dnf
    keep_ref[...] = hold[pl.ds(pl.multiple_of(core * rows, 16), rows), :]
    send_ref[...] = hold[pl.ds(pl.multiple_of((1 - core) * rows, 16), rows), :].astype(BF)


def ffn(part, m, out, x, weights, gf, gain):
    n, width = m[0].shape
    d = x.shape[1]
    ff = weights.shape[0] // 3
    here = pl.BlockSpec((n, d), lambda i: (part, 0))
    outs = [shaped((n // 2, d)), shaped((n, d), BF), shaped((ff, n), BF), shaped((2 * ff, n), BF),
            shaped((n // 2, d)), shaped((n // 2, d), BF), shaped((1, d))]
    return pl.pallas_call(
        functools.partial(ffn_kernel, ff),
        grid=(1,),
        in_specs=[whole(v.shape) for v in (*m, *out)] + [here, whole(weights.shape), here, whole((1, d))],
        out_specs=[whole(v.shape) for v in outs],
        out_shape=outs,
        scratch_shapes=[pltpu.VMEM((n, d), F32)],
        compiler_params=params(),
        cost_estimate=COST,
        name="ffn",
    )(*m, *out, x, weights, gf, gain)


def grad_kernel(part, n, *refs):
    lows, others, (mid_ref, cot_ref, coty_ref, gain_ref, grad_ref, low_out) = refs[:n], refs[n:2 * n], refs[2 * n:]
    chip = lax.axis_index("tensor") // 2
    mid = mid_ref[...]
    factor = lax.rsqrt(jnp.mean(mid * mid, axis=-1, keepdims=True) + 1e-6)
    d_nf = jnp.concatenate([a[...].astype(F32) + b[...].astype(F32) for a, b in zip(lows, others)], axis=0)
    u = d_nf * gain_ref[0:1, :]
    cot = jnp.where(chip == part, cot_ref[...], coty_ref[...]).astype(F32)
    grad = cot + factor * u - mid * (factor * factor * factor) * jnp.mean(u * mid, axis=-1, keepdims=True)
    grad_ref[...] = grad
    low_out[...] = grad.astype(BF)


def grad_rows(part, lows, others, mid, cot, cot_y, gain):
    return pl.pallas_call(
        functools.partial(grad_kernel, part, len(lows)),
        out_shape=[shaped(mid.shape), shaped(mid.shape, BF)],
        compiler_params=pltpu.CompilerParams(vmem_limit_bytes=24 * 2**20),
        cost_estimate=TINY,
        name="grad_rows",
    )(*lows, *others, mid, cot, cot_y, gain)


def down_kernel(hid0_ref, hid1_ref, w_ref, send_ref, keep_ref, hold):
    core = lax.axis_index("tensor") % 2
    rows = send_ref.shape[1]
    for i, hid in enumerate((hid0_ref, hid1_ref)):
        hold[...] = lax.dot_general(hid[...], w_ref[...], TN, preferred_element_type=F32)
        keep_ref[i] = hold[pl.ds(pl.multiple_of(core * rows, 16), rows), :]
        send_ref[i] = hold[pl.ds(pl.multiple_of((1 - core) * rows, 16), rows), :].astype(BF)


def down(hid0, hid1, weights, wait_for):
    ff, n = hid0.shape
    d = weights.shape[1]
    outs = [shaped((2, n // 2, d), BF), shaped((2, n // 2, d))]

    def body(*refs):
        down_kernel(*refs[:3], *refs[3 + len(wait_for):])

    return pl.pallas_call(
        body,
        grid=(1,),
        in_specs=[whole(hid0.shape)] * 2 + [pl.BlockSpec((ff, d), lambda i: (2, 0))] + [pl.BlockSpec(memory_space=pl.ANY)] * len(wait_for),
        out_specs=[whole(v.shape) for v in outs],
        out_shape=outs,
        scratch_shapes=[pltpu.VMEM((n, d), F32)],
        compiler_params=params(),
        cost_estimate=TINY,
        name="down",
    )(hid0, hid1, weights, *wait_for)


def ffn_grads_kernel(ff, parts, *refs):
    gf_ref, o_ref = refs[3 * parts], refs[-1]
    n = refs[0].shape[1]
    up = down = None
    for i in range(parts):
        dgu, hid, nf = refs[3 * i:3 * i + 3]
        a = jnp.dot(dgu[...], nf[...], preferred_element_type=F32)
        b = jnp.dot(hid[...], gf_ref[i * n:(i + 1) * n, :], preferred_element_type=F32)
        up = a if up is None else up + a
        down = b if down is None else down + b
    for k in range(o_ref.shape[0]):
        lanes = slice(k * 128, (k + 1) * 128)
        o_ref[k, :2 * ff, :] = up[:, lanes].astype(BF)
        o_ref[k, 2 * ff:, :] = down[:, lanes].astype(BF)


def ffn_grads(pieces, gf, wait_for, step=256):
    ff = pieces[0][1].shape[0]
    n, d = gf.shape
    flat, specs = [], []
    for dgu, hid, nf in pieces:
        flat += [dgu, hid, nf]
        specs += [whole(dgu.shape), whole(hid.shape), pl.BlockSpec((nf.shape[0], step), lambda i: (0, i))]
    return pl.pallas_call(
        functools.partial(ffn_grads_kernel, ff, len(pieces)),
        grid=(d // step,),
        in_specs=specs + [pl.BlockSpec((n, step), lambda i: (0, i))] + [pl.BlockSpec(memory_space=pl.ANY)] * len(wait_for),
        out_specs=pl.BlockSpec((step // 128, 3 * ff, 128), lambda i: (i, 0, 0)),
        out_shape=shaped((d // 128, 3 * ff, 128), BF),
        compiler_params=params(),
        cost_estimate=pl.CostEstimate(flops=5 * 10**9, bytes_accessed=10**7, transcendentals=0),
        name="ffn_grads",
    )(*flat, gf, *wait_for)


def to_chips_kernel(keep, got, wait_for, mine_ref, away_ref):
    chip = lax.axis_index("tensor") // 2
    mine_ref[...] = keep[chip] + got[chip].astype(F32)
    away_ref[...] = (keep[1 - chip] + got[1 - chip].astype(F32)).astype(BF)


def to_chips(keep, got, wait_for):
    spec = pl.BlockSpec(memory_space=pltpu.VMEM)
    return pl.pallas_call(
        to_chips_kernel,
        in_specs=[spec] * 2 + [pl.BlockSpec(memory_space=pl.ANY)],
        out_shape=[shaped(keep.shape[1:]), shaped(keep.shape[1:], BF)],
        compiler_params=pltpu.CompilerParams(vmem_limit_bytes=60 * 2**20),
        cost_estimate=TINY,
        name="to_chips",
    )(keep, got, wait_for)


def last_kernel(g0, g1, na, na_y, x_ref, gain_ref, mid0, mid1, out, out_y, in_ref, block_ref):
    first = lax.axis_index("tensor") // 2 == 0
    x = x_ref[...].astype(F32)
    factor = lax.rsqrt(jnp.mean(x * x, axis=-1, keepdims=True) + 1e-6)
    u = (na[...] + na_y[...].astype(F32)) * gain_ref[0:1, :]
    in_ref[...] = jnp.where(first, g0[...], g1[...]) + (factor * u - x * (factor * factor * factor) * jnp.mean(u * x, axis=-1, keepdims=True))
    block_ref[...] = (jnp.where(first, mid0[...], mid1[...]) + out[...] + out_y[...].astype(F32)).astype(BF)


def last_rows(g0, g1, na, na_y, x, gain, mid0, mid1, out, out_y):
    return pl.pallas_call(
        last_kernel,
        out_shape=[shaped(g0.shape), shaped(g0.shape, BF)],
        compiler_params=pltpu.CompilerParams(vmem_limit_bytes=60 * 2**20),
        cost_estimate=TINY,
        name="last_rows",
    )(g0, g1, na, na_y, x, gain, mid0, mid1, out, out_y)


def ffn_cast_kernel(d_ref, expand_ref, down_ref):
    ff = down_ref.shape[0]
    expand_ref[0] = d_ref[:ff, :].astype(F32)
    expand_ref[1] = d_ref[ff:2 * ff, :].astype(F32)
    down_ref[...] = d_ref[2 * ff:, :].astype(F32)


def ffn_cast(d):
    ff, w = d.shape[0] // 3, d.shape[1]
    return pl.pallas_call(
        ffn_cast_kernel,
        out_shape=[shaped((2, ff, w)), shaped((ff, w))],
        compiler_params=pltpu.CompilerParams(vmem_limit_bytes=60 * 2**20),
        cost_estimate=TINY,
        name="ffn_cast",
    )(d)


def ffn_split_kernel(ff, parts, *refs):
    blocks, expand, away, keep = refs[-1], refs[-4], refs[-3], refs[-2]
    ffn_grads_kernel(ff, parts, *refs[:3 * parts + 1], blocks)
    me = lax.axis_index("fsdp")
    for k in range(blocks.shape[0]):
        expand[k] = blocks[k, :2 * ff, :]
        block = pl.program_id(0) * blocks.shape[0] + k

        @pl.when(block % 2 == me % 2)
        def _(k=k, block=block):
            keep[block // 2] = blocks[k, 2 * ff:, :]

        @pl.when(block % 2 != me % 2)
        def _(k=k, block=block):
            away[block // 2] = blocks[k, 2 * ff:, :]


def ffn_split_grads(pieces, gf, wait_for, step=256):
    ff = pieces[0][1].shape[0]
    n, d = gf.shape
    flat, specs = [], []
    for dgu, hid, nf in pieces:
        flat += [dgu, hid, nf]
        specs += [whole(dgu.shape), whole(hid.shape), pl.BlockSpec((nf.shape[0], step), lambda i: (0, i))]
    per = step // 128
    halves = shaped((d // 256, ff, 128), BF)
    return pl.pallas_call(
        functools.partial(ffn_split_kernel, ff, len(pieces)),
        grid=(d // step,),
        in_specs=specs + [pl.BlockSpec((n, step), lambda i: (0, i))] + [pl.BlockSpec(memory_space=pl.ANY)] * len(wait_for),
        out_specs=[pl.BlockSpec((per, 2 * ff, 128), lambda i: (i, 0, 0)), whole(halves.shape), whole(halves.shape)],
        out_shape=[shaped((d // 128, 2 * ff, 128), BF), halves, halves],
        scratch_shapes=[pltpu.VMEM((per, 3 * ff, 128), BF)],
        compiler_params=params(),
        cost_estimate=COST,
        name="ffn_grads",
    )(*flat, gf, *wait_for)


def halve_kernel(bit, k_ref, g_ref, wait_for, away, keep):
    mine = (lax.axis_index("fsdp") // bit) % 2
    count = k_ref.shape[0] // 2
    for j in range(count):
        ours, theirs = (2 * j + mine, 2 * j + 1 - mine) if bit == 2 else (mine, 1 - mine)
        away[j] = (k_ref[theirs].astype(F32) + g_ref[theirs].astype(F32)).astype(BF)
        keep[j] = (k_ref[ours].astype(F32) + g_ref[ours].astype(F32)).astype(BF)


def halve(bit, k, g, wait_for):
    m, ff, w = k.shape
    spec = pl.BlockSpec(memory_space=pltpu.VMEM)
    return pl.pallas_call(
        functools.partial(halve_kernel, bit),
        in_specs=[spec] * 2 + [pl.BlockSpec(memory_space=pl.ANY)],
        out_shape=[shaped((m // 2, ff, w), BF)] * 2,
        compiler_params=pltpu.CompilerParams(vmem_limit_bytes=60 * 2**20),
        cost_estimate=TINY,
        name="halve",
    )(k, g, wait_for)


def split_cast_kernel(d_ref, k_ref, g_ref, expand_ref, down_ref):
    ff = down_ref.shape[0]
    expand_ref[0] = d_ref[:ff, :].astype(F32)
    expand_ref[1] = d_ref[ff:, :].astype(F32)
    down_ref[...] = k_ref[0].astype(F32) + g_ref[0].astype(F32)


def split_cast(d, k, g):
    ff, w = d.shape[0] // 2, d.shape[1]
    return pl.pallas_call(
        split_cast_kernel,
        out_shape=[shaped((2, ff, w)), shaped((ff, w))],
        compiler_params=pltpu.CompilerParams(vmem_limit_bytes=60 * 2**20),
        cost_estimate=TINY,
        name="ffn_cast",
    )(d, k, g)


def pack_kernel(qkv_ref, beta_ref, out_ref, o_ref):
    width = qkv_ref.shape[2]
    n = o_ref.shape[0]
    for i in range(3):
        o_ref[:, i * width:(i + 1) * width] = qkv_ref[i]
    beta = beta_ref[...].astype(F32)
    heads = beta.shape[1]
    o_ref[:, 3 * width:3 * width + 128] = jnp.concatenate([beta, jnp.zeros((n, 128 - heads), F32)], axis=1).astype(BF)
    o_ref[:, 3 * width + 128:] = out_ref[...].astype(F32).T.astype(BF)


def pack(qkv, beta, out):
    n, width = qkv.shape[1:]
    return pl.pallas_call(
        pack_kernel,
        out_shape=shaped((n, 4 * width + 128), BF),
        compiler_params=pltpu.CompilerParams(vmem_limit_bytes=60 * 2**20),
        name="pack",
    )(qkv, beta, out)


def columns(seg, pad):
    n = seg.shape[0]
    cols = []
    for j in range(1, 4):
        before = jnp.concatenate([jnp.full((j,), -1, seg.dtype), seg[:n - j]])
        cols.append((before == seg).astype(F32))
    cols += [pad.astype(F32), seg.astype(F32)]
    cols += [jnp.zeros((n,), F32)] * 3
    return jnp.stack(cols, axis=1)


def hop(value, axis, bit):
    n = lax.axis_size(axis)
    return lax.ppermute(value, axis, [(i, i ^ bit) for i in range(n)])


def fence(*values):
    return lax.optimization_barrier(values)


def y_hop(value):
    return hop(value, "tensor", 2)


def core_hop(value):
    return hop(value, "tensor", 1)


def in_order(own, other_chip, pair):
    me = lax.axis_index("tensor")
    full = jnp.zeros((4,) + own.shape, own.dtype)
    for k, block in ((0, own), (2, other_chip), (1, pair[0]), (3, pair[1])):
        full = lax.dynamic_update_slice(full, block[None], (me ^ k,) + (0,) * own.ndim)
    return full.reshape((4 * own.shape[0],) + own.shape[1:])


class Ring:
    def __init__(self, value):
        n = lax.axis_size("fsdp")
        order = [i for i in range(0, n, 2)] + [i for i in reversed(range(1, n, 2))]
        me = lax.axis_index("fsdp")
        self.n = n
        self.me = jnp.where(me % 2 == 0, me // 2, n - 1 - me // 2)
        self.right = [(order[i], order[(i + 1) % n]) for i in range(n)]
        self.left = [(b, a) for a, b in self.right]
        self.rows = value.shape[0]
        self.full = jnp.zeros((n * self.rows,) + value.shape[1:], value.dtype)
        self.a = self.b = value
        self.k = 0
        self.put(value, 0, 0)

    def put(self, part, steps, start):
        place = lax.rem(self.me + steps + self.n, self.n)
        owner = jnp.where(place < self.n // 2, 2 * place, 2 * (self.n - 1 - place) + 1)
        self.full = lax.dynamic_update_slice(self.full, part, (owner * self.rows + start, 0))

    def step(self):
        self.k += 1
        k, half = self.k, self.rows // 2
        self.split = 2 * k == self.n and half % 16 == 0
        if self.split:
            self.a = lax.ppermute(self.a[:half], "fsdp", self.right)
            self.b = lax.ppermute(self.b[half:], "fsdp", self.left)
            return
        self.a = lax.ppermute(self.a, "fsdp", self.right)
        if 2 * k < self.n:
            self.b = lax.ppermute(self.b, "fsdp", self.left)

    def keep(self):
        self.put(self.a, -self.k, 0)
        if self.split or 2 * self.k < self.n:
            self.put(self.b, self.k, self.rows // 2 if self.split else 0)


def hop_sum(value, axis, bit):
    return value + hop(value, axis, bit)


def on_device(
    layer_input, segment_ids, pad_mask, attn_gain, ffn_gain, out_gain,
    qkv_weight, beta_weight, conv_weight, out_weight, expand_weight, down_weight, cotangent,
):
    n_f = lax.axis_size("fsdp")
    me_t = lax.axis_index("tensor")
    chip = me_t // 2
    rows, d_model = layer_input.shape
    width = qkv_weight.shape[3]
    heads = beta_weight.shape[2]
    ff = down_weight.shape[1]
    shard = qkv_weight.shape[2]
    taps = conv_weight[0]
    ntap = taps.shape[1]
    first_bits, second_bits = stage_bits(n_f)

    packed = pack(qkv_weight[0], beta_weight[0], out_weight[0])
    packed, expand_own, down_own = fence(packed, expand_weight[0], down_weight[0])
    ring = Ring(packed)
    ring.step()
    x_y = y_hop(layer_input)
    x_c = core_hop(layer_input)
    ffn_own = jnp.concatenate([expand_own[0].T, expand_own[1].T, down_own], axis=0)
    weights = lax.all_gather(ffn_own, "fsdp", axis=1, tiled=True)
    seg = segment_ids[0]
    cols = columns(seg, pad_mask[0])
    segr = seg.astype(F32)[None]
    ring.a, ring.b, x_y, x_c = fence(ring.a, ring.b, x_y, x_c)
    ring.keep()
    ring.step()
    x_cy = core_hop(x_y)
    c_y = y_hop(cotangent)
    c_c = core_hop(cotangent)
    ring.a, ring.b, x_cy, c_y = fence(ring.a, ring.b, x_cy, c_y)
    ring.keep()
    ring.step()
    c_cy = core_hop(c_y)
    x_full = in_order(layer_input, x_y, (x_c, x_cy))
    ring.a, ring.b, x_full, cols, c_cy = fence(ring.a, ring.b, x_full, cols, c_cy)
    ring.keep()
    g_f = in_order(cotangent, c_y, (c_c, c_cy))
    while 2 * ring.k < n_f:
        ring.step()
        ring.keep()
    wide, g_f = fence(ring.full, g_f)

    out_own = wide[:, 3 * width + HEAD:]
    tail = state = None

    def mix(i, tail, state, old):
        m, *kept, tail, state = mixer_fwd(i, 2, x_full, wide, attn_gain, cols, segr, seg, taps, out_gain, tail, state, old)
        return m, kept, tail, state

    ow_y = y_hop(out_own)
    ow_c = core_hop(out_own)
    m0, kept, tail, state = mix(0, tail, state, [])
    ow_y, ow_c, m0, tail, state = fence(ow_y, ow_c, m0, tail, state)
    m0_y = y_hop(m0)
    m0_c = core_hop(m0)
    ow_cy = core_hop(ow_y)
    m1, kept, tail, state = mix(1, tail, state, kept)
    m0_y, m0_c, ow_cy, m1 = fence(m0_y, m0_c, ow_cy, m1)

    def feed(i, *m):
        return ffn(i, m, (out_own, ow_y, ow_c, ow_cy), x_full, weights, g_f, ffn_gain)

    m1_y = y_hop(m1)
    m1_c = core_hop(m1)
    m0_cy = core_hop(m0_y)
    mid0, nf0, hid0, dgu0, keep0, send0, dgain0 = feed(0, m0, m0_y, m0_c, m0_cy)
    m1_y, m1_c, send0 = fence(m1_y, m1_c, send0)
    m1_cy = core_hop(m1_y)
    low0 = (keep0 + core_hop(send0).astype(F32)).astype(BF)
    m1_cy, low0 = fence(m1_cy, low0)
    low0_y = y_hop(low0)
    mid1, nf1, hid1, dgu1, keep1, send1, dgain1 = feed(1, m1, m1_y, m1_c, m1_cy)
    low0_y, send1 = fence(low0_y, send1)
    cut = rows // 2
    got1 = core_hop(send1)
    low1 = (keep1[:cut] + got1[:cut].astype(F32)).astype(BF)
    low1b = (keep1[cut:] + got1[cut:].astype(F32)).astype(BF)
    grad0, ga0 = grad_rows(0, [low0], [low0_y], mid0, cotangent, c_y, ffn_gain)
    low1, low1b, ga0 = fence(low1, low1b, ga0)
    low1_y, low1b_y = y_hop(low1), y_hop(low1b)
    ga0_c = core_hop(ga0)
    blocks = ffn_grads([(dgu0, hid0, nf0), (dgu1, hid1, nf1)], g_f, [low1])
    q = d_model // 128
    if q != n_f:
        blocks = blocks.reshape(q, 3 * ff, n_f // q, shard).transpose(0, 2, 1, 3).reshape(n_f, 3 * ff, shard)
    send_out, keep_out = down(hid0, hid1, weights, [blocks])
    low1_y, ga0_c, blocks = fence(low1_y, ga0_c, blocks)
    low1b_y, send_out, done_blocks = fence(low1b_y, send_out, blocks)
    d_ffn = lax.psum_scatter(blocks, "fsdp", scatter_dimension=0, tiled=False)
    grad1, ga1 = grad_rows(1, [low1, low1b], [low1_y, low1b_y], mid1, cotangent, c_y, ffn_gain)
    ga1_c = core_hop(ga1)
    ga1, ga1_c = fence(ga1, ga1_c)

    out_c = core_hop(send_out)
    made = mixer_bwd(
        n_f, shard, (ga0, ga0_c, ga1, ga1_c), out_own, wide, x_full, (dgain0, dgain1), cols, segr, seg, taps, out_gain, kept)
    away1, k1, away2, k2, send_na, keep_na, gains, small, out_c = fence(*made, out_c)

    g1 = hop(away1, "fsdp", first_bits[0])
    g2 = hop(away2, "fsdp", second_bits[0])
    na_c = core_hop(send_na)
    gains_got = [hop(gains, "tensor", k) for k in range(1, 4)]
    out, out_away = to_chips(keep_out, out_c, done_blocks)
    na, na_away = to_chips(keep_na, na_c, gains)
    g1, g2, na_away, out_away, *gains_got = fence(g1, g2, na_away, out_away, *gains_got)
    count = len(first_bits)
    small = small + gains + gains_got[0] + (gains_got[1] + gains_got[2])
    for stage in range(1, count):
        away1, k1, away2, k2 = fold(n_f, stage, k1, g1, k2, g2)
        if stage == 1:
            na_y, out_y = y_hop(na_away), y_hop(out_away)
        g1 = hop(away1, "fsdp", first_bits[stage])
        g2 = hop(away2, "fsdp", second_bits[stage])
        if stage < count - 1:
            small = hop_sum(small, "fsdp", first_bits[stage - 1])
            g1, g2, small, na_y = fence(g1, g2, small, na_y)
    if n_f == 8:
        got = [hop(small, "fsdp", k) for k in (2, 4, 6)]
    else:
        small = hop_sum(small, "fsdp", first_bits[count - 2])
        got = [hop(small, "fsdp", first_bits[count - 1])]
    input_grad, block_outs = last_rows(grad0, grad1, na, na_y, layer_input, attn_gain, mid0, mid1, out, out_y)
    block_outs = block_outs[None]
    expand_grad, down_grad = ffn_cast(d_ffn)
    qkv_grad, out_grad, conv_grad, beta_grad, attn_total, ffn_total, head_total = finish(heads, ntap, k1, g1, k2, g2, small, got, down_grad)
    if shard != 128:
        beta_grad = lax.dynamic_slice(beta_grad, (0, lax.axis_index("fsdp") * shard), (heads, shard))
    beta_grad = beta_grad.T
    expand_grad = expand_grad.transpose(0, 2, 1)
    return (
        block_outs, input_grad, attn_total, ffn_total, head_total, qkv_grad[None], beta_grad[None],
        conv_grad[None], out_grad[None], expand_grad[None], down_grad[None],
    )


def solution(mesh):
    in_specs = (
        P(("fsdp", "tensor"), None),
        P("fsdp", None),
        P("fsdp", None),
        P(),
        P(),
        P(),
        P(None, None, "fsdp", "tensor"),
        P(None, "fsdp", "tensor"),
        P(None, None, None, "tensor"),
        P(None, "tensor", "fsdp"),
        P(None, None, "fsdp", "tensor"),
        P(None, "tensor", "fsdp"),
        P(("fsdp", "tensor"), None),
    )
    out_specs = (
        P(None, ("fsdp", "tensor"), None),
        P(("fsdp", "tensor"), None),
        P(),
        P(),
        P(),
        P(None, None, "fsdp", "tensor"),
        P(None, "fsdp", "tensor"),
        P(None, None, None, "tensor"),
        P(None, "tensor", "fsdp"),
        P(None, None, "fsdp", "tensor"),
        P(None, "tensor", "fsdp"),
    )
    return jax.shard_map(
        on_device, mesh=mesh, in_specs=in_specs, out_specs=out_specs, check_vma=False
    )
```

```python
import functools
import jax
import jax.numpy as jnp
from jax import lax
from jax.experimental import pallas as pl
from jax.experimental.pallas import tpu as pltpu
from jax.sharding import PartitionSpec as P

HEAD = 128
C = 128
F32 = jnp.float32
BF = jnp.bfloat16

NN = (((1,), (0,)), ((), ()))
NT = (((1,), (1,)), ((), ()))
TN = (((0,), (0,)), ((), ()))


def dot1(a, b, dims=NN):
    return lax.dot_general(a.astype(BF), b.astype(BF), dims, preferred_element_type=F32)


def split(x):
    hi = x.astype(BF)
    return hi, (x - hi.astype(F32)).astype(BF)


def dot3(a, b, dims=NN):
    a1, a2 = split(a) if not isinstance(a, tuple) else a
    b1, b2 = split(b) if not isinstance(b, tuple) else b
    ka, kb = dims[0][0][0], dims[0][1][0]
    left = jnp.concatenate([a1, a2], axis=ka)
    n = b1.shape[1 - kb]
    if n == 128:
        right = jnp.concatenate([jnp.concatenate([b1, b2], axis=1 - kb), jnp.concatenate([b1, jnp.zeros_like(b1)], axis=1 - kb)], axis=kb)
        r = lax.dot_general(left, right, dims, preferred_element_type=F32)
        return r[:, :128] + r[:, 128:]
    r = lax.dot_general(left, jnp.concatenate([b1, b1], axis=kb), dims, preferred_element_type=F32)
    return r + lax.dot_general(a1, b2, dims, preferred_element_type=F32)


def dot3_old(a, b, dims=NN):
    a1, a2 = split(a) if not isinstance(a, tuple) else a
    b1, b2 = split(b) if not isinstance(b, tuple) else b
    d = functools.partial(lax.dot_general, dimension_numbers=dims, preferred_element_type=F32)
    return d(a1, b1) + (d(a1, b2) + d(a2, b1))


def block_masks():
    r = lax.broadcasted_iota(jnp.int32, (C, C), 0)
    c = lax.broadcasted_iota(jnp.int32, (C, C), 1)
    return r, c


def invert(systems, dot):
    r, c = block_masks()
    eye = (r == c).astype(F32)
    x = r ^ c
    lows = [low.astype(BF) for low in systems]
    out = [eye - jnp.where((x == 1), low, 0.0) for low in systems]
    size = 2
    while size < C:
        here = (x >= size) & (x < 2 * size)
        short = [t.astype(BF) for t in out]
        mids = [dot1(jnp.where(here, low, 0.0).astype(BF), t) for low, t in zip(lows, short)]
        out = [t - dot1(b, m) for t, b, m in zip(out, short, mids)]
        size *= 2
    splits = [split(t) for t in out]
    errors = [eye - t - dot(low, p) for low, t, p in zip(systems, out, splits)]
    return [t + dot1(p[0], e) for t, p, e in zip(out, splits, errors)]


def sigmoid(x):
    return 1.0 / (1.0 + jnp.exp(-x))


def taps_down(ext, rows, j):
    return lax.slice_in_dim(ext, 8 - j, 8 - j + rows, axis=0)


def row_sum(x):
    return jnp.dot(x.astype(BF), jnp.ones((HEAD, HEAD), BF), preferred_element_type=F32)


def head_norm(x):
    return x * lax.rsqrt(row_sum(x * x) + 1e-6)


def segment_parts(seg_s, cols_ref, segr_ref, first, sl):
    prev = jnp.where(first > 0, seg_s[jnp.maximum(first - 1, 0)], -1)
    last = seg_s[first + C - 1]
    segc = cols_ref[sl, 4:5]
    same = segc == segr_ref[0:1, sl]
    lead = (segc == prev.astype(F32)).astype(F32)
    trail = (segc == last.astype(F32)).astype(F32)
    return same, lead, trail, (prev == last).astype(F32)


def fwd_kernel(heads, cb, base, seg_s, x_ref, wide_ref, again_ref, cols_ref, segr_ref, taps_ref, gain_ref, tail_in, state_in,
               mixed_ref, kept_ref, na_ref, pre_ref, conv_ref, o_ref, t_ref, a_ref, p_ref, n_ref, z_ref, s_ref, u_ref, g_ref,
               tail, state, line):
    step = pl.program_id(0)
    width = heads * HEAD
    rows = cb * C
    taps = taps_ref.shape[1]

    @pl.when(step == 0)
    def _():
        tail[...] = jnp.zeros_like(tail) if tail_in is None else tail_in[...]
        state[...] = jnp.zeros_like(state) if state_in is None else state_in[...]

    r, c = block_masks()
    x = x_ref[...].astype(F32)
    na = (x * lax.rsqrt(jnp.mean(x * x, axis=-1, keepdims=True) + 1e-6) * again_ref[0:1, :]).astype(BF)
    na_ref[...] = na
    pre_ref[...] = jnp.dot(na, wide_ref[...], preferred_element_type=F32)
    tap = lambda j: jnp.concatenate([taps_ref[i, j:j + 1, :] for i in range(3)], axis=1)
    cur = pre_ref[:, :3 * width]
    line[:8, :] = tail[...]
    line[8:, :] = cur
    tot = cur * tap(0)
    for j in range(1, taps):
        tot = tot + line[8 - j:8 - j + rows, :] * tap(j) * cols_ref[:, j - 1:j]
    tail[...] = line[rows:, :]
    conv_ref[...] = tot
    tot = tot * sigmoid(tot)
    parts = [tot[:, i * width:(i + 1) * width] for i in range(3)]
    eye = (r == c).astype(F32)
    items = []
    for b in range(cb):
        sl = slice(b * C, (b + 1) * C)
        same, lead, trail, keep = segment_parts(seg_s, cols_ref, segr_ref, ((base + step) * cb + b) * C, sl)
        for h in range(heads):
            hs = slice(h * HEAD, (h + 1) * HEAD)
            q, k, v = (part[sl, hs] for part in parts)
            beta = sigmoid(pre_ref[sl, 3 * width + h:3 * width + h + 1]) * cols_ref[sl, 3:4]
            items.append(dict(b=b, h=h, q=head_norm(q), k=head_norm(k), v=v, beta=beta, same=same, lead=lead,
                              trail=trail, keep=keep, sl=sl, hs=hs))
    for it in items:
        it["kk"] = split(it["k"])
        p = jnp.where(it["same"] & (r > c), dot3(it["kk"], it["kk"], NT), 0.0)
        it["p"] = p
        it["low"] = p * it["beta"]
        it["a"] = jnp.where(it["same"] & (r >= c), dot3(it["q"], it["kk"], NT), 0.0)
    inv = invert([it["low"] for it in items], dot3)
    for it, t in zip(items, inv):
        rhs = jnp.concatenate([it["beta"] * it["v"], (it["beta"] * it["lead"]) * it["k"]], axis=1)
        tw = dot3(t, rhs)
        tws = split(tw)
        aw = dot3(it["a"], tws)
        bz = dot3(it["trail"] * it["k"], tws, TN)
        it["tv"], it["w"] = tw[:, :HEAD], tw[:, HEAD:]
        it["o0"], it["n"] = aw[:, :HEAD], it["lead"] * it["q"] - aw[:, HEAD:]
        it["bk"], it["z"] = bz[:, :HEAD], it["keep"] * eye - bz[:, HEAD:]
        it["t"] = t
    for it in items:
        b, h = it["b"], it["h"]
        s = state[h]
        ss = split(s)
        u = it["tv"] - dot3(it["w"], ss)
        o = it["o0"] + dot3(it["n"], ss)
        g = it["v"] - it["lead"] * dot3(it["kk"], ss)
        state[h] = it["bk"] + dot3(it["z"], ss)
        s_ref[b, h] = s
        u_ref[b, h] = u
        g_ref[b, h] = g
        t_ref[b, h] = it["t"]
        a_ref[b, h] = it["a"]
        p_ref[b, h] = it["p"]
        n_ref[b, h] = it["n"]
        z_ref[b, h] = it["z"]
        o_ref[it["sl"], it["hs"]] = o
        mixed = (o * lax.rsqrt(row_sum(o * o) * (1.0 / HEAD) + 1e-5) * gain_ref[0:1, :]).astype(BF)
        mixed_ref[it["sl"], it["hs"]] = mixed
        kept_ref[it["sl"], it["hs"]] = mixed


def stage_bits(n):
    bits = [1 << i for i in range(n.bit_length() - 1)]
    return bits, [bits[1], bits[0]] + bits[2:]


def bwd_kernel(heads, cb, n_f, shard, seg_s, ga0_ref, ga0c_ref, ga1_ref, ga1c_ref, mix_ref, na_ref, out_ref, wide_ref, x_ref, dffn0_ref, dffn1_ref,
               pre_ref, conv_ref, o_ref, cols_ref, segr_ref, taps_ref, gain_ref,
               t_ref, a_ref, p_ref, n_ref, z_ref, s_ref, u_ref, g_ref,
               away1_ref, keep1_ref, away2_ref, keep2_ref, sna_ref, kna_ref, gains_ref, small_ref,
               head_rows, dstate, acc, dpre):
    step = pl.program_id(0)
    steps = pl.num_programs(0)
    width = heads * HEAD
    rows = cb * C
    taps = taps_ref.shape[1]
    back = steps - 1 - step
    core = lax.axis_index("tensor") % 2

    @pl.when(step == 0)
    def _():
        head_rows[...] = jnp.zeros_like(head_rows)
        dstate[...] = jnp.zeros_like(dstate)
        acc[...] = jnp.zeros_like(acc)
        gains_ref[...] = jnp.zeros_like(gains_ref)
        gains_ref[6:7, :] = dffn0_ref[...] + dffn1_ref[...]
        small_ref[...] = jnp.zeros_like(small_ref)

    r, c = block_masks()
    dcs = [[[None] * heads for _ in range(cb)] for _ in range(3)]
    dgain = jnp.zeros((1, HEAD), F32)
    dlog = [None] * cb
    ga = jnp.where(back % 2 == core, jnp.where(back >= 2, ga1_ref[...], ga0_ref[...]),
                   jnp.where(back >= 2, ga1c_ref[...], ga0c_ref[...]))
    dmix = jnp.dot(ga, out_ref[...], preferred_element_type=F32)
    acc[:, 3 * width:4 * width] += lax.dot_general(ga, mix_ref[...], TN, preferred_element_type=F32)
    for b in reversed(range(cb)):
        sl = slice(b * C, (b + 1) * C)
        same, lead, trail, keep = segment_parts(seg_s, cols_ref, segr_ref, (back * cb + b) * C, sl)
        lane = lax.broadcasted_iota(jnp.int32, (C, HEAD), 1)
        dl = jnp.zeros((C, HEAD), F32)
        for h in range(heads):
            hs = slice(h * HEAD, (h + 1) * HEAD)
            cq, ck, cv = (conv_ref[sl, i * width + h * HEAD:i * width + (h + 1) * HEAD] for i in range(3))
            gq, gk, gv = sigmoid(cq), sigmoid(ck), sigmoid(cv)
            q, k = cq * gq, ck * gk
            rq = lax.rsqrt(jnp.sum(q * q, axis=-1, keepdims=True) + 1e-6)
            rk = lax.rsqrt(jnp.sum(k * k, axis=-1, keepdims=True) + 1e-6)
            q, k = q * rq, k * rk
            gb = sigmoid(pre_ref[sl, 3 * width + h:3 * width + h + 1])
            pad = cols_ref[sl, 3:4]
            beta = gb * pad
            o = o_ref[sl, hs]
            dm = dmix[sl, hs]
            ro = lax.rsqrt(jnp.mean(o * o, axis=-1, keepdims=True) + 1e-5)
            oh = o * ro
            dgain = dgain + jnp.sum(dm * oh, axis=0, keepdims=True)
            du0 = dm * gain_ref[0:1, :]
            do = ro * (du0 - oh * jnp.mean(du0 * oh, axis=-1, keepdims=True))
            ds1 = dstate[h]
            u = u_ref[b, h]
            s = s_ref[b, h]
            a = a_ref[b, h]
            p = p_ref[b, h]
            ks = split(k)
            ds1s = split(ds1)
            dos = split(do)
            us = split(u)
            dstate[h] = dot3(z_ref[b, h], ds1s, TN) + dot3(n_ref[b, h], dos, TN)
            du = dot3(a, dos, TN) + trail * dot3(ks, ds1s)
            dr = dot3(t_ref[b, h], du, TN)
            drs = split(dr)
            ss = split(s)
            dlow = jnp.where(same & (r > c), -dot3(drs, us, NT), 0.0)
            da = jnp.where(same & (r >= c), dot3(dos, us, NT), 0.0)
            dv = beta * dr
            dbeta = jnp.sum(dr * g_ref[b, h] , axis=-1, keepdims=True) + jnp.sum(dlow * p, axis=-1, keepdims=True)
            dp = split(beta * dlow)
            das = split(da)
            dq = lead * dot3(dos, ss, NT) + dot3(das, ks)
            dk = (dot3(das, q, TN) + trail * dot3(us, ds1s, NT) - (beta * lead) * dot3(drs, ss, NT)
                  + dot3(dp, ks) + dot3(dp, ks, TN))
            dsq = rq * (dq - q * jnp.sum(q * dq, axis=-1, keepdims=True))
            dsk = rk * (dk - k * jnp.sum(k * dk, axis=-1, keepdims=True))
            dcs[0][b][h] = dsq * gq * (1.0 + cq * (1.0 - gq))
            dcs[1][b][h] = dsk * gk * (1.0 + ck * (1.0 - gk))
            dcs[2][b][h] = dv * gv * (1.0 + cv * (1.0 - gv))
            dl = jnp.where(lane == h, dbeta * pad * gb * (1.0 - gb), dl)
        dlog[b] = dl
    gains_ref[7:8, :HEAD] += dgain
    for b in range(cb):
        dpre[b * C:(b + 1) * C, 3 * width:] = dlog[b].astype(BF)
    for i in range(3):
        dc = jnp.concatenate([jnp.concatenate(dcs[i][b], axis=1) for b in range(cb)], axis=0)
        pre = pre_ref[:, i * width:(i + 1) * width]
        tot = dc * taps_ref[i, 0:1, :]
        grads = [jnp.sum(dc * pre, axis=0, keepdims=True)]
        for j in range(1, taps):
            e = dc * cols_ref[:, j - 1:j]
            ext = jnp.concatenate([e, head_rows[j - 1, :, i * width:(i + 1) * width]], axis=0)
            head_rows[j - 1, :, i * width:(i + 1) * width] = e[:8]
            e = lax.slice_in_dim(ext, j, j + rows, axis=0)
            tot = tot + e * taps_ref[i, j:j + 1, :]
            grads.append(jnp.sum(e * pre, axis=0, keepdims=True))
        dpre[:, i * width:(i + 1) * width] = tot.astype(BF)
        small_ref[i:i + 1, :taps * width] += jnp.concatenate(grads, axis=1)
    low = dpre[...]
    acc[:, :3 * width] += lax.dot_general(na_ref[...], low[:, :3 * width], TN, preferred_element_type=F32)
    acc[:, 4 * width:] += lax.dot_general(na_ref[...], low[:, 3 * width:], TN, preferred_element_type=F32)
    dna = lax.dot_general(low, wide_ref[...], NT, preferred_element_type=F32)
    x = x_ref[...].astype(F32)
    gains_ref[5:6, :] += jnp.sum(dna * (x * lax.rsqrt(jnp.mean(x * x, axis=-1, keepdims=True) + 1e-6)), axis=0, keepdims=True)

    @pl.when(back % 2 == core)
    def _():
        kna_ref[back // 2] = dna

    @pl.when(back % 2 != core)
    def _():
        sna_ref[back // 2] = dna.astype(BF)

    @pl.when(step == steps - 1)
    def _():
        small_ref[3:3 + heads, :] = acc[:, 4 * width:].T[:heads, :]
        me = lax.axis_index("fsdp")
        first, second = stage_bits(n_f)
        half = 2 * width
        for ref, other, bit, lanes in ((away1_ref, keep1_ref, first[0], slice(0, half)), (away2_ref, keep2_ref, second[0], slice(half, 2 * half))):
            mine = (me // bit) % 2
            for j in range(n_f // 2):
                low_bits = j % bit
                there = (j - low_bits) * 2 + low_bits
                ref[j] = acc[pl.ds(pl.multiple_of((there + (1 - mine) * bit) * shard, 16), shard), lanes].astype(BF)
                other[j] = acc[pl.ds(pl.multiple_of((there + mine * bit) * shard, 16), shard), lanes].astype(other.dtype)


def whole(shape):
    return pl.BlockSpec(shape, lambda i, *_: (0,) * len(shape), pipeline_mode=pl.Buffered(1))


def shaped(shape, dtype=F32):
    return jax.ShapeDtypeStruct(shape, dtype)


def params(limit=60):
    return pltpu.CompilerParams(dimension_semantics=("arbitrary",), vmem_limit_bytes=limit * 2**20)


COST = pl.CostEstimate(flops=10**10, bytes_accessed=10**7, transcendentals=0)
TINY = pl.CostEstimate(flops=1, bytes_accessed=1, transcendentals=0)


def fwd_call_kernel(heads, cb, base, n_old, *refs):
    ins, rest = ((*refs[:8], None, None), refs[8:]) if n_old == 0 else (refs[:10], refs[10 + n_old:])
    outs, tail_out, state_out, tail, state, line = rest[:14], rest[14], rest[15], rest[16], rest[17], rest[18]
    fwd_kernel(heads, cb, base, *ins, *outs, tail, state, line)

    @pl.when(pl.program_id(0) == pl.num_programs(0) - 1)
    def _():
        tail_out[...] = tail[...]
        state_out[...] = state[...]


def mixer_fwd(part, parts, x, wide, again, cols, segr, seg, taps, gain, tail, state, old, cb=4):
    n, d = x.shape
    width = taps.shape[2]
    heads = width // HEAD
    wide_cols = 3 * width + HEAD
    rows = cb * C
    steps = n // parts // rows
    base = part * steps
    sq = shaped((n // C, heads, C, HEAD))
    sqspec = pl.BlockSpec((cb, heads, C, HEAD), lambda i, s: (i + base, 0, 0, 0))
    here = lambda w: pl.BlockSpec((rows, w), lambda i, s: (i + base, 0))
    ins = [x, wide, again, cols, segr, taps, gain] + ([tail, state] if old else [])
    tail, state = shaped((8, 3 * width)), shaped((heads, HEAD, HEAD))
    kept = [shaped((n, width), BF), shaped((n, d), BF), shaped((n, wide_cols)), shaped((n, 3 * width)), shaped((n, width))] + [sq] * 8
    return pl.pallas_call(
        functools.partial(fwd_call_kernel, heads, cb, base, len(old)),
        grid_spec=pltpu.PrefetchScalarGridSpec(
            num_scalar_prefetch=1, grid=(steps,),
            in_specs=[here(d), whole((d, wide_cols)), whole((1, d)), here(cols.shape[1]),
                      pl.BlockSpec((1, rows), lambda i, s: (0, i + base)),
                      whole(taps.shape), whole((1, HEAD))] + ([whole(tail.shape), whole(state.shape)] if old else [])
            + [pl.BlockSpec(memory_space=pl.ANY)] * len(old),
            out_specs=[pl.BlockSpec((rows, width), lambda i, s: (i, 0)), here(width), here(d), here(wide_cols), here(3 * width), here(width)]
            + [sqspec] * 8 + [whole(tail.shape), whole(state.shape)],
            scratch_shapes=[pltpu.VMEM(tail.shape, F32), pltpu.VMEM(state.shape, F32), pltpu.VMEM((rows + 8, 3 * width), F32)]),
        out_shape=[shaped((n // parts, width), BF)] + kept + [shaped(tail.shape), shaped(state.shape)],
        input_output_aliases={1 + len(ins) + i: 1 + i for i in range(len(old))},
        compiler_params=params(),
        cost_estimate=COST,
        name="mixer_fwd",
    )(seg, *ins, *old)


def mixer_bwd(n_f, shard, ga, out, wide, x, dffn, cols, segr, seg, taps, gain, kept, cb=2):
    mix, na, pre, conv, o, *rest = kept
    n, wide_cols = pre.shape
    d = x.shape[1]
    width = taps.shape[2]
    heads = width // HEAD
    rows = cb * C
    steps = n // rows
    ntap = taps.shape[1]
    sqspec = pl.BlockSpec((cb, heads, C, HEAD), lambda i, s: (steps - 1 - i, 0, 0, 0))
    row = lambda w: pl.BlockSpec((rows, w), lambda i, s: (steps - 1 - i, 0))
    outs = [shaped((n_f // 2, shard, 2 * width), BF)] * 4 + [
            shaped((2, rows, d), BF), shaped((2, rows, d)), shaped((8, d)), shaped((8, d))]
    return pl.pallas_call(
        functools.partial(bwd_kernel, heads, cb, n_f, shard),
        grid_spec=pltpu.PrefetchScalarGridSpec(
            num_scalar_prefetch=1, grid=(steps,),
            in_specs=[whole((rows, d))] * 4 + [row(width), row(d), whole(out.shape), whole((d, wide_cols)), row(d), whole((1, d)), whole((1, d)),
                      row(wide_cols), row(3 * width), row(width),
                      row(cols.shape[1]), pl.BlockSpec((1, rows), lambda i, s: (0, steps - 1 - i)),
                      whole(taps.shape), whole((1, HEAD))] + [sqspec] * 8,
            out_specs=[whole(v.shape) for v in outs],
            scratch_shapes=[pltpu.VMEM((ntap - 1, 8, 3 * width), F32), pltpu.VMEM((heads, HEAD, HEAD), F32),
                            pltpu.VMEM((d, 4 * width + HEAD), F32), pltpu.VMEM((rows, wide_cols), BF)]),
        out_shape=outs,
        compiler_params=params(),
        cost_estimate=COST,
        name="mixer_bwd",
    )(seg, *ga, mix, na, out, wide, x, *dffn, pre, conv, o, cols, segr, taps, gain, *rest)


def fold_kernel(n_f, stage, k1_ref, g1_ref, k2_ref, g2_ref, a1_out, k1_out, a2_out, k2_out):
    me = lax.axis_index("fsdp")
    for order, keep, got, away_out, keep_out in ((0, k1_ref, g1_ref, a1_out, k1_out), (1, k2_ref, g2_ref, a2_out, k2_out)):
        bits = stage_bits(n_f)[order]
        bit = bits[stage]
        left = sorted(b for b in bits[stage:])
        place = 1 << left.index(bit)
        mine = (me // bit) % 2
        for j in range(keep.shape[0] // 2):
            low = j % place
            there = (j - low) * 2 + low
            theirs = there + (1 - mine) * place
            away_out[j] = (keep[theirs].astype(F32) + got[theirs].astype(F32)).astype(BF)
            ours = there + mine * place
            keep_out[j] = (keep[ours].astype(F32) + got[ours].astype(F32)).astype(keep_out.dtype)


def fold(n_f, stage, k1, g1, k2, g2):
    m, shard, w = k1.shape
    outs = [shaped((m // 2, shard, w), BF)] * 4
    return pl.pallas_call(
        functools.partial(fold_kernel, n_f, stage),
        out_shape=outs,
        compiler_params=pltpu.CompilerParams(vmem_limit_bytes=60 * 2**20),
        cost_estimate=TINY,
        name="fold",
    )(k1, g1, k2, g2)


def finish_kernel(heads, ntap, k1_ref, g1_ref, k2_ref, g2_ref, s_ref, *refs):
    got, (qkv_ref, out_ref, taps_ref, beta_ref, attn_ref, ffn_ref, head_ref, hold) = refs[:-9], refs[-8:]
    width = qkv_ref.shape[2]
    shard = qkv_ref.shape[1]
    a = k1_ref[0].astype(F32) + g1_ref[0].astype(F32)
    b = k2_ref[0].astype(F32) + g2_ref[0].astype(F32)
    qkv_ref[0] = a[:, :width]
    qkv_ref[1] = a[:, width:]
    qkv_ref[2] = b[:, :width]
    out_ref[...] = b[:, width:].T
    small = s_ref[...]
    for g in got:
        small = small + g[...]
    width = taps_ref.shape[2]
    for i in range(3):
        for k in range(ntap):
            taps_ref[i, k:k + 1, :] = small[i:i + 1, k * width:(k + 1) * width]
    attn_ref[...] = small[5:6]
    ffn_ref[...] = small[6:7]
    head_ref[...] = small[7:8, :HEAD]
    if shard == 128:
        hold[...] = small
        me = lax.axis_index("fsdp")
        beta_ref[...] = hold[3:3 + heads, pl.ds(pl.multiple_of(me * shard, 128), shard)]
    else:
        beta_ref[...] = small[3:3 + heads]


def finish(heads, ntap, k1, g1, k2, g2, small, got, wait_for):
    m, shard, w = k1.shape
    d = small.shape[1]
    return pl.pallas_call(
        functools.partial(finish_kernel, heads, ntap),
        in_specs=[pl.BlockSpec(memory_space=pltpu.VMEM)] * (5 + len(got)) + [pl.BlockSpec(memory_space=pl.ANY)],
        out_shape=[shaped((3, shard, w // 2)), shaped((w // 2, shard)), shaped((3, ntap, w // 2)),
                   shaped((heads, 128 if shard == 128 else d)), shaped((1, d)), shaped((1, d)), shaped((1, HEAD))],
        scratch_shapes=[pltpu.VMEM((8, d), F32)],
        compiler_params=pltpu.CompilerParams(vmem_limit_bytes=60 * 2**20),
        cost_estimate=TINY,
        name="finish",
    )(k1, g1, k2, g2, small, *got, wait_for)


def ffn_kernel(ff, *refs):
    m, out, (x_ref, w_ref, gf_ref, gain_ref), rest = refs[:4], refs[4:8], refs[8:12], refs[12:]
    mid_ref, nf_ref, hid_ref, dgu_ref, keep_ref, send_ref, dgain_ref, hold = rest
    rows = keep_ref.shape[0]
    core = lax.axis_index("tensor") % 2
    mid = x_ref[...].astype(F32)
    for k in range(4):
        mid = mid + lax.dot_general(m[k][...], out[k][...], NT, preferred_element_type=F32)
    hold[...] = mid
    unit = mid * lax.rsqrt(jnp.mean(mid * mid, axis=-1, keepdims=True) + 1e-6)
    nf = (unit * gain_ref[0:1, :]).astype(BF)
    nf_ref[...] = nf
    mid_ref[...] = hold[pl.ds(pl.multiple_of(core * rows, 16), rows), :]
    gate = lax.dot_general(w_ref[:ff, :], nf, NT, preferred_element_type=F32)
    up = lax.dot_general(w_ref[ff:2 * ff, :], nf, NT, preferred_element_type=F32)
    dh = lax.dot_general(w_ref[2 * ff:, :], gf_ref[...], NT, preferred_element_type=F32)
    sig = sigmoid(gate)
    act = gate * sig
    hid_ref[...] = (act * up).astype(BF)
    dgu_ref[:ff, :] = (dh * up * sig * (1.0 + gate * (1.0 - sig))).astype(BF)
    dgu_ref[ff:, :] = (dh * act).astype(BF)
    dnf = lax.dot_general(dgu_ref[...], w_ref[:2 * ff, :], TN, preferred_element_type=F32)
    dgain_ref[...] = jnp.sum(dnf * unit, axis=0, keepdims=True)
    hold[...] = dnf
    keep_ref[...] = hold[pl.ds(pl.multiple_of(core * rows, 16), rows), :]
    send_ref[...] = hold[pl.ds(pl.multiple_of((1 - core) * rows, 16), rows), :].astype(BF)


def ffn(part, m, out, x, weights, gf, gain):
    n, width = m[0].shape
    d = x.shape[1]
    ff = weights.shape[0] // 3
    here = pl.BlockSpec((n, d), lambda i: (part, 0))
    outs = [shaped((n // 2, d)), shaped((n, d), BF), shaped((ff, n), BF), shaped((2 * ff, n), BF),
            shaped((n // 2, d)), shaped((n // 2, d), BF), shaped((1, d))]
    return pl.pallas_call(
        functools.partial(ffn_kernel, ff),
        grid=(1,),
        in_specs=[whole(v.shape) for v in (*m, *out)] + [here, whole(weights.shape), here, whole((1, d))],
        out_specs=[whole(v.shape) for v in outs],
        out_shape=outs,
        scratch_shapes=[pltpu.VMEM((n, d), F32)],
        compiler_params=params(),
        cost_estimate=COST,
        name="ffn",
    )(*m, *out, x, weights, gf, gain)


def grad_kernel(part, n, *refs):
    lows, others, (mid_ref, cot_ref, coty_ref, gain_ref, grad_ref, low_out) = refs[:n], refs[n:2 * n], refs[2 * n:]
    chip = lax.axis_index("tensor") // 2
    mid = mid_ref[...]
    factor = lax.rsqrt(jnp.mean(mid * mid, axis=-1, keepdims=True) + 1e-6)
    d_nf = jnp.concatenate([a[...].astype(F32) + b[...].astype(F32) for a, b in zip(lows, others)], axis=0)
    u = d_nf * gain_ref[0:1, :]
    cot = jnp.where(chip == part, cot_ref[...], coty_ref[...]).astype(F32)
    grad = cot + factor * u - mid * (factor * factor * factor) * jnp.mean(u * mid, axis=-1, keepdims=True)
    grad_ref[...] = grad
    low_out[...] = grad.astype(BF)


def grad_rows(part, lows, others, mid, cot, cot_y, gain):
    return pl.pallas_call(
        functools.partial(grad_kernel, part, len(lows)),
        out_shape=[shaped(mid.shape), shaped(mid.shape, BF)],
        compiler_params=pltpu.CompilerParams(vmem_limit_bytes=24 * 2**20),
        cost_estimate=TINY,
        name="grad_rows",
    )(*lows, *others, mid, cot, cot_y, gain)


def down_kernel(hid0_ref, hid1_ref, w_ref, send_ref, keep_ref, hold):
    core = lax.axis_index("tensor") % 2
    rows = send_ref.shape[1]
    for i, hid in enumerate((hid0_ref, hid1_ref)):
        hold[...] = lax.dot_general(hid[...], w_ref[...], TN, preferred_element_type=F32)
        keep_ref[i] = hold[pl.ds(pl.multiple_of(core * rows, 16), rows), :]
        send_ref[i] = hold[pl.ds(pl.multiple_of((1 - core) * rows, 16), rows), :].astype(BF)


def down(hid0, hid1, weights, wait_for):
    ff, n = hid0.shape
    d = weights.shape[1]
    outs = [shaped((2, n // 2, d), BF), shaped((2, n // 2, d))]

    def body(*refs):
        down_kernel(*refs[:3], *refs[3 + len(wait_for):])

    return pl.pallas_call(
        body,
        grid=(1,),
        in_specs=[whole(hid0.shape)] * 2 + [pl.BlockSpec((ff, d), lambda i: (2, 0))] + [pl.BlockSpec(memory_space=pl.ANY)] * len(wait_for),
        out_specs=[whole(v.shape) for v in outs],
        out_shape=outs,
        scratch_shapes=[pltpu.VMEM((n, d), F32)],
        compiler_params=params(),
        cost_estimate=TINY,
        name="down",
    )(hid0, hid1, weights, *wait_for)


def ffn_grads_kernel(ff, parts, *refs):
    gf_ref, o_ref = refs[3 * parts], refs[-1]
    n = refs[0].shape[1]
    up = down = None
    for i in range(parts):
        dgu, hid, nf = refs[3 * i:3 * i + 3]
        a = jnp.dot(dgu[...], nf[...], preferred_element_type=F32)
        b = jnp.dot(hid[...], gf_ref[i * n:(i + 1) * n, :], preferred_element_type=F32)
        up = a if up is None else up + a
        down = b if down is None else down + b
    for k in range(o_ref.shape[0]):
        lanes = slice(k * 128, (k + 1) * 128)
        o_ref[k, :2 * ff, :] = up[:, lanes].astype(BF)
        o_ref[k, 2 * ff:, :] = down[:, lanes].astype(BF)


def ffn_grads(pieces, gf, wait_for, step=256):
    ff = pieces[0][1].shape[0]
    n, d = gf.shape
    flat, specs = [], []
    for dgu, hid, nf in pieces:
        flat += [dgu, hid, nf]
        specs += [whole(dgu.shape), whole(hid.shape), pl.BlockSpec((nf.shape[0], step), lambda i: (0, i))]
    return pl.pallas_call(
        functools.partial(ffn_grads_kernel, ff, len(pieces)),
        grid=(d // step,),
        in_specs=specs + [pl.BlockSpec((n, step), lambda i: (0, i))] + [pl.BlockSpec(memory_space=pl.ANY)] * len(wait_for),
        out_specs=pl.BlockSpec((step // 128, 3 * ff, 128), lambda i: (i, 0, 0)),
        out_shape=shaped((d // 128, 3 * ff, 128), BF),
        compiler_params=params(),
        cost_estimate=pl.CostEstimate(flops=5 * 10**9, bytes_accessed=10**7, transcendentals=0),
        name="ffn_grads",
    )(*flat, gf, *wait_for)


def to_chips_kernel(keep, got, wait_for, mine_ref, away_ref):
    chip = lax.axis_index("tensor") // 2
    mine_ref[...] = keep[chip] + got[chip].astype(F32)
    away_ref[...] = (keep[1 - chip] + got[1 - chip].astype(F32)).astype(BF)


def to_chips(keep, got, wait_for):
    spec = pl.BlockSpec(memory_space=pltpu.VMEM)
    return pl.pallas_call(
        to_chips_kernel,
        in_specs=[spec] * 2 + [pl.BlockSpec(memory_space=pl.ANY)],
        out_shape=[shaped(keep.shape[1:]), shaped(keep.shape[1:], BF)],
        compiler_params=pltpu.CompilerParams(vmem_limit_bytes=60 * 2**20),
        cost_estimate=TINY,
        name="to_chips",
    )(keep, got, wait_for)


def last_kernel(g0, g1, na, na_y, x_ref, gain_ref, mid0, mid1, out, out_y, in_ref, block_ref):
    first = lax.axis_index("tensor") // 2 == 0
    x = x_ref[...].astype(F32)
    factor = lax.rsqrt(jnp.mean(x * x, axis=-1, keepdims=True) + 1e-6)
    u = (na[...] + na_y[...].astype(F32)) * gain_ref[0:1, :]
    in_ref[...] = jnp.where(first, g0[...], g1[...]) + (factor * u - x * (factor * factor * factor) * jnp.mean(u * x, axis=-1, keepdims=True))
    block_ref[...] = (jnp.where(first, mid0[...], mid1[...]) + out[...] + out_y[...].astype(F32)).astype(BF)


def last_rows(g0, g1, na, na_y, x, gain, mid0, mid1, out, out_y):
    return pl.pallas_call(
        last_kernel,
        out_shape=[shaped(g0.shape), shaped(g0.shape, BF)],
        compiler_params=pltpu.CompilerParams(vmem_limit_bytes=60 * 2**20),
        cost_estimate=TINY,
        name="last_rows",
    )(g0, g1, na, na_y, x, gain, mid0, mid1, out, out_y)


def ffn_cast_kernel(d_ref, expand_ref, down_ref):
    ff = down_ref.shape[0]
    expand_ref[0] = d_ref[:ff, :].astype(F32)
    expand_ref[1] = d_ref[ff:2 * ff, :].astype(F32)
    down_ref[...] = d_ref[2 * ff:, :].astype(F32)


def ffn_cast(d):
    ff, w = d.shape[0] // 3, d.shape[1]
    return pl.pallas_call(
        ffn_cast_kernel,
        out_shape=[shaped((2, ff, w)), shaped((ff, w))],
        compiler_params=pltpu.CompilerParams(vmem_limit_bytes=60 * 2**20),
        cost_estimate=TINY,
        name="ffn_cast",
    )(d)


def ffn_split_kernel(ff, parts, *refs):
    blocks, expand, away, keep = refs[-1], refs[-4], refs[-3], refs[-2]
    ffn_grads_kernel(ff, parts, *refs[:3 * parts + 1], blocks)
    me = lax.axis_index("fsdp")
    for k in range(blocks.shape[0]):
        expand[k] = blocks[k, :2 * ff, :]
        block = pl.program_id(0) * blocks.shape[0] + k

        @pl.when(block % 2 == me % 2)
        def _(k=k, block=block):
            keep[block // 2] = blocks[k, 2 * ff:, :]

        @pl.when(block % 2 != me % 2)
        def _(k=k, block=block):
            away[block // 2] = blocks[k, 2 * ff:, :]


def ffn_split_grads(pieces, gf, wait_for, step=256):
    ff = pieces[0][1].shape[0]
    n, d = gf.shape
    flat, specs = [], []
    for dgu, hid, nf in pieces:
        flat += [dgu, hid, nf]
        specs += [whole(dgu.shape), whole(hid.shape), pl.BlockSpec((nf.shape[0], step), lambda i: (0, i))]
    per = step // 128
    halves = shaped((d // 256, ff, 128), BF)
    return pl.pallas_call(
        functools.partial(ffn_split_kernel, ff, len(pieces)),
        grid=(d // step,),
        in_specs=specs + [pl.BlockSpec((n, step), lambda i: (0, i))] + [pl.BlockSpec(memory_space=pl.ANY)] * len(wait_for),
        out_specs=[pl.BlockSpec((per, 2 * ff, 128), lambda i: (i, 0, 0)), whole(halves.shape), whole(halves.shape)],
        out_shape=[shaped((d // 128, 2 * ff, 128), BF), halves, halves],
        scratch_shapes=[pltpu.VMEM((per, 3 * ff, 128), BF)],
        compiler_params=params(),
        cost_estimate=COST,
        name="ffn_grads",
    )(*flat, gf, *wait_for)


def halve_kernel(bit, k_ref, g_ref, wait_for, away, keep):
    mine = (lax.axis_index("fsdp") // bit) % 2
    count = k_ref.shape[0] // 2
    for j in range(count):
        ours, theirs = (2 * j + mine, 2 * j + 1 - mine) if bit == 2 else (mine, 1 - mine)
        away[j] = (k_ref[theirs].astype(F32) + g_ref[theirs].astype(F32)).astype(BF)
        keep[j] = (k_ref[ours].astype(F32) + g_ref[ours].astype(F32)).astype(BF)


def halve(bit, k, g, wait_for):
    m, ff, w = k.shape
    spec = pl.BlockSpec(memory_space=pltpu.VMEM)
    return pl.pallas_call(
        functools.partial(halve_kernel, bit),
        in_specs=[spec] * 2 + [pl.BlockSpec(memory_space=pl.ANY)],
        out_shape=[shaped((m // 2, ff, w), BF)] * 2,
        compiler_params=pltpu.CompilerParams(vmem_limit_bytes=60 * 2**20),
        cost_estimate=TINY,
        name="halve",
    )(k, g, wait_for)


def split_cast_kernel(d_ref, k_ref, g_ref, expand_ref, down_ref):
    ff = down_ref.shape[0]
    expand_ref[0] = d_ref[:ff, :].astype(F32)
    expand_ref[1] = d_ref[ff:, :].astype(F32)
    down_ref[...] = k_ref[0].astype(F32) + g_ref[0].astype(F32)


def split_cast(d, k, g):
    ff, w = d.shape[0] // 2, d.shape[1]
    return pl.pallas_call(
        split_cast_kernel,
        out_shape=[shaped((2, ff, w)), shaped((ff, w))],
        compiler_params=pltpu.CompilerParams(vmem_limit_bytes=60 * 2**20),
        cost_estimate=TINY,
        name="ffn_cast",
    )(d, k, g)


def pack_kernel(qkv_ref, beta_ref, out_ref, o_ref):
    width = qkv_ref.shape[2]
    n = o_ref.shape[0]
    for i in range(3):
        o_ref[:, i * width:(i + 1) * width] = qkv_ref[i]
    beta = beta_ref[...].astype(F32)
    heads = beta.shape[1]
    o_ref[:, 3 * width:3 * width + 128] = jnp.concatenate([beta, jnp.zeros((n, 128 - heads), F32)], axis=1).astype(BF)
    o_ref[:, 3 * width + 128:] = out_ref[...].astype(F32).T.astype(BF)


def pack(qkv, beta, out):
    n, width = qkv.shape[1:]
    return pl.pallas_call(
        pack_kernel,
        out_shape=shaped((n, 4 * width + 128), BF),
        compiler_params=pltpu.CompilerParams(vmem_limit_bytes=60 * 2**20),
        name="pack",
    )(qkv, beta, out)


def columns(seg, pad):
    n = seg.shape[0]
    cols = []
    for j in range(1, 4):
        before = jnp.concatenate([jnp.full((j,), -1, seg.dtype), seg[:n - j]])
        cols.append((before == seg).astype(F32))
    cols += [pad.astype(F32), seg.astype(F32)]
    cols += [jnp.zeros((n,), F32)] * 3
    return jnp.stack(cols, axis=1)


def hop(value, axis, bit):
    n = lax.axis_size(axis)
    return lax.ppermute(value, axis, [(i, i ^ bit) for i in range(n)])


def fence(*values):
    return lax.optimization_barrier(values)


def y_hop(value):
    return hop(value, "tensor", 2)


def core_hop(value):
    return hop(value, "tensor", 1)


def in_order(own, other_chip, pair):
    me = lax.axis_index("tensor")
    full = jnp.zeros((4,) + own.shape, own.dtype)
    for k, block in ((0, own), (2, other_chip), (1, pair[0]), (3, pair[1])):
        full = lax.dynamic_update_slice(full, block[None], (me ^ k,) + (0,) * own.ndim)
    return full.reshape((4 * own.shape[0],) + own.shape[1:])


class Ring:
    def __init__(self, value):
        n = lax.axis_size("fsdp")
        order = [i for i in range(0, n, 2)] + [i for i in reversed(range(1, n, 2))]
        me = lax.axis_index("fsdp")
        self.n = n
        self.me = jnp.where(me % 2 == 0, me // 2, n - 1 - me // 2)
        self.right = [(order[i], order[(i + 1) % n]) for i in range(n)]
        self.left = [(b, a) for a, b in self.right]
        self.rows = value.shape[0]
        self.full = jnp.zeros((n * self.rows,) + value.shape[1:], value.dtype)
        self.a = self.b = value
        self.k = 0
        self.put(value, 0, 0)

    def put(self, part, steps, start):
        place = lax.rem(self.me + steps + self.n, self.n)
        owner = jnp.where(place < self.n // 2, 2 * place, 2 * (self.n - 1 - place) + 1)
        self.full = lax.dynamic_update_slice(self.full, part, (owner * self.rows + start, 0))

    def step(self):
        self.k += 1
        k, half = self.k, self.rows // 2
        self.split = 2 * k == self.n and half % 16 == 0
        if self.split:
            self.a = lax.ppermute(self.a[:half], "fsdp", self.right)
            self.b = lax.ppermute(self.b[half:], "fsdp", self.left)
            return
        self.a = lax.ppermute(self.a, "fsdp", self.right)
        if 2 * k < self.n:
            self.b = lax.ppermute(self.b, "fsdp", self.left)

    def keep(self):
        self.put(self.a, -self.k, 0)
        if self.split or 2 * self.k < self.n:
            self.put(self.b, self.k, self.rows // 2 if self.split else 0)


def hop_sum(value, axis, bit):
    return value + hop(value, axis, bit)


def on_device(
    layer_input, segment_ids, pad_mask, attn_gain, ffn_gain, out_gain,
    qkv_weight, beta_weight, conv_weight, out_weight, expand_weight, down_weight, cotangent,
):
    n_f = lax.axis_size("fsdp")
    me_t = lax.axis_index("tensor")
    chip = me_t // 2
    rows, d_model = layer_input.shape
    width = qkv_weight.shape[3]
    heads = beta_weight.shape[2]
    ff = down_weight.shape[1]
    shard = qkv_weight.shape[2]
    taps = conv_weight[0]
    ntap = taps.shape[1]
    first_bits, second_bits = stage_bits(n_f)

    packed = pack(qkv_weight[0], beta_weight[0], out_weight[0])
    packed, expand_own, down_own = fence(packed, expand_weight[0], down_weight[0])
    ring = Ring(packed)
    ring.step()
    x_y = y_hop(layer_input)
    x_c = core_hop(layer_input)
    ffn_own = jnp.concatenate([expand_own[0].T, expand_own[1].T, down_own], axis=0)
    weights = lax.all_gather(ffn_own, "fsdp", axis=1, tiled=True)
    seg = segment_ids[0]
    cols = columns(seg, pad_mask[0])
    segr = seg.astype(F32)[None]
    ring.a, ring.b, x_c = fence(ring.a, ring.b, x_c)
    ring.keep()
    ring.step()
    c_y = y_hop(cotangent)
    c_c = core_hop(cotangent)
    ring.a, ring.b, x_y, c_y = fence(ring.a, ring.b, x_y, c_y)
    ring.keep()
    ring.step()
    x_cy = core_hop(x_y)
    c_cy = core_hop(c_y)
    ring.a, ring.b, cols, x_cy, c_cy = fence(ring.a, ring.b, cols, x_cy, c_cy)
    ring.keep()
    x_full = in_order(layer_input, x_y, (x_c, x_cy))
    g_f = in_order(cotangent, c_y, (c_c, c_cy))
    while 2 * ring.k < n_f:
        ring.step()
        ring.keep()
    wide, x_full, g_f = fence(ring.full, x_full, g_f)

    out_own = wide[:, 3 * width + HEAD:]
    tail = state = None

    def mix(i, tail, state, old):
        m, *kept, tail, state = mixer_fwd(i, 2, x_full, wide, attn_gain, cols, segr, seg, taps, out_gain, tail, state, old)
        return m, kept, tail, state

    ow_y = y_hop(out_own)
    ow_c = core_hop(out_own)
    m0, kept, tail, state = mix(0, tail, state, [])
    ow_y, ow_c, m0, tail, state = fence(ow_y, ow_c, m0, tail, state)
    m0_y = y_hop(m0)
    m0_c = core_hop(m0)
    ow_cy = core_hop(ow_y)
    m1, kept, tail, state = mix(1, tail, state, kept)
    m0_y, m0_c, ow_cy, m1 = fence(m0_y, m0_c, ow_cy, m1)

    def feed(i, *m):
        return ffn(i, m, (out_own, ow_y, ow_c, ow_cy), x_full, weights, g_f, ffn_gain)

    m1_y = y_hop(m1)
    m1_c = core_hop(m1)
    m0_cy = core_hop(m0_y)
    mid0, nf0, hid0, dgu0, keep0, send0, dgain0 = feed(0, m0, m0_y, m0_c, m0_cy)
    m1_y, m1_c, send0 = fence(m1_y, m1_c, send0)
    m1_cy = core_hop(m1_y)
    low0 = (keep0 + core_hop(send0).astype(F32)).astype(BF)
    m1_cy, low0 = fence(m1_cy, low0)
    low0_y = y_hop(low0)
    mid1, nf1, hid1, dgu1, keep1, send1, dgain1 = feed(1, m1, m1_y, m1_c, m1_cy)
    low0_y, send1 = fence(low0_y, send1)
    cut = rows // 2
    got1 = core_hop(send1)
    low1 = (keep1[:cut] + got1[:cut].astype(F32)).astype(BF)
    low1b = (keep1[cut:] + got1[cut:].astype(F32)).astype(BF)
    grad0, ga0 = grad_rows(0, [low0], [low0_y], mid0, cotangent, c_y, ffn_gain)
    low1, low1b, ga0 = fence(low1, low1b, ga0)
    low1_y, low1b_y = y_hop(low1), y_hop(low1b)
    ga0_c = core_hop(ga0)
    blocks = ffn_grads([(dgu0, hid0, nf0), (dgu1, hid1, nf1)], g_f, [low1])
    q = d_model // 128
    if q != n_f:
        blocks = blocks.reshape(q, 3 * ff, n_f // q, shard).transpose(0, 2, 1, 3).reshape(n_f, 3 * ff, shard)
    send_out, keep_out = down(hid0, hid1, weights, [blocks])
    low1_y, ga0_c, blocks = fence(low1_y, ga0_c, blocks)
    low1b_y, send_out, done_blocks = fence(low1b_y, send_out, blocks)
    d_ffn = lax.psum_scatter(blocks, "fsdp", scatter_dimension=0, tiled=False)
    grad1, ga1 = grad_rows(1, [low1, low1b], [low1_y, low1b_y], mid1, cotangent, c_y, ffn_gain)
    ga1_c = core_hop(ga1)
    ga1, ga1_c = fence(ga1, ga1_c)

    out_c = core_hop(send_out)
    made = mixer_bwd(
        n_f, shard, (ga0, ga0_c, ga1, ga1_c), out_own, wide, x_full, (dgain0, dgain1), cols, segr, seg, taps, out_gain, kept)
    away1, k1, away2, k2, send_na, keep_na, gains, small, out_c = fence(*made, out_c)

    g1 = hop(away1, "fsdp", first_bits[0])
    g2 = hop(away2, "fsdp", second_bits[0])
    na_c = core_hop(send_na)
    gains_got = [hop(gains, "tensor", k) for k in range(1, 4)]
    out, out_away = to_chips(keep_out, out_c, done_blocks)
    na, na_away = to_chips(keep_na, na_c, gains)
    g1, g2, na_away, out_away, *gains_got = fence(g1, g2, na_away, out_away, *gains_got)
    count = len(first_bits)
    small = small + gains + gains_got[0] + (gains_got[1] + gains_got[2])
    for stage in range(1, count):
        away1, k1, away2, k2 = fold(n_f, stage, k1, g1, k2, g2)
        if stage == 1:
            na_y, out_y = y_hop(na_away), y_hop(out_away)
        g1 = hop(away1, "fsdp", first_bits[stage])
        g2 = hop(away2, "fsdp", second_bits[stage])
        if stage < count - 1:
            small = hop_sum(small, "fsdp", first_bits[stage - 1])
            g1, g2, small, na_y = fence(g1, g2, small, na_y)
    if n_f == 8:
        got = [hop(small, "fsdp", k) for k in (2, 4, 6)]
    else:
        small = hop_sum(small, "fsdp", first_bits[count - 2])
        got = [hop(small, "fsdp", first_bits[count - 1])]
    input_grad, block_outs = last_rows(grad0, grad1, na, na_y, layer_input, attn_gain, mid0, mid1, out, out_y)
    block_outs = block_outs[None]
    expand_grad, down_grad = ffn_cast(d_ffn)
    qkv_grad, out_grad, conv_grad, beta_grad, attn_total, ffn_total, head_total = finish(heads, ntap, k1, g1, k2, g2, small, got, down_grad)
    if shard != 128:
        beta_grad = lax.dynamic_slice(beta_grad, (0, lax.axis_index("fsdp") * shard), (heads, shard))
    beta_grad = beta_grad.T
    expand_grad = expand_grad.transpose(0, 2, 1)
    return (
        block_outs, input_grad, attn_total, ffn_total, head_total, qkv_grad[None], beta_grad[None],
        conv_grad[None], out_grad[None], expand_grad[None], down_grad[None],
    )


def solution(mesh):
    in_specs = (
        P(("fsdp", "tensor"), None),
        P("fsdp", None),
        P("fsdp", None),
        P(),
        P(),
        P(),
        P(None, None, "fsdp", "tensor"),
        P(None, "fsdp", "tensor"),
        P(None, None, None, "tensor"),
        P(None, "tensor", "fsdp"),
        P(None, None, "fsdp", "tensor"),
        P(None, "tensor", "fsdp"),
        P(("fsdp", "tensor"), None),
    )
    out_specs = (
        P(None, ("fsdp", "tensor"), None),
        P(("fsdp", "tensor"), None),
        P(),
        P(),
        P(),
        P(None, None, "fsdp", "tensor"),
        P(None, "fsdp", "tensor"),
        P(None, None, None, "tensor"),
        P(None, "tensor", "fsdp"),
        P(None, None, "fsdp", "tensor"),
        P(None, "tensor", "fsdp"),
    )
    return jax.shard_map(
        on_device, mesh=mesh, in_specs=in_specs, out_specs=out_specs, check_vma=False
    )
```

```python
import functools
import jax
import jax.numpy as jnp
from jax import lax
from jax.experimental import pallas as pl
from jax.experimental.pallas import tpu as pltpu
from jax.sharding import PartitionSpec as P

HEAD = 128
C = 128
F32 = jnp.float32
BF = jnp.bfloat16

NN = (((1,), (0,)), ((), ()))
NT = (((1,), (1,)), ((), ()))
TN = (((0,), (0,)), ((), ()))


def dot1(a, b, dims=NN):
    return lax.dot_general(a.astype(BF), b.astype(BF), dims, preferred_element_type=F32)


def split(x):
    hi = x.astype(BF)
    return hi, (x - hi.astype(F32)).astype(BF)


def dot3(a, b, dims=NN):
    a1, a2 = split(a) if not isinstance(a, tuple) else a
    b1, b2 = split(b) if not isinstance(b, tuple) else b
    ka, kb = dims[0][0][0], dims[0][1][0]
    left = jnp.concatenate([a1, a2], axis=ka)
    n = b1.shape[1 - kb]
    if n == 128:
        right = jnp.concatenate([jnp.concatenate([b1, b2], axis=1 - kb), jnp.concatenate([b1, jnp.zeros_like(b1)], axis=1 - kb)], axis=kb)
        r = lax.dot_general(left, right, dims, preferred_element_type=F32)
        return r[:, :128] + r[:, 128:]
    r = lax.dot_general(left, jnp.concatenate([b1, b1], axis=kb), dims, preferred_element_type=F32)
    return r + lax.dot_general(a1, b2, dims, preferred_element_type=F32)


def dot3_old(a, b, dims=NN):
    a1, a2 = split(a) if not isinstance(a, tuple) else a
    b1, b2 = split(b) if not isinstance(b, tuple) else b
    d = functools.partial(lax.dot_general, dimension_numbers=dims, preferred_element_type=F32)
    return d(a1, b1) + (d(a1, b2) + d(a2, b1))


def block_masks():
    r = lax.broadcasted_iota(jnp.int32, (C, C), 0)
    c = lax.broadcasted_iota(jnp.int32, (C, C), 1)
    return r, c


def invert(systems, dot):
    r, c = block_masks()
    eye = (r == c).astype(F32)
    x = r ^ c
    lows = [low.astype(BF) for low in systems]
    out = [eye - jnp.where((x == 1), low, 0.0) for low in systems]
    size = 2
    while size < C:
        here = (x >= size) & (x < 2 * size)
        short = [t.astype(BF) for t in out]
        mids = [dot1(jnp.where(here, low, 0.0).astype(BF), t) for low, t in zip(lows, short)]
        out = [t - dot1(b, m) for t, b, m in zip(out, short, mids)]
        size *= 2
    splits = [split(t) for t in out]
    errors = [eye - t - dot(low, p) for low, t, p in zip(systems, out, splits)]
    return [t + dot1(p[0], e) for t, p, e in zip(out, splits, errors)]


def sigmoid(x):
    return 1.0 / (1.0 + jnp.exp(-x))


def taps_down(ext, rows, j):
    return lax.slice_in_dim(ext, 8 - j, 8 - j + rows, axis=0)


def row_sum(x):
    return jnp.dot(x.astype(BF), jnp.ones((HEAD, HEAD), BF), preferred_element_type=F32)


def head_norm(x):
    return x * lax.rsqrt(row_sum(x * x) + 1e-6)


def segment_parts(seg_s, cols_ref, segr_ref, first, sl):
    prev = jnp.where(first > 0, seg_s[jnp.maximum(first - 1, 0)], -1)
    last = seg_s[first + C - 1]
    segc = cols_ref[sl, 4:5]
    same = segc == segr_ref[0:1, sl]
    lead = (segc == prev.astype(F32)).astype(F32)
    trail = (segc == last.astype(F32)).astype(F32)
    return same, lead, trail, (prev == last).astype(F32)


def fwd_kernel(heads, cb, base, seg_s, x_ref, wide_ref, again_ref, cols_ref, segr_ref, taps_ref, gain_ref, tail_in, state_in,
               mixed_ref, kept_ref, na_ref, pre_ref, conv_ref, o_ref, t_ref, a_ref, p_ref, n_ref, z_ref, s_ref, u_ref, g_ref,
               tail, state, line):
    step = pl.program_id(0)
    width = heads * HEAD
    rows = cb * C
    taps = taps_ref.shape[1]

    @pl.when(step == 0)
    def _():
        tail[...] = jnp.zeros_like(tail) if tail_in is None else tail_in[...]
        state[...] = jnp.zeros_like(state) if state_in is None else state_in[...]

    r, c = block_masks()
    x = x_ref[...].astype(F32)
    na = (x * lax.rsqrt(jnp.mean(x * x, axis=-1, keepdims=True) + 1e-6) * again_ref[0:1, :]).astype(BF)
    na_ref[...] = na
    pre_ref[...] = jnp.dot(na, wide_ref[...], preferred_element_type=F32)
    tap = lambda j: jnp.concatenate([taps_ref[i, j:j + 1, :] for i in range(3)], axis=1)
    cur = pre_ref[:, :3 * width]
    line[:8, :] = tail[...]
    line[8:, :] = cur
    tot = cur * tap(0)
    for j in range(1, taps):
        tot = tot + line[8 - j:8 - j + rows, :] * tap(j) * cols_ref[:, j - 1:j]
    tail[...] = line[rows:, :]
    conv_ref[...] = tot
    tot = tot * sigmoid(tot)
    parts = [tot[:, i * width:(i + 1) * width] for i in range(3)]
    eye = (r == c).astype(F32)
    items = []
    for b in range(cb):
        sl = slice(b * C, (b + 1) * C)
        same, lead, trail, keep = segment_parts(seg_s, cols_ref, segr_ref, ((base + step) * cb + b) * C, sl)
        for h in range(heads):
            hs = slice(h * HEAD, (h + 1) * HEAD)
            q, k, v = (part[sl, hs] for part in parts)
            beta = sigmoid(pre_ref[sl, 3 * width + h:3 * width + h + 1]) * cols_ref[sl, 3:4]
            items.append(dict(b=b, h=h, q=head_norm(q), k=head_norm(k), v=v, beta=beta, same=same, lead=lead,
                              trail=trail, keep=keep, sl=sl, hs=hs))
    for it in items:
        it["kk"] = split(it["k"])
        p = jnp.where(it["same"] & (r > c), dot3(it["kk"], it["kk"], NT), 0.0)
        it["p"] = p
        it["low"] = p * it["beta"]
        it["a"] = jnp.where(it["same"] & (r >= c), dot3(it["q"], it["kk"], NT), 0.0)
    inv = invert([it["low"] for it in items], dot3)
    for it, t in zip(items, inv):
        rhs = jnp.concatenate([it["beta"] * it["v"], (it["beta"] * it["lead"]) * it["k"]], axis=1)
        tw = dot3(t, rhs)
        tws = split(tw)
        aw = dot3(it["a"], tws)
        bz = dot3(it["trail"] * it["k"], tws, TN)
        it["tv"], it["w"] = tw[:, :HEAD], tw[:, HEAD:]
        it["o0"], it["n"] = aw[:, :HEAD], it["lead"] * it["q"] - aw[:, HEAD:]
        it["bk"], it["z"] = bz[:, :HEAD], it["keep"] * eye - bz[:, HEAD:]
        it["t"] = t
    for it in items:
        b, h = it["b"], it["h"]
        s = state[h]
        ss = split(s)
        u = it["tv"] - dot3(it["w"], ss)
        o = it["o0"] + dot3(it["n"], ss)
        g = it["v"] - it["lead"] * dot3(it["kk"], ss)
        state[h] = it["bk"] + dot3(it["z"], ss)
        s_ref[b, h] = s
        u_ref[b, h] = u
        g_ref[b, h] = g
        t_ref[b, h] = it["t"]
        a_ref[b, h] = it["a"]
        p_ref[b, h] = it["p"]
        n_ref[b, h] = it["n"]
        z_ref[b, h] = it["z"]
        o_ref[it["sl"], it["hs"]] = o
        mixed = (o * lax.rsqrt(row_sum(o * o) * (1.0 / HEAD) + 1e-5) * gain_ref[0:1, :]).astype(BF)
        mixed_ref[it["sl"], it["hs"]] = mixed
        kept_ref[it["sl"], it["hs"]] = mixed


def stage_bits(n):
    bits = [1 << i for i in range(n.bit_length() - 1)]
    return bits, [bits[1], bits[0]] + bits[2:]


def bwd_kernel(heads, cb, n_f, shard, seg_s, ga0_ref, ga0c_ref, ga1_ref, ga1c_ref, mix_ref, na_ref, out_ref, wide_ref, x_ref, dffn0_ref, dffn1_ref,
               pre_ref, conv_ref, o_ref, cols_ref, segr_ref, taps_ref, gain_ref,
               t_ref, a_ref, p_ref, n_ref, z_ref, s_ref, u_ref, g_ref,
               away1_ref, keep1_ref, away2_ref, keep2_ref, sna_ref, kna_ref, gains_ref, small_ref,
               head_rows, dstate, acc, dpre):
    step = pl.program_id(0)
    steps = pl.num_programs(0)
    width = heads * HEAD
    rows = cb * C
    taps = taps_ref.shape[1]
    back = steps - 1 - step
    core = lax.axis_index("tensor") % 2

    @pl.when(step == 0)
    def _():
        head_rows[...] = jnp.zeros_like(head_rows)
        dstate[...] = jnp.zeros_like(dstate)
        acc[...] = jnp.zeros_like(acc)
        gains_ref[...] = jnp.zeros_like(gains_ref)
        gains_ref[6:7, :] = dffn0_ref[...] + dffn1_ref[...]
        small_ref[...] = jnp.zeros_like(small_ref)

    r, c = block_masks()
    dcs = [[[None] * heads for _ in range(cb)] for _ in range(3)]
    dgain = jnp.zeros((1, HEAD), F32)
    dlog = [None] * cb
    ga = jnp.where(back % 2 == core, jnp.where(back >= 2, ga1_ref[...], ga0_ref[...]),
                   jnp.where(back >= 2, ga1c_ref[...], ga0c_ref[...]))
    dmix = jnp.dot(ga, out_ref[...], preferred_element_type=F32)
    acc[:, 3 * width:4 * width] += lax.dot_general(ga, mix_ref[...], TN, preferred_element_type=F32)
    for b in reversed(range(cb)):
        sl = slice(b * C, (b + 1) * C)
        same, lead, trail, keep = segment_parts(seg_s, cols_ref, segr_ref, (back * cb + b) * C, sl)
        lane = lax.broadcasted_iota(jnp.int32, (C, HEAD), 1)
        dl = jnp.zeros((C, HEAD), F32)
        for h in range(heads):
            hs = slice(h * HEAD, (h + 1) * HEAD)
            cq, ck, cv = (conv_ref[sl, i * width + h * HEAD:i * width + (h + 1) * HEAD] for i in range(3))
            gq, gk, gv = sigmoid(cq), sigmoid(ck), sigmoid(cv)
            q, k = cq * gq, ck * gk
            rq = lax.rsqrt(jnp.sum(q * q, axis=-1, keepdims=True) + 1e-6)
            rk = lax.rsqrt(jnp.sum(k * k, axis=-1, keepdims=True) + 1e-6)
            q, k = q * rq, k * rk
            gb = sigmoid(pre_ref[sl, 3 * width + h:3 * width + h + 1])
            pad = cols_ref[sl, 3:4]
            beta = gb * pad
            o = o_ref[sl, hs]
            dm = dmix[sl, hs]
            ro = lax.rsqrt(jnp.mean(o * o, axis=-1, keepdims=True) + 1e-5)
            oh = o * ro
            dgain = dgain + jnp.sum(dm * oh, axis=0, keepdims=True)
            du0 = dm * gain_ref[0:1, :]
            do = ro * (du0 - oh * jnp.mean(du0 * oh, axis=-1, keepdims=True))
            ds1 = dstate[h]
            u = u_ref[b, h]
            s = s_ref[b, h]
            a = a_ref[b, h]
            p = p_ref[b, h]
            ks = split(k)
            ds1s = split(ds1)
            dos = split(do)
            us = split(u)
            dstate[h] = dot3(z_ref[b, h], ds1s, TN) + dot3(n_ref[b, h], dos, TN)
            du = dot3(a, dos, TN) + trail * dot3(ks, ds1s)
            dr = dot3(t_ref[b, h], du, TN)
            drs = split(dr)
            ss = split(s)
            dlow = jnp.where(same & (r > c), -dot3(drs, us, NT), 0.0)
            da = jnp.where(same & (r >= c), dot3(dos, us, NT), 0.0)
            dv = beta * dr
            dbeta = jnp.sum(dr * g_ref[b, h] , axis=-1, keepdims=True) + jnp.sum(dlow * p, axis=-1, keepdims=True)
            dp = split(beta * dlow)
            das = split(da)
            dq = lead * dot3(dos, ss, NT) + dot3(das, ks)
            dk = (dot3(das, q, TN) + trail * dot3(us, ds1s, NT) - (beta * lead) * dot3(drs, ss, NT)
                  + dot3(dp, ks) + dot3(dp, ks, TN))
            dsq = rq * (dq - q * jnp.sum(q * dq, axis=-1, keepdims=True))
            dsk = rk * (dk - k * jnp.sum(k * dk, axis=-1, keepdims=True))
            dcs[0][b][h] = dsq * gq * (1.0 + cq * (1.0 - gq))
            dcs[1][b][h] = dsk * gk * (1.0 + ck * (1.0 - gk))
            dcs[2][b][h] = dv * gv * (1.0 + cv * (1.0 - gv))
            dl = jnp.where(lane == h, dbeta * pad * gb * (1.0 - gb), dl)
        dlog[b] = dl
    gains_ref[7:8, :HEAD] += dgain
    for b in range(cb):
        dpre[b * C:(b + 1) * C, 3 * width:] = dlog[b].astype(BF)
    for i in range(3):
        dc = jnp.concatenate([jnp.concatenate(dcs[i][b], axis=1) for b in range(cb)], axis=0)
        pre = pre_ref[:, i * width:(i + 1) * width]
        tot = dc * taps_ref[i, 0:1, :]
        grads = [jnp.sum(dc * pre, axis=0, keepdims=True)]
        for j in range(1, taps):
            e = dc * cols_ref[:, j - 1:j]
            ext = jnp.concatenate([e, head_rows[j - 1, :, i * width:(i + 1) * width]], axis=0)
            head_rows[j - 1, :, i * width:(i + 1) * width] = e[:8]
            e = lax.slice_in_dim(ext, j, j + rows, axis=0)
            tot = tot + e * taps_ref[i, j:j + 1, :]
            grads.append(jnp.sum(e * pre, axis=0, keepdims=True))
        dpre[:, i * width:(i + 1) * width] = tot.astype(BF)
        small_ref[i:i + 1, :taps * width] += jnp.concatenate(grads, axis=1)
    low = dpre[...]
    acc[:, :3 * width] += lax.dot_general(na_ref[...], low[:, :3 * width], TN, preferred_element_type=F32)
    acc[:, 4 * width:] += lax.dot_general(na_ref[...], low[:, 3 * width:], TN, preferred_element_type=F32)
    dna = lax.dot_general(low, wide_ref[...], NT, preferred_element_type=F32)
    x = x_ref[...].astype(F32)
    gains_ref[5:6, :] += jnp.sum(dna * (x * lax.rsqrt(jnp.mean(x * x, axis=-1, keepdims=True) + 1e-6)), axis=0, keepdims=True)

    @pl.when(back % 2 == core)
    def _():
        kna_ref[back // 2] = dna

    @pl.when(back % 2 != core)
    def _():
        sna_ref[back // 2] = dna.astype(BF)

    @pl.when(step == steps - 1)
    def _():
        small_ref[3:3 + heads, :] = acc[:, 4 * width:].T[:heads, :]
        me = lax.axis_index("fsdp")
        first, second = stage_bits(n_f)
        half = 2 * width
        for ref, other, bit, lanes in ((away1_ref, keep1_ref, first[0], slice(0, half)), (away2_ref, keep2_ref, second[0], slice(half, 2 * half))):
            mine = (me // bit) % 2
            for j in range(n_f // 2):
                low_bits = j % bit
                there = (j - low_bits) * 2 + low_bits
                ref[j] = acc[pl.ds(pl.multiple_of((there + (1 - mine) * bit) * shard, 16), shard), lanes].astype(BF)
                other[j] = acc[pl.ds(pl.multiple_of((there + mine * bit) * shard, 16), shard), lanes].astype(other.dtype)


def whole(shape):
    return pl.BlockSpec(shape, lambda i, *_: (0,) * len(shape), pipeline_mode=pl.Buffered(1))


def shaped(shape, dtype=F32):
    return jax.ShapeDtypeStruct(shape, dtype)


def params(limit=60):
    return pltpu.CompilerParams(dimension_semantics=("arbitrary",), vmem_limit_bytes=limit * 2**20)


COST = pl.CostEstimate(flops=10**10, bytes_accessed=10**7, transcendentals=0)
TINY = pl.CostEstimate(flops=1, bytes_accessed=1, transcendentals=0)


def fwd_call_kernel(heads, cb, base, n_old, *refs):
    ins, rest = ((*refs[:8], None, None), refs[8:]) if n_old == 0 else (refs[:10], refs[10 + n_old:])
    outs, tail_out, state_out, tail, state, line = rest[:14], rest[14], rest[15], rest[16], rest[17], rest[18]
    fwd_kernel(heads, cb, base, *ins, *outs, tail, state, line)

    @pl.when(pl.program_id(0) == pl.num_programs(0) - 1)
    def _():
        tail_out[...] = tail[...]
        state_out[...] = state[...]


def mixer_fwd(part, parts, x, wide, again, cols, segr, seg, taps, gain, tail, state, old, cb=4):
    n, d = x.shape
    width = taps.shape[2]
    heads = width // HEAD
    wide_cols = 3 * width + HEAD
    rows = cb * C
    steps = n // parts // rows
    base = part * steps
    sq = shaped((n // C, heads, C, HEAD))
    sqspec = pl.BlockSpec((cb, heads, C, HEAD), lambda i, s: (i + base, 0, 0, 0))
    here = lambda w: pl.BlockSpec((rows, w), lambda i, s: (i + base, 0))
    ins = [x, wide, again, cols, segr, taps, gain] + ([tail, state] if old else [])
    tail, state = shaped((8, 3 * width)), shaped((heads, HEAD, HEAD))
    kept = [shaped((n, width), BF), shaped((n, d), BF), shaped((n, wide_cols)), shaped((n, 3 * width)), shaped((n, width))] + [sq] * 8
    return pl.pallas_call(
        functools.partial(fwd_call_kernel, heads, cb, base, len(old)),
        grid_spec=pltpu.PrefetchScalarGridSpec(
            num_scalar_prefetch=1, grid=(steps,),
            in_specs=[here(d), whole((d, wide_cols)), whole((1, d)), here(cols.shape[1]),
                      pl.BlockSpec((1, rows), lambda i, s: (0, i + base)),
                      whole(taps.shape), whole((1, HEAD))] + ([whole(tail.shape), whole(state.shape)] if old else [])
            + [pl.BlockSpec(memory_space=pl.ANY)] * len(old),
            out_specs=[pl.BlockSpec((rows, width), lambda i, s: (i, 0)), here(width), here(d), here(wide_cols), here(3 * width), here(width)]
            + [sqspec] * 8 + [whole(tail.shape), whole(state.shape)],
            scratch_shapes=[pltpu.VMEM(tail.shape, F32), pltpu.VMEM(state.shape, F32), pltpu.VMEM((rows + 8, 3 * width), F32)]),
        out_shape=[shaped((n // parts, width), BF)] + kept + [shaped(tail.shape), shaped(state.shape)],
        input_output_aliases={1 + len(ins) + i: 1 + i for i in range(len(old))},
        compiler_params=params(),
        cost_estimate=COST,
        name="mixer_fwd",
    )(seg, *ins, *old)


def mixer_bwd(n_f, shard, ga, out, wide, x, dffn, cols, segr, seg, taps, gain, kept, cb=2):
    mix, na, pre, conv, o, *rest = kept
    n, wide_cols = pre.shape
    d = x.shape[1]
    width = taps.shape[2]
    heads = width // HEAD
    rows = cb * C
    steps = n // rows
    ntap = taps.shape[1]
    sqspec = pl.BlockSpec((cb, heads, C, HEAD), lambda i, s: (steps - 1 - i, 0, 0, 0))
    row = lambda w: pl.BlockSpec((rows, w), lambda i, s: (steps - 1 - i, 0))
    outs = [shaped((n_f // 2, shard, 2 * width), BF)] * 4 + [
            shaped((2, rows, d), BF), shaped((2, rows, d)), shaped((8, d)), shaped((8, d))]
    return pl.pallas_call(
        functools.partial(bwd_kernel, heads, cb, n_f, shard),
        grid_spec=pltpu.PrefetchScalarGridSpec(
            num_scalar_prefetch=1, grid=(steps,),
            in_specs=[whole((rows, d))] * 4 + [row(width), row(d), whole(out.shape), whole((d, wide_cols)), row(d), whole((1, d)), whole((1, d)),
                      row(wide_cols), row(3 * width), row(width),
                      row(cols.shape[1]), pl.BlockSpec((1, rows), lambda i, s: (0, steps - 1 - i)),
                      whole(taps.shape), whole((1, HEAD))] + [sqspec] * 8,
            out_specs=[whole(v.shape) for v in outs],
            scratch_shapes=[pltpu.VMEM((ntap - 1, 8, 3 * width), F32), pltpu.VMEM((heads, HEAD, HEAD), F32),
                            pltpu.VMEM((d, 4 * width + HEAD), F32), pltpu.VMEM((rows, wide_cols), BF)]),
        out_shape=outs,
        compiler_params=params(),
        cost_estimate=COST,
        name="mixer_bwd",
    )(seg, *ga, mix, na, out, wide, x, *dffn, pre, conv, o, cols, segr, taps, gain, *rest)


def fold_kernel(n_f, stage, k1_ref, g1_ref, k2_ref, g2_ref, a1_out, k1_out, a2_out, k2_out):
    me = lax.axis_index("fsdp")
    for order, keep, got, away_out, keep_out in ((0, k1_ref, g1_ref, a1_out, k1_out), (1, k2_ref, g2_ref, a2_out, k2_out)):
        bits = stage_bits(n_f)[order]
        bit = bits[stage]
        left = sorted(b for b in bits[stage:])
        place = 1 << left.index(bit)
        mine = (me // bit) % 2
        for j in range(keep.shape[0] // 2):
            low = j % place
            there = (j - low) * 2 + low
            theirs = there + (1 - mine) * place
            away_out[j] = (keep[theirs].astype(F32) + got[theirs].astype(F32)).astype(BF)
            ours = there + mine * place
            keep_out[j] = (keep[ours].astype(F32) + got[ours].astype(F32)).astype(keep_out.dtype)


def fold(n_f, stage, k1, g1, k2, g2):
    m, shard, w = k1.shape
    outs = [shaped((m // 2, shard, w), BF)] * 4
    return pl.pallas_call(
        functools.partial(fold_kernel, n_f, stage),
        out_shape=outs,
        compiler_params=pltpu.CompilerParams(vmem_limit_bytes=60 * 2**20),
        cost_estimate=TINY,
        name="fold",
    )(k1, g1, k2, g2)


def finish_kernel(heads, ntap, k1_ref, g1_ref, k2_ref, g2_ref, s_ref, *refs):
    got, (qkv_ref, out_ref, taps_ref, beta_ref, attn_ref, ffn_ref, head_ref, hold) = refs[:-9], refs[-8:]
    width = qkv_ref.shape[2]
    shard = qkv_ref.shape[1]
    a = k1_ref[0].astype(F32) + g1_ref[0].astype(F32)
    b = k2_ref[0].astype(F32) + g2_ref[0].astype(F32)
    qkv_ref[0] = a[:, :width]
    qkv_ref[1] = a[:, width:]
    qkv_ref[2] = b[:, :width]
    out_ref[...] = b[:, width:].T
    small = s_ref[...]
    for g in got:
        small = small + g[...]
    width = taps_ref.shape[2]
    for i in range(3):
        for k in range(ntap):
            taps_ref[i, k:k + 1, :] = small[i:i + 1, k * width:(k + 1) * width]
    attn_ref[...] = small[5:6]
    ffn_ref[...] = small[6:7]
    head_ref[...] = small[7:8, :HEAD]
    if shard == 128:
        hold[...] = small
        me = lax.axis_index("fsdp")
        beta_ref[...] = hold[3:3 + heads, pl.ds(pl.multiple_of(me * shard, 128), shard)]
    else:
        beta_ref[...] = small[3:3 + heads]


def finish(heads, ntap, k1, g1, k2, g2, small, got, wait_for):
    m, shard, w = k1.shape
    d = small.shape[1]
    return pl.pallas_call(
        functools.partial(finish_kernel, heads, ntap),
        in_specs=[pl.BlockSpec(memory_space=pltpu.VMEM)] * (5 + len(got)) + [pl.BlockSpec(memory_space=pl.ANY)],
        out_shape=[shaped((3, shard, w // 2)), shaped((w // 2, shard)), shaped((3, ntap, w // 2)),
                   shaped((heads, 128 if shard == 128 else d)), shaped((1, d)), shaped((1, d)), shaped((1, HEAD))],
        scratch_shapes=[pltpu.VMEM((8, d), F32)],
        compiler_params=pltpu.CompilerParams(vmem_limit_bytes=60 * 2**20),
        cost_estimate=TINY,
        name="finish",
    )(k1, g1, k2, g2, small, *got, wait_for)


def ffn_kernel(ff, *refs):
    m, out, (x_ref, w_ref, gf_ref, gain_ref), rest = refs[:4], refs[4:8], refs[8:12], refs[12:]
    mid_ref, nf_ref, hid_ref, dgu_ref, keep_ref, send_ref, dgain_ref, hold = rest
    rows = keep_ref.shape[0]
    core = lax.axis_index("tensor") % 2
    mid = x_ref[...].astype(F32)
    for k in range(4):
        mid = mid + lax.dot_general(m[k][...], out[k][...], NT, preferred_element_type=F32)
    hold[...] = mid
    unit = mid * lax.rsqrt(jnp.mean(mid * mid, axis=-1, keepdims=True) + 1e-6)
    nf = (unit * gain_ref[0:1, :]).astype(BF)
    nf_ref[...] = nf
    mid_ref[...] = hold[pl.ds(pl.multiple_of(core * rows, 16), rows), :]
    gate = lax.dot_general(w_ref[:ff, :], nf, NT, preferred_element_type=F32)
    up = lax.dot_general(w_ref[ff:2 * ff, :], nf, NT, preferred_element_type=F32)
    dh = lax.dot_general(w_ref[2 * ff:, :], gf_ref[...], NT, preferred_element_type=F32)
    sig = sigmoid(gate)
    act = gate * sig
    hid_ref[...] = (act * up).astype(BF)
    dgu_ref[:ff, :] = (dh * up * sig * (1.0 + gate * (1.0 - sig))).astype(BF)
    dgu_ref[ff:, :] = (dh * act).astype(BF)
    dnf = lax.dot_general(dgu_ref[...], w_ref[:2 * ff, :], TN, preferred_element_type=F32)
    dgain_ref[...] = jnp.sum(dnf * unit, axis=0, keepdims=True)
    hold[...] = dnf
    keep_ref[...] = hold[pl.ds(pl.multiple_of(core * rows, 16), rows), :]
    send_ref[...] = hold[pl.ds(pl.multiple_of((1 - core) * rows, 16), rows), :].astype(BF)


def ffn(part, m, out, x, weights, gf, gain):
    n, width = m[0].shape
    d = x.shape[1]
    ff = weights.shape[0] // 3
    here = pl.BlockSpec((n, d), lambda i: (part, 0))
    outs = [shaped((n // 2, d)), shaped((n, d), BF), shaped((ff, n), BF), shaped((2 * ff, n), BF),
            shaped((n // 2, d)), shaped((n // 2, d), BF), shaped((1, d))]
    return pl.pallas_call(
        functools.partial(ffn_kernel, ff),
        grid=(1,),
        in_specs=[whole(v.shape) for v in (*m, *out)] + [here, whole(weights.shape), here, whole((1, d))],
        out_specs=[whole(v.shape) for v in outs],
        out_shape=outs,
        scratch_shapes=[pltpu.VMEM((n, d), F32)],
        compiler_params=params(),
        cost_estimate=COST,
        name="ffn",
    )(*m, *out, x, weights, gf, gain)


def grad_kernel(part, n, *refs):
    lows, others, (mid_ref, cot_ref, coty_ref, gain_ref, grad_ref, low_out) = refs[:n], refs[n:2 * n], refs[2 * n:]
    chip = lax.axis_index("tensor") // 2
    mid = mid_ref[...]
    factor = lax.rsqrt(jnp.mean(mid * mid, axis=-1, keepdims=True) + 1e-6)
    d_nf = jnp.concatenate([a[...].astype(F32) + b[...].astype(F32) for a, b in zip(lows, others)], axis=0)
    u = d_nf * gain_ref[0:1, :]
    cot = jnp.where(chip == part, cot_ref[...], coty_ref[...]).astype(F32)
    grad = cot + factor * u - mid * (factor * factor * factor) * jnp.mean(u * mid, axis=-1, keepdims=True)
    grad_ref[...] = grad
    low_out[...] = grad.astype(BF)


def grad_rows(part, lows, others, mid, cot, cot_y, gain):
    return pl.pallas_call(
        functools.partial(grad_kernel, part, len(lows)),
        out_shape=[shaped(mid.shape), shaped(mid.shape, BF)],
        compiler_params=pltpu.CompilerParams(vmem_limit_bytes=24 * 2**20),
        cost_estimate=TINY,
        name="grad_rows",
    )(*lows, *others, mid, cot, cot_y, gain)


def down_kernel(hid0_ref, hid1_ref, w_ref, send_ref, keep_ref, hold):
    core = lax.axis_index("tensor") % 2
    rows = send_ref.shape[1]
    for i, hid in enumerate((hid0_ref, hid1_ref)):
        hold[...] = lax.dot_general(hid[...], w_ref[...], TN, preferred_element_type=F32)
        keep_ref[i] = hold[pl.ds(pl.multiple_of(core * rows, 16), rows), :]
        send_ref[i] = hold[pl.ds(pl.multiple_of((1 - core) * rows, 16), rows), :].astype(BF)


def down(hid0, hid1, weights, wait_for):
    ff, n = hid0.shape
    d = weights.shape[1]
    outs = [shaped((2, n // 2, d), BF), shaped((2, n // 2, d))]

    def body(*refs):
        down_kernel(*refs[:3], *refs[3 + len(wait_for):])

    return pl.pallas_call(
        body,
        grid=(1,),
        in_specs=[whole(hid0.shape)] * 2 + [pl.BlockSpec((ff, d), lambda i: (2, 0))] + [pl.BlockSpec(memory_space=pl.ANY)] * len(wait_for),
        out_specs=[whole(v.shape) for v in outs],
        out_shape=outs,
        scratch_shapes=[pltpu.VMEM((n, d), F32)],
        compiler_params=params(),
        cost_estimate=TINY,
        name="down",
    )(hid0, hid1, weights, *wait_for)


def ffn_grads_kernel(ff, parts, *refs):
    gf_ref, o_ref = refs[3 * parts], refs[-1]
    n = refs[0].shape[1]
    up = down = None
    for i in range(parts):
        dgu, hid, nf = refs[3 * i:3 * i + 3]
        a = jnp.dot(dgu[...], nf[...], preferred_element_type=F32)
        b = jnp.dot(hid[...], gf_ref[i * n:(i + 1) * n, :], preferred_element_type=F32)
        up = a if up is None else up + a
        down = b if down is None else down + b
    for k in range(o_ref.shape[0]):
        lanes = slice(k * 128, (k + 1) * 128)
        o_ref[k, :2 * ff, :] = up[:, lanes].astype(BF)
        o_ref[k, 2 * ff:, :] = down[:, lanes].astype(BF)


def ffn_grads(pieces, gf, wait_for, step=256):
    ff = pieces[0][1].shape[0]
    n, d = gf.shape
    flat, specs = [], []
    for dgu, hid, nf in pieces:
        flat += [dgu, hid, nf]
        specs += [whole(dgu.shape), whole(hid.shape), pl.BlockSpec((nf.shape[0], step), lambda i: (0, i))]
    return pl.pallas_call(
        functools.partial(ffn_grads_kernel, ff, len(pieces)),
        grid=(d // step,),
        in_specs=specs + [pl.BlockSpec((n, step), lambda i: (0, i))] + [pl.BlockSpec(memory_space=pl.ANY)] * len(wait_for),
        out_specs=pl.BlockSpec((step // 128, 3 * ff, 128), lambda i: (i, 0, 0)),
        out_shape=shaped((d // 128, 3 * ff, 128), BF),
        compiler_params=params(),
        cost_estimate=pl.CostEstimate(flops=5 * 10**9, bytes_accessed=10**7, transcendentals=0),
        name="ffn_grads",
    )(*flat, gf, *wait_for)


def to_chips_kernel(keep, got, wait_for, mine_ref, away_ref):
    chip = lax.axis_index("tensor") // 2
    mine_ref[...] = keep[chip] + got[chip].astype(F32)
    away_ref[...] = (keep[1 - chip] + got[1 - chip].astype(F32)).astype(BF)


def to_chips(keep, got, wait_for):
    spec = pl.BlockSpec(memory_space=pltpu.VMEM)
    return pl.pallas_call(
        to_chips_kernel,
        in_specs=[spec] * 2 + [pl.BlockSpec(memory_space=pl.ANY)],
        out_shape=[shaped(keep.shape[1:]), shaped(keep.shape[1:], BF)],
        compiler_params=pltpu.CompilerParams(vmem_limit_bytes=60 * 2**20),
        cost_estimate=TINY,
        name="to_chips",
    )(keep, got, wait_for)


def last_kernel(g0, g1, na, na_y, x_ref, gain_ref, mid0, mid1, out, out_y, in_ref, block_ref):
    first = lax.axis_index("tensor") // 2 == 0
    x = x_ref[...].astype(F32)
    factor = lax.rsqrt(jnp.mean(x * x, axis=-1, keepdims=True) + 1e-6)
    u = (na[...] + na_y[...].astype(F32)) * gain_ref[0:1, :]
    in_ref[...] = jnp.where(first, g0[...], g1[...]) + (factor * u - x * (factor * factor * factor) * jnp.mean(u * x, axis=-1, keepdims=True))
    block_ref[...] = (jnp.where(first, mid0[...], mid1[...]) + out[...] + out_y[...].astype(F32)).astype(BF)


def last_rows(g0, g1, na, na_y, x, gain, mid0, mid1, out, out_y):
    return pl.pallas_call(
        last_kernel,
        out_shape=[shaped(g0.shape), shaped(g0.shape, BF)],
        compiler_params=pltpu.CompilerParams(vmem_limit_bytes=60 * 2**20),
        cost_estimate=TINY,
        name="last_rows",
    )(g0, g1, na, na_y, x, gain, mid0, mid1, out, out_y)


def ffn_cast_kernel(d_ref, expand_ref, down_ref):
    ff = down_ref.shape[0]
    expand_ref[0] = d_ref[:ff, :].astype(F32)
    expand_ref[1] = d_ref[ff:2 * ff, :].astype(F32)
    down_ref[...] = d_ref[2 * ff:, :].astype(F32)


def ffn_cast(d):
    ff, w = d.shape[0] // 3, d.shape[1]
    return pl.pallas_call(
        ffn_cast_kernel,
        out_shape=[shaped((2, ff, w)), shaped((ff, w))],
        compiler_params=pltpu.CompilerParams(vmem_limit_bytes=60 * 2**20),
        cost_estimate=TINY,
        name="ffn_cast",
    )(d)


def ffn_split_kernel(ff, parts, *refs):
    blocks, expand, away, keep = refs[-1], refs[-4], refs[-3], refs[-2]
    ffn_grads_kernel(ff, parts, *refs[:3 * parts + 1], blocks)
    me = lax.axis_index("fsdp")
    for k in range(blocks.shape[0]):
        expand[k] = blocks[k, :2 * ff, :]
        block = pl.program_id(0) * blocks.shape[0] + k

        @pl.when(block % 2 == me % 2)
        def _(k=k, block=block):
            keep[block // 2] = blocks[k, 2 * ff:, :]

        @pl.when(block % 2 != me % 2)
        def _(k=k, block=block):
            away[block // 2] = blocks[k, 2 * ff:, :]


def ffn_split_grads(pieces, gf, wait_for, step=256):
    ff = pieces[0][1].shape[0]
    n, d = gf.shape
    flat, specs = [], []
    for dgu, hid, nf in pieces:
        flat += [dgu, hid, nf]
        specs += [whole(dgu.shape), whole(hid.shape), pl.BlockSpec((nf.shape[0], step), lambda i: (0, i))]
    per = step // 128
    halves = shaped((d // 256, ff, 128), BF)
    return pl.pallas_call(
        functools.partial(ffn_split_kernel, ff, len(pieces)),
        grid=(d // step,),
        in_specs=specs + [pl.BlockSpec((n, step), lambda i: (0, i))] + [pl.BlockSpec(memory_space=pl.ANY)] * len(wait_for),
        out_specs=[pl.BlockSpec((per, 2 * ff, 128), lambda i: (i, 0, 0)), whole(halves.shape), whole(halves.shape)],
        out_shape=[shaped((d // 128, 2 * ff, 128), BF), halves, halves],
        scratch_shapes=[pltpu.VMEM((per, 3 * ff, 128), BF)],
        compiler_params=params(),
        cost_estimate=COST,
        name="ffn_grads",
    )(*flat, gf, *wait_for)


def halve_kernel(bit, k_ref, g_ref, wait_for, away, keep):
    mine = (lax.axis_index("fsdp") // bit) % 2
    count = k_ref.shape[0] // 2
    for j in range(count):
        ours, theirs = (2 * j + mine, 2 * j + 1 - mine) if bit == 2 else (mine, 1 - mine)
        away[j] = (k_ref[theirs].astype(F32) + g_ref[theirs].astype(F32)).astype(BF)
        keep[j] = (k_ref[ours].astype(F32) + g_ref[ours].astype(F32)).astype(BF)


def halve(bit, k, g, wait_for):
    m, ff, w = k.shape
    spec = pl.BlockSpec(memory_space=pltpu.VMEM)
    return pl.pallas_call(
        functools.partial(halve_kernel, bit),
        in_specs=[spec] * 2 + [pl.BlockSpec(memory_space=pl.ANY)],
        out_shape=[shaped((m // 2, ff, w), BF)] * 2,
        compiler_params=pltpu.CompilerParams(vmem_limit_bytes=60 * 2**20),
        cost_estimate=TINY,
        name="halve",
    )(k, g, wait_for)


def split_cast_kernel(d_ref, k_ref, g_ref, expand_ref, down_ref):
    ff = down_ref.shape[0]
    expand_ref[0] = d_ref[:ff, :].astype(F32)
    expand_ref[1] = d_ref[ff:, :].astype(F32)
    down_ref[...] = k_ref[0].astype(F32) + g_ref[0].astype(F32)


def split_cast(d, k, g):
    ff, w = d.shape[0] // 2, d.shape[1]
    return pl.pallas_call(
        split_cast_kernel,
        out_shape=[shaped((2, ff, w)), shaped((ff, w))],
        compiler_params=pltpu.CompilerParams(vmem_limit_bytes=60 * 2**20),
        cost_estimate=TINY,
        name="ffn_cast",
    )(d, k, g)


def pack_kernel(qkv_ref, beta_ref, out_ref, o_ref):
    width = qkv_ref.shape[2]
    n = o_ref.shape[0]
    for i in range(3):
        o_ref[:, i * width:(i + 1) * width] = qkv_ref[i]
    beta = beta_ref[...].astype(F32)
    heads = beta.shape[1]
    o_ref[:, 3 * width:3 * width + 128] = jnp.concatenate([beta, jnp.zeros((n, 128 - heads), F32)], axis=1).astype(BF)
    o_ref[:, 3 * width + 128:] = out_ref[...].astype(F32).T.astype(BF)


def pack(qkv, beta, out):
    n, width = qkv.shape[1:]
    return pl.pallas_call(
        pack_kernel,
        out_shape=shaped((n, 4 * width + 128), BF),
        compiler_params=pltpu.CompilerParams(vmem_limit_bytes=60 * 2**20),
        name="pack",
    )(qkv, beta, out)


def columns(seg, pad):
    n = seg.shape[0]
    cols = []
    for j in range(1, 4):
        before = jnp.concatenate([jnp.full((j,), -1, seg.dtype), seg[:n - j]])
        cols.append((before == seg).astype(F32))
    cols += [pad.astype(F32), seg.astype(F32)]
    cols += [jnp.zeros((n,), F32)] * 3
    return jnp.stack(cols, axis=1)


def hop(value, axis, bit):
    n = lax.axis_size(axis)
    return lax.ppermute(value, axis, [(i, i ^ bit) for i in range(n)])


def fence(*values):
    return lax.optimization_barrier(values)


def y_hop(value):
    return hop(value, "tensor", 2)


def core_hop(value):
    return hop(value, "tensor", 1)


def in_order(own, other_chip, pair):
    me = lax.axis_index("tensor")
    full = jnp.zeros((4,) + own.shape, own.dtype)
    for k, block in ((0, own), (2, other_chip), (1, pair[0]), (3, pair[1])):
        full = lax.dynamic_update_slice(full, block[None], (me ^ k,) + (0,) * own.ndim)
    return full.reshape((4 * own.shape[0],) + own.shape[1:])


class Ring:
    def __init__(self, value):
        n = lax.axis_size("fsdp")
        order = [i for i in range(0, n, 2)] + [i for i in reversed(range(1, n, 2))]
        me = lax.axis_index("fsdp")
        self.n = n
        self.me = jnp.where(me % 2 == 0, me // 2, n - 1 - me // 2)
        self.right = [(order[i], order[(i + 1) % n]) for i in range(n)]
        self.left = [(b, a) for a, b in self.right]
        self.rows = value.shape[0]
        self.full = jnp.zeros((n * self.rows,) + value.shape[1:], value.dtype)
        self.a = self.b = value
        self.k = 0
        self.put(value, 0, 0)

    def put(self, part, steps, start):
        place = lax.rem(self.me + steps + self.n, self.n)
        owner = jnp.where(place < self.n // 2, 2 * place, 2 * (self.n - 1 - place) + 1)
        self.full = lax.dynamic_update_slice(self.full, part, (owner * self.rows + start, 0))

    def step(self):
        self.k += 1
        k, half = self.k, self.rows // 2
        self.split = 2 * k == self.n and half % 16 == 0
        if self.split:
            self.a = lax.ppermute(self.a[:half], "fsdp", self.right)
            self.b = lax.ppermute(self.b[half:], "fsdp", self.left)
            return
        self.a = lax.ppermute(self.a, "fsdp", self.right)
        if 2 * k < self.n:
            self.b = lax.ppermute(self.b, "fsdp", self.left)

    def keep(self):
        self.put(self.a, -self.k, 0)
        if self.split or 2 * self.k < self.n:
            self.put(self.b, self.k, self.rows // 2 if self.split else 0)


def hop_sum(value, axis, bit):
    return value + hop(value, axis, bit)


def on_device(
    layer_input, segment_ids, pad_mask, attn_gain, ffn_gain, out_gain,
    qkv_weight, beta_weight, conv_weight, out_weight, expand_weight, down_weight, cotangent,
):
    n_f = lax.axis_size("fsdp")
    me_t = lax.axis_index("tensor")
    chip = me_t // 2
    rows, d_model = layer_input.shape
    width = qkv_weight.shape[3]
    heads = beta_weight.shape[2]
    ff = down_weight.shape[1]
    shard = qkv_weight.shape[2]
    taps = conv_weight[0]
    ntap = taps.shape[1]
    first_bits, second_bits = stage_bits(n_f)

    packed = pack(qkv_weight[0], beta_weight[0], out_weight[0])
    packed, expand_own, down_own = fence(packed, expand_weight[0], down_weight[0])
    ring = Ring(packed)
    ring.step()
    x_y = y_hop(layer_input)
    x_c = core_hop(layer_input)
    ffn_own = jnp.concatenate([expand_own[0].T, expand_own[1].T, down_own], axis=0)
    weights = lax.all_gather(ffn_own, "fsdp", axis=1, tiled=True)
    seg = segment_ids[0]
    cols = columns(seg, pad_mask[0])
    segr = seg.astype(F32)[None]
    ring.a, ring.b, x_c = fence(ring.a, ring.b, x_c)
    ring.keep()
    ring.step()
    c_y = y_hop(cotangent)
    c_c = core_hop(cotangent)
    ring.a, ring.b, x_y, c_y = fence(ring.a, ring.b, x_y, c_y)
    ring.keep()
    ring.step()
    x_cy = core_hop(x_y)
    c_cy = core_hop(c_y)
    ring.a, ring.b, cols, x_cy, c_cy = fence(ring.a, ring.b, cols, x_cy, c_cy)
    ring.keep()
    x_full = in_order(layer_input, x_y, (x_c, x_cy))
    g_f = in_order(cotangent, c_y, (c_c, c_cy))
    while 2 * ring.k < n_f:
        ring.step()
        ring.keep()
    wide, x_full, g_f = fence(ring.full, x_full, g_f)

    out_own = wide[:, 3 * width + HEAD:]
    tail = state = None

    def mix(i, tail, state, old):
        m, *kept, tail, state = mixer_fwd(i, 2, x_full, wide, attn_gain, cols, segr, seg, taps, out_gain, tail, state, old)
        return m, kept, tail, state

    ow_y = y_hop(out_own)
    ow_c = core_hop(out_own)
    m0, kept, tail, state = mix(0, tail, state, [])
    ow_y, ow_c, m0, tail, state = fence(ow_y, ow_c, m0, tail, state)
    m0_y = y_hop(m0)
    m0_c = core_hop(m0)
    ow_cy = core_hop(ow_y)
    m1, kept, tail, state = mix(1, tail, state, kept)
    m0_y, m0_c, ow_cy, m1 = fence(m0_y, m0_c, ow_cy, m1)

    def feed(i, *m):
        return ffn(i, m, (out_own, ow_y, ow_c, ow_cy), x_full, weights, g_f, ffn_gain)

    m1_y = y_hop(m1)
    m1_c = core_hop(m1)
    m0_cy = core_hop(m0_y)
    mid0, nf0, hid0, dgu0, keep0, send0, dgain0 = feed(0, m0, m0_y, m0_c, m0_cy)
    m1_y, m1_c, send0 = fence(m1_y, m1_c, send0)
    m1_cy = core_hop(m1_y)
    low0 = (keep0 + core_hop(send0).astype(F32)).astype(BF)
    m1_cy, low0 = fence(m1_cy, low0)
    low0_y = y_hop(low0)
    mid1, nf1, hid1, dgu1, keep1, send1, dgain1 = feed(1, m1, m1_y, m1_c, m1_cy)
    low0_y, send1 = fence(low0_y, send1)
    cut = rows // 2
    got1 = core_hop(send1)
    low1 = (keep1[:cut] + got1[:cut].astype(F32)).astype(BF)
    low1b = (keep1[cut:] + got1[cut:].astype(F32)).astype(BF)
    grad0, ga0 = grad_rows(0, [low0], [low0_y], mid0, cotangent, c_y, ffn_gain)
    low1, low1b, ga0 = fence(low1, low1b, ga0)
    low1_y, low1b_y = y_hop(low1), y_hop(low1b)
    ga0_c = core_hop(ga0)
    blocks = ffn_grads([(dgu0, hid0, nf0), (dgu1, hid1, nf1)], g_f, [low1])
    q = d_model // 128
    if q != n_f:
        blocks = blocks.reshape(q, 3 * ff, n_f // q, shard).transpose(0, 2, 1, 3).reshape(n_f, 3 * ff, shard)
    send_out, keep_out = down(hid0, hid1, weights, [blocks])
    low1_y, ga0_c, blocks = fence(low1_y, ga0_c, blocks)
    low1b_y, send_out, done_blocks = fence(low1b_y, send_out, blocks)
    d_ffn = lax.psum_scatter(blocks, "fsdp", scatter_dimension=0, tiled=False)
    grad1, ga1 = grad_rows(1, [low1, low1b], [low1_y, low1b_y], mid1, cotangent, c_y, ffn_gain)
    ga1_c = core_hop(ga1)
    ga1, ga1_c = fence(ga1, ga1_c)

    out_c = core_hop(send_out)
    made = mixer_bwd(
        n_f, shard, (ga0, ga0_c, ga1, ga1_c), out_own, wide, x_full, (dgain0, dgain1), cols, segr, seg, taps, out_gain, kept)
    away1, k1, away2, k2, send_na, keep_na, gains, small, out_c = fence(*made, out_c)

    g1 = hop(away1, "fsdp", first_bits[0])
    g2 = hop(away2, "fsdp", second_bits[0])
    na_c = core_hop(send_na)
    gains_got = [hop(gains, "tensor", k) for k in range(1, 4)]
    out, out_away = to_chips(keep_out, out_c, done_blocks)
    na, na_away = to_chips(keep_na, na_c, gains)
    g1, g2, na_away, out_away, *gains_got = fence(g1, g2, na_away, out_away, *gains_got)
    count = len(first_bits)
    small = small + gains + gains_got[0] + (gains_got[1] + gains_got[2])
    for stage in range(1, count):
        away1, k1, away2, k2 = fold(n_f, stage, k1, g1, k2, g2)
        if stage == 1:
            na_y, out_y = y_hop(na_away), y_hop(out_away)
        g1 = hop(away1, "fsdp", first_bits[stage])
        g2 = hop(away2, "fsdp", second_bits[stage])
        if stage < count - 1:
            small = hop_sum(small, "fsdp", first_bits[stage - 1])
            g1, g2, small = fence(g1, g2, small)
    if n_f == 8:
        got = [hop(small, "fsdp", k) for k in (2, 4, 6)]
    else:
        small = hop_sum(small, "fsdp", first_bits[count - 2])
        got = [hop(small, "fsdp", first_bits[count - 1])]
    input_grad, block_outs = last_rows(grad0, grad1, na, na_y, layer_input, attn_gain, mid0, mid1, out, out_y)
    block_outs = block_outs[None]
    expand_grad, down_grad = ffn_cast(d_ffn)
    qkv_grad, out_grad, conv_grad, beta_grad, attn_total, ffn_total, head_total = finish(heads, ntap, k1, g1, k2, g2, small, got, down_grad)
    if shard != 128:
        beta_grad = lax.dynamic_slice(beta_grad, (0, lax.axis_index("fsdp") * shard), (heads, shard))
    beta_grad = beta_grad.T
    expand_grad = expand_grad.transpose(0, 2, 1)
    return (
        block_outs, input_grad, attn_total, ffn_total, head_total, qkv_grad[None], beta_grad[None],
        conv_grad[None], out_grad[None], expand_grad[None], down_grad[None],
    )


def solution(mesh):
    in_specs = (
        P(("fsdp", "tensor"), None),
        P("fsdp", None),
        P("fsdp", None),
        P(),
        P(),
        P(),
        P(None, None, "fsdp", "tensor"),
        P(None, "fsdp", "tensor"),
        P(None, None, None, "tensor"),
        P(None, "tensor", "fsdp"),
        P(None, None, "fsdp", "tensor"),
        P(None, "tensor", "fsdp"),
        P(("fsdp", "tensor"), None),
    )
    out_specs = (
        P(None, ("fsdp", "tensor"), None),
        P(("fsdp", "tensor"), None),
        P(),
        P(),
        P(),
        P(None, None, "fsdp", "tensor"),
        P(None, "fsdp", "tensor"),
        P(None, None, None, "tensor"),
        P(None, "tensor", "fsdp"),
        P(None, None, "fsdp", "tensor"),
        P(None, "tensor", "fsdp"),
    )
    return jax.shard_map(
        on_device, mesh=mesh, in_specs=in_specs, out_specs=out_specs, check_vma=False
    )
```
